128 devices in a mesh: fsdp: 64 (over z, y, x_lo, core), tp: 2 (over x_hi).
Axes of the slice: x: 4 (x_hi: 2, x_lo: 2; x = x_hi * 2 + x_lo), y: 4, z: 4, core: 2. Of those that a mesh axis runs over, the one named last changes fastest.
Arguments:
- latents: bfloat16 [128, 128, 1152], P('fsdp', 'tp'), may hold values from -6 to 6
- condition: bfloat16 [96, 1152], replicated, may hold values from -6 to 6
- counts: int32 [64], replicated, may hold values from 1 to 2, 96 in all
- order: int32 [96], replicated, may hold values from 0 to 95, each once
- w_ada: bfloat16 [1152, 6, 1152], P(None, None, ('fsdp', 'tp')), may hold values from -0.1875 to 0.1875
- b_ada: float32 [6, 1152], P(None, ('fsdp', 'tp')), may hold values from -1.8 to 1.8
- w_qkv: bfloat16 [3, 1152, 1152], P(None, 'fsdp', 'tp'), may hold values from -0.1875 to 0.1875
- b_qv: float32 [2, 1152], P(None, 'tp'), may hold values from -1.8 to 1.8
- w_proj: bfloat16 [1152, 1152], P('tp', 'fsdp'), may hold values from -0.75 to 0.75
- b_proj: float32 [1152], replicated, may hold values from -1.8 to 1.8
- w_up: bfloat16 [1152, 4608], P('fsdp', 'tp'), may hold values from -0.1875 to 0.1875
- b_up: float32 [4608], P('tp'), may hold values from -1.8 to 1.8
- w_down: bfloat16 [4608, 1152], P('tp', 'fsdp'), may hold values from -0.09375 to 0.09375
- b_down: float32 [1152], replicated, may hold values from -1.8 to 1.8
- cotangent: bfloat16 [128, 128, 1152], P('fsdp', 'tp'), may hold values from -6 to 6
Outputs:
- block_output: bfloat16 [128, 128, 1152], P('fsdp', 'tp')
- grad_latents: float32 [128, 128, 1152], P('fsdp', 'tp')
- grad_condition: float32 [96, 1152], replicated
- grad_w_ada: float32 [1152, 6, 1152], P(None, None, ('fsdp', 'tp'))
- grad_b_ada: float32 [6, 1152], P(None, ('fsdp', 'tp'))
- grad_w_qkv: float32 [3, 1152, 1152], P(None, 'fsdp', 'tp')
- grad_b_qv: float32 [2, 1152], P(None, 'tp')
- grad_w_proj: float32 [1152, 1152], P('tp', 'fsdp')
- grad_b_proj: float32 [1152], replicated
- grad_w_up: float32 [1152, 4608], P('fsdp', 'tp')
- grad_b_up: float32 [4608], P('tp')
- grad_w_down: float32 [4608, 1152], P('tp', 'fsdp')
- grad_b_down: float32 [1152], replicated
The draws below stay inside these ranges and needn't reach their ends.
Inputs may be any that keep to these rules, and one draw needn't show every extreme that they name: counts[g] latents sit in the first slots of group g; they add up to 96, and some group holds 2. Each latent number appears once; group g holds latents order[o] to order[o + counts[g] - 1], o the sum of counts before g. Tokens in empty slots are read by no output.
All inputs are finite; a program needn't handle non-finite values.
Results may differ from the reference program's by a relative error of at most 0.015.
The reference program's roundings to bfloat16 on the way count: a program that leaves them out, or rounds other values in their place, can miss the bound.
Values may be sent and summed in bfloat16 or wider, within the bound.
A program may use at most 128 MiB of HBM per device.

```python
import math
import jax
import jax.numpy as jnp
import numpy as np
from jax import lax

D = 1152
HEADS = 16
HEAD_DIM = 72
FF = 4608
SEQ = 128
CAP = 2
SLOTS = 128
LATENTS = 96
N_FSDP = 64


def level_of(stream_key, extent, cuts, low, largest):
    level, own = 1.0, jax.random.fold_in(stream_key, 6)
    for dim, shards_of in cuts:
        heights = jnp.exp(jax.random.uniform(jax.random.fold_in(own, dim), (shards_of,), jnp.float32, low / len(cuts), largest / len(cuts)))
        level = level * jnp.repeat(heights, extent[dim] // shards_of).reshape([-1 if axis == dim else 1 for axis in range(len(extent))])
    return level


def profile(number_of, total, limit, slope):
    portions = [(1 << 20) // math.isqrt(standing ** slope) + 1 for standing in range(2, number_of + 1)]
    surplus, given = total - limit - (number_of - 1), [1] * (number_of - 1)
    while surplus > 0:
        movable = [i for i in range(number_of - 1) if given[i] < limit]
        mass, budget = sum([portions[i] for i in movable]), surplus
        for i in movable:
            addition = min(limit - given[i], max(1, budget * portions[i] // mass), surplus)
            given[i] = given[i] + addition
            surplus = surplus - addition
    return np.array([limit] + given)


def ragged_sizes(rng, number_of, total, reach, slope):
    if number_of == 2:
        one = jax.random.randint(rng, (), max(1, total - reach), min(reach, total - 1) + 1)
        return jnp.stack([one, total - one])
    sizes = jnp.asarray(profile(number_of, total, reach, slope), jnp.int32)
    pairs = (number_of - 1) // 2
    donor, sink = sizes[1:1 + 2 * pairs:2], sizes[2:2 + 2 * pairs:2]
    slack = jnp.minimum(donor - 1, reach - sink)
    passed = jax.random.randint(jax.random.fold_in(rng, 1), (pairs,), 0, 1 << 20) % (slack + 1)
    sizes = sizes.at[1:1 + 2 * pairs:2].set(donor - passed).at[2:2 + 2 * pairs:2].set(sink + passed)
    return sizes[jax.random.permutation(jax.random.fold_in(rng, 2), number_of)]


def normal_values(key, shape, scale, most, shards=(), kind=jnp.bfloat16):
    level = level_of(key, shape, shards, -0.22, 0.18) if shards else 1.0
    array = jax.random.normal(key, shape, jnp.float32) * scale * level
    return jnp.minimum(jnp.maximum(array, -most), most).astype(kind)


def setup_inputs(seed: int = 0) -> dict:
    streams_of = jax.random.split(jax.random.key(seed), 16)
    return {
        "latents": normal_values(streams_of[0], (SLOTS, SEQ, D), 1.0, 6.0, ((0, 64), (1, 2))),
        "condition": normal_values(streams_of[1], (LATENTS, D), 1.0, 6.0),
        "counts": ragged_sizes(streams_of[2], N_FSDP, LATENTS, CAP, 0).astype(jnp.int32),
        "order": jax.random.permutation(streams_of[3], LATENTS).astype(jnp.int32),
        "w_ada": normal_values(streams_of[4], (D, 6, D), D ** -0.5, 0.1875, ((2, 128),)),
        "b_ada": normal_values(streams_of[5], (6, D), 0.3, 1.8, ((1, 128),), jnp.float32),
        "w_qkv": normal_values(streams_of[6], (3, D, D), D ** -0.5, 0.1875, ((1, 64), (2, 2))),
        "b_qv": normal_values(streams_of[7], (2, D), 0.3, 1.8, ((1, 2),), jnp.float32),
        "w_proj": normal_values(streams_of[8], (D, D), HEAD_DIM ** -0.5, 0.75, ((0, 2), (1, 64))),
        "b_proj": normal_values(streams_of[9], (D,), 0.3, 1.8, (), jnp.float32),
        "w_up": normal_values(streams_of[10], (D, FF), D ** -0.5, 0.1875, ((0, 64), (1, 2))),
        "b_up": normal_values(streams_of[11], (FF,), 0.3, 1.8, ((0, 2),), jnp.float32),
        "w_down": normal_values(streams_of[12], (FF, D), FF ** -0.5, 0.09375, ((0, 2), (1, 64))),
        "b_down": normal_values(streams_of[13], (D,), 0.3, 1.8, (), jnp.float32),
        "cotangent": normal_values(streams_of[14], (SLOTS, SEQ, D), 1.0, 6.0, ((0, 64), (1, 2))),
    }


@jax.custom_vjp
def low(v):
    return lax.optimization_barrier(v.astype(jnp.bfloat16)).astype(jnp.float32)

@jax.custom_vjp
def low_back(v):
    return v

def low_keep(v):
    return (low(v), None)

def low_pass(kept, grad):
    return (grad,)

def back_keep(v):
    return (v, None)

def back_low(kept, grad):
    return (low(grad),)
low.defvjp(low_keep, low_pass)
low_back.defvjp(back_keep, back_low)
highest = lax.Precision.HIGHEST
norm_eps = 1e-06

def modulate(rows, shift, scale):
    centred = rows - lax.optimization_barrier(jnp.mean(rows, axis=-1, keepdims=True))
    normed = centred * lax.rsqrt(lax.optimization_barrier(jnp.mean(centred * centred, axis=-1, keepdims=True)) + norm_eps)
    return normed * (1.0 + scale) + shift

def gelu_tanh(values):
    return jax.nn.gelu(values, approximate=True)

def block_rows(rows, mods, alive, params):
    w_qkv, b_qv, w_proj, b_proj, w_up, b_up, w_down, b_down = params
    batch, length, width = rows.shape
    h_one = low(modulate(rows, mods[:, 0:1], mods[:, 1:2]))
    bias_three = jnp.stack([b_qv[0], jnp.zeros_like(b_qv[0]), b_qv[1]])
    projected = jnp.einsum('bld,kde->kble', h_one, w_qkv, precision=highest) + bias_three[:, None, None, :]
    triple = low(low_back(projected))
    heads_shape = (batch, length, HEADS, HEAD_DIM)
    queries = triple[0].reshape(heads_shape)
    keys = triple[1].reshape(heads_shape)
    values = triple[2].reshape(heads_shape)
    scores = low_back(jnp.einsum('blhe,bmhe->bhlm', queries, keys, precision=highest) * HEAD_DIM ** (-0.5))
    probs = jax.nn.softmax(scores, axis=-1)
    mixed = jnp.einsum('bhlm,bmhe->blhe', low(probs), values, precision=highest)
    attended = low(low_back(mixed)).reshape(batch, length, width)
    branch = low_back(jnp.einsum('ble,ed->bld', attended, w_proj, precision=highest) + b_proj)
    middle = rows + mods[:, 2:3] * branch
    h_two = low(modulate(middle, mods[:, 3:4], mods[:, 4:5]))
    upper = low_back(jnp.einsum('bld,df->blf', h_two, w_up, precision=highest) + b_up)
    acted = low(gelu_tanh(upper))
    down = low_back(jnp.einsum('blf,fd->bld', acted, w_down, precision=highest) + b_down)
    return (middle + mods[:, 5:6] * down) * alive[:, None, None]

def reference(latents, condition, counts, order, w_ada, b_ada, w_qkv, b_qv, w_proj, b_proj, w_up, b_up, w_down, b_down, cotangent):
    slots = latents.shape[0]
    offsets = (jnp.cumsum(counts) - counts).astype(jnp.int32)
    slot_rank = jnp.arange(CAP, dtype=jnp.int32)
    place = jnp.clip(offsets[:, None] + slot_rank[None, :], 0, LATENTS - 1).astype(jnp.int32)
    owner = order[place.reshape(-1)]
    alive = (slot_rank[None, :] < counts[:, None]).reshape(-1).astype(jnp.float32)
    per_block = math.gcd(slots, max(1, 4096 // SEQ))

    def blocked(values):
        return values.reshape((slots // per_block, per_block) + values.shape[1:])

    def forward(rows, cond, ada_w, ada_b, qkv_w, qv_b, proj_w, proj_b, up_w, up_b, down_w, down_b):
        soft = jax.nn.silu(cond)
        table = low(jnp.einsum('nd,dke->nke', soft, ada_w, precision=highest) + ada_b)
        mods = table[owner]
        params = (qkv_w, qv_b, proj_w, proj_b, up_w, up_b, down_w, down_b)

        def run(pieces):
            return block_rows(pieces[0], pieces[1], pieces[2], params)
        outs = lax.map(jax.checkpoint(run), (blocked(rows), blocked(mods), blocked(alive)))
        return outs.reshape(rows.shape)
    primals = (latents.astype(jnp.float32), condition.astype(jnp.float32), w_ada.astype(jnp.float32), b_ada.astype(jnp.float32), w_qkv.astype(jnp.float32), b_qv.astype(jnp.float32), w_proj.astype(jnp.float32), b_proj.astype(jnp.float32), w_up.astype(jnp.float32), b_up.astype(jnp.float32), w_down.astype(jnp.float32), b_down.astype(jnp.float32))
    result, pullback = jax.vjp(forward, *primals)
    grads = pullback(cotangent.astype(jnp.float32))
    return (result.astype(jnp.bfloat16), grads[0], grads[1], grads[2], grads[3], grads[4], grads[5], grads[6], grads[7], grads[8], grads[9], grads[10], grads[11])
```

```python
import functools

import jax
import jax.numpy as jnp
from jax import lax
from jax.experimental import pallas as pl
from jax.experimental.pallas import tpu as pltpu
from jax.sharding import PartitionSpec as P

MESH = pl.DeviceIdType.MESH
OFFS = (0, 3, 1, 2)


def place_of():
    f = lax.axis_index("fsdp")
    return f // 16, (f // 4) % 4, (f // 2) % 2, f % 2, lax.axis_index("tp")


def peers(z, y, x, c, t):
    def at(z, y, x, c):
        return (z * 16 + y * 4 + x * 2 + c, t)

    return {
        "z": (at((z + 3) % 4, y, x, c), at((z + 1) % 4, y, x, c)),
        "y": (at(z, (y + 3) % 4, x, c), at(z, (y + 1) % 4, x, c)),
        "x": at(z, y, 1 - x, c),
        "c": at(z, y, x, 1 - c),
    }


def greet(near):
    barrier = pltpu.get_barrier_semaphore()
    group = (*near["z"], *near["y"], near["x"], near["c"])
    for peer in group:
        pl.semaphore_signal(barrier, inc=1, device_id=peer, device_id_type=MESH)
    pl.semaphore_wait(barrier, len(group))


def gather_kernel(firsts, *refs):
    n = len(firsts)
    ins, outs = refs[:n], refs[n : 2 * n]
    local_sem, send_sem, recv_sem, core_send, core_recv = refs[2 * n :]
    z, y, x, c, t = place_of()
    near = peers(z, y, x, c, t)
    greet(near)
    started = []

    def spot(p, u, v):
        return (c, u, v) if firsts[p] == "z" else (c, v, u)

    def remote(src, dst, ssem, rsem, peer):
        return pltpu.make_async_remote_copy(
            src_ref=src, dst_ref=dst, send_sem=ssem, recv_sem=rsem, device_id=peer, device_id_type=MESH
        )

    def send(p, k, ref, peer, src=None):
        cp = remote(ref if src is None else src, ref, send_sem.at[p, k], recv_sem.at[p, k], peer)
        cp.start()
        started.append(cp)

    def arrive(p, k, ref):
        remote(ref, ref, send_sem.at[p, k], recv_sem.at[p, k], near["x"]).wait_recv()

    def share(p, k, ref):
        cp = remote(ref, ref, core_send.at[p, k], core_recv.at[p, k], near["c"])
        cp.start()
        started.append(cp)

    def axes(p):
        if firsts[p] == "z":
            return z, y, near["z"], near["y"]
        return y, z, near["y"], near["z"]

    locals_ = []
    for p in range(n):
        own = outs[p].at[c, z, y, x]
        send(p, 0, own, near["x"], ins[p])
        cp = pltpu.make_async_copy(ins[p], own, local_sem.at[p])
        cp.start()
        locals_.append(cp)
    for p in range(n):
        u, v, one, two = axes(p)
        locals_[p].wait()
        arrive(p, 0, outs[p].at[c, z, y, 1 - x])
        pair = outs[p].at[spot(p, u, v)]
        send(p, 1, pair, one[1])
        send(p, 2, pair, one[0])
        share(p, 0, pair)
    for p in range(n):
        u, v, one, two = axes(p)
        pair = outs[p].at[spot(p, u, v)]
        send(p, 5, pair, two[1])
        send(p, 6, pair, two[0])
    for p in range(n):
        u, v, one, two = axes(p)
        for k, way in ((1, 1), (2, 0)):
            uu = (u + OFFS[k]) % 4
            pair = outs[p].at[spot(p, uu, v)]
            arrive(p, k, pair)
            send(p, 2 + k, outs[p].at[(*spot(p, uu, v), 1 - way)], one[way])
            send(p, 5 + 4 * k, pair, two[1])
            send(p, 6 + 4 * k, pair, two[0])
            share(p, 4 * k, pair)
    for p in range(n):
        u, v, one, two = axes(p)
        uu = (u + 2) % 4
        arrive(p, 3, outs[p].at[(*spot(p, uu, v), 0)])
        arrive(p, 4, outs[p].at[(*spot(p, uu, v), 1)])
        pair = outs[p].at[spot(p, uu, v)]
        send(p, 17, pair, two[1])
        send(p, 18, pair, two[0])
        share(p, 12, pair)
    for k in range(4):
        for p in range(n):
            u, v, one, two = axes(p)
            uu = (u + OFFS[k]) % 4
            for side, way in ((1, 1), (2, 0)):
                vv = (v + OFFS[side]) % 4
                pair = outs[p].at[spot(p, uu, vv)]
                arrive(p, 4 + 4 * k + side, pair)
                send(p, 6 + 4 * k + side, outs[p].at[(*spot(p, uu, vv), 1 - way)], two[way])
                share(p, 4 * k + side, pair)
    for k in range(4):
        for p in range(n):
            u, v, one, two = axes(p)
            uu, vv = (u + OFFS[k]) % 4, (v + 2) % 4
            arrive(p, 7 + 4 * k, outs[p].at[(*spot(p, uu, vv), 0)])
            arrive(p, 8 + 4 * k, outs[p].at[(*spot(p, uu, vv), 1)])
            share(p, 4 * k + 3, outs[p].at[spot(p, uu, vv)])
    for p in range(n):
        for k in range(16):
            ref = outs[p].at[1 - c, k // 4, k % 4]
            remote(ref, ref, core_send.at[p, k], core_recv.at[p, k], near["c"]).wait_recv()
    for cp in started:
        cp.wait_send()


def gather_blocks(firsts, parts, collective_id):
    n = len(parts)
    return pl.pallas_call(
        functools.partial(gather_kernel, firsts),
        out_shape=[jax.ShapeDtypeStruct((2, 4, 4, 2) + part.shape, part.dtype) for part in parts],
        in_specs=[pl.BlockSpec(memory_space=pl.ANY)] * n,
        out_specs=[pl.BlockSpec(memory_space=pl.ANY)] * n,
        scratch_shapes=[
            pltpu.SemaphoreType.DMA((n,)),
            pltpu.SemaphoreType.DMA((n, 21)),
            pltpu.SemaphoreType.DMA((n, 21)),
            pltpu.SemaphoreType.DMA((n, 16)),
            pltpu.SemaphoreType.DMA((n, 16)),
        ],
        compiler_params=pltpu.CompilerParams(collective_id=collective_id, has_side_effects=True),
    )(*parts)


def add_into(dst, *srcs):
    width = dst.shape[-1]

    def step(i, carry):
        cols = pl.ds(pl.multiple_of(i * 128, 128), 128)
        lead = (slice(None),) * (len(dst.shape) - 1)
        total = srcs[0][(*lead, cols)].astype(jnp.float32)
        for src in srcs[1:]:
            total = total + src[(*lead, cols)].astype(jnp.float32)
        dst[(*lead, cols)] = total.astype(dst.dtype)
        return carry

    lax.fori_loop(0, width // 128, step, 0)


def scatter_kernel(firsts, *refs):
    n = len(firsts)
    grads, outs = refs[:n], refs[n : 2 * n]
    refs = refs[2 * n :]
    twins, sums, inner, mids, outer, ends, last = (refs[i * n : (i + 1) * n] for i in range(7))
    send_sem, recv_sem, core_send, core_recv = refs[7 * n :]
    z, y, x, c, t = place_of()
    near = peers(z, y, x, c, t)
    greet(near)
    started = []

    def remote(src, dst, ssem, rsem, peer):
        return pltpu.make_async_remote_copy(
            src_ref=src, dst_ref=dst, send_sem=ssem, recv_sem=rsem, device_id=peer, device_id_type=MESH
        )

    def axes(p):
        if firsts[p] == "z":
            return z, y, near["z"], near["y"]
        return y, z, near["y"], near["z"]

    def spot(p, u, v):
        return (u, v) if firsts[p] == "z" else (v, u)

    def send(p, k, src, dst, peer):
        cp = remote(src, dst, send_sem.at[p, k], recv_sem.at[p, k], peer)
        cp.start()
        started.append(cp)

    def arrive(p, k, ref):
        remote(ref, ref, send_sem.at[p, k], recv_sem.at[p, k], near["x"]).wait_recv()

    order = (3, 2, 1, 0)
    sides = (3, 2, 1, 0)
    for side in sides:
        for k in order:
            for p in range(n):
                u, v, one, two = axes(p)
                at = spot(p, (u + OFFS[k]) % 4, (v + OFFS[side]) % 4)
                j = 4 * k + side
                cp = remote(
                    grads[p].at[(1 - c, *at)], twins[p].at[at], core_send.at[p, j], core_recv.at[p, j], near["c"]
                )
                cp.start()
                started.append(cp)

    def combine(p, k, side):
        u, v, one, two = axes(p)
        at = spot(p, (u + OFFS[k]) % 4, (v + OFFS[side]) % 4)
        j = 4 * k + side
        twin = twins[p].at[at]
        remote(twin, twin, core_send.at[p, j], core_recv.at[p, j], near["c"]).wait_recv()
        add_into(sums[p].at[at], grads[p].at[(c, *at)], twin)

    for k in order:
        for p in range(n):
            u, v, one, two = axes(p)
            combine(p, k, 3)
            src = sums[p].at[spot(p, (u + OFFS[k]) % 4, (v + 2) % 4)]
            send(p, 6 * k, src.at[0], inner[p].at[k, 0], two[1])
            send(p, 6 * k + 1, src.at[1], inner[p].at[k, 1], two[0])
    for k in order:
        for p in range(n):
            u, v, one, two = axes(p)
            combine(p, k, 2)
            src = sums[p].at[spot(p, (u + OFFS[k]) % 4, (v + 1) % 4)]
            send(p, 6 * k + 2, src.at[1], inner[p].at[k, 2], two[1])
            combine(p, k, 1)
            src = sums[p].at[spot(p, (u + OFFS[k]) % 4, (v + 3) % 4)]
            send(p, 6 * k + 4, src.at[0], inner[p].at[k, 4], two[0])
    for k in order:
        for p in range(n):
            u, v, one, two = axes(p)
            arrive(p, 6 * k, inner[p].at[k, 0])
            src = sums[p].at[spot(p, (u + OFFS[k]) % 4, (v + 1) % 4)].at[0]
            add_into(src, src, inner[p].at[k, 0])
            send(p, 6 * k + 3, src, inner[p].at[k, 3], two[1])
            arrive(p, 6 * k + 1, inner[p].at[k, 1])
            src = sums[p].at[spot(p, (u + OFFS[k]) % 4, (v + 3) % 4)].at[1]
            add_into(src, src, inner[p].at[k, 1])
            send(p, 6 * k + 5, src, inner[p].at[k, 5], two[0])
    for k in order:
        for p in range(n):
            combine(p, k, 0)
    for k in order:
        for p in range(n):
            u, v, one, two = axes(p)
            own = sums[p].at[spot(p, (u + OFFS[k]) % 4, v)]
            for j in range(2, 6):
                arrive(p, 6 * k + j, inner[p].at[k, j])
            add_into(mids[p].at[k, 0], own.at[0], inner[p].at[k, 3], inner[p].at[k, 4])
            add_into(mids[p].at[k, 1], own.at[1], inner[p].at[k, 2], inner[p].at[k, 5])
            if k == 3:
                send(p, 24, mids[p].at[3, 0], outer[p].at[0], one[1])
                send(p, 25, mids[p].at[3, 1], outer[p].at[1], one[0])
            if k == 2:
                send(p, 26, mids[p].at[2, 1], outer[p].at[2], one[1])
            if k == 1:
                send(p, 28, mids[p].at[1, 0], outer[p].at[4], one[0])
    for p in range(n):
        u, v, one, two = axes(p)
        arrive(p, 24, outer[p].at[0])
        add_into(mids[p].at[2, 0], mids[p].at[2, 0], outer[p].at[0])
        send(p, 27, mids[p].at[2, 0], outer[p].at[3], one[1])
        arrive(p, 25, outer[p].at[1])
        add_into(mids[p].at[1, 1], mids[p].at[1, 1], outer[p].at[1])
        send(p, 29, mids[p].at[1, 1], outer[p].at[5], one[0])
    for p in range(n):
        for j in range(2, 6):
            arrive(p, 24 + j, outer[p].at[j])
        add_into(ends[p].at[0], mids[p].at[0, 0], outer[p].at[3], outer[p].at[4])
        add_into(ends[p].at[1], mids[p].at[0, 1], outer[p].at[2], outer[p].at[5])
        send(p, 30, ends[p].at[1 - x], last[p], near["x"])
    for p in range(n):
        arrive(p, 30, last[p])
        add_into(outs[p], ends[p].at[x], last[p])
    for cp in started:
        cp.wait_send()


def scatter_blocks(firsts, parts, collective_id):
    n = len(parts)
    rows = [part.shape[4:] for part in parts]

    def room(*lead):
        return [pltpu.VMEM(lead + row, jnp.bfloat16) for row in rows]

    return pl.pallas_call(
        functools.partial(scatter_kernel, firsts),
        out_shape=[jax.ShapeDtypeStruct(row, jnp.float32) for row in rows],
        in_specs=[pl.BlockSpec(memory_space=pltpu.VMEM)] * n,
        out_specs=[pl.BlockSpec(memory_space=pltpu.VMEM)] * n,
        scratch_shapes=[
            *room(4, 4, 2),
            *room(4, 4, 2),
            *room(4, 6),
            *room(4, 2),
            *room(6),
            *room(2),
            *room(),
            pltpu.SemaphoreType.DMA((n, 31)),
            pltpu.SemaphoreType.DMA((n, 31)),
            pltpu.SemaphoreType.DMA((n, 16)),
            pltpu.SemaphoreType.DMA((n, 16)),
        ],
        compiler_params=pltpu.CompilerParams(
            collective_id=collective_id, has_side_effects=True, vmem_limit_bytes=60 * 1024 * 1024
        ),
    )(*parts)


def everyone():
    f, t = lax.axis_index("fsdp"), lax.axis_index("tp")
    me = f * 2 + t
    count = lax.axis_size("fsdp") * lax.axis_size("tp")

    def peer(i):
        other = lax.rem(me + i, count)
        return other, (other // 2, other % 2)

    return me, count, peer


def greet_all(count, peer):
    barrier = pltpu.get_barrier_semaphore()

    def hello(i, carry):
        pl.semaphore_signal(barrier, inc=1, device_id=peer(i)[1], device_id_type=MESH)
        return carry

    lax.fori_loop(1, count, hello, 0)
    pl.semaphore_wait(barrier, count - 1)


def spread(count, peer, source, target, send_sem, recv_sem):
    def go(i, carry):
        other, where = peer(i)
        pltpu.make_async_remote_copy(
            src_ref=source(other),
            dst_ref=target,
            send_sem=send_sem,
            recv_sem=recv_sem,
            device_id=where,
            device_id_type=MESH,
        ).start()
        return carry

    lax.fori_loop(1, count, go, 0)


def settle(count, buffer, sem):
    ref = buffer.at[pl.ds(0, count - 1)]
    pltpu.make_async_copy(ref, ref, sem).wait()


def exchange_kernel(halve, in_ref, out_ref, send_sem, recv_sem):
    me, count, peer = everyone()
    greet_all(count, peer)

    def source(other):
        return in_ref.at[other // 2 if halve else other]

    spread(count, peer, source, out_ref.at[me], send_sem, recv_sem)
    out_ref[me] = source(me)[...]
    settle(count, out_ref, recv_sem)
    settle(count, out_ref, send_sem)


def exchange(parts, halve, count, collective_id):
    return pl.pallas_call(
        functools.partial(exchange_kernel, halve),
        out_shape=jax.ShapeDtypeStruct((count,) + parts.shape[1:], parts.dtype),
        in_specs=[pl.BlockSpec(memory_space=pltpu.VMEM)],
        out_specs=pl.BlockSpec(memory_space=pltpu.VMEM),
        scratch_shapes=[pltpu.SemaphoreType.DMA, pltpu.SemaphoreType.DMA],
        compiler_params=pltpu.CompilerParams(collective_id=collective_id, has_side_effects=True),
    )(parts)


def total_kernel(in_ref, out_ref, held, mine, send_one, recv_one, send_two, recv_two):
    me, count, peer = everyone()
    greet_all(count, peer)
    spread(count, peer, lambda other: in_ref.at[other], held.at[me], send_one, recv_one)
    held[me] = in_ref[me]
    settle(count, held, recv_one)

    def add(i, total):
        return total + held[i]

    total = lax.fori_loop(0, count, add, jnp.zeros(mine.shape, jnp.float32))
    mine[...] = total
    out_ref[me] = total
    spread(count, peer, lambda other: mine, out_ref.at[me], send_two, recv_two)
    settle(count, out_ref, recv_two)
    settle(count, held, send_one)
    settle(count, out_ref, send_two)


def total_everywhere(parts, collective_id):
    return pl.pallas_call(
        total_kernel,
        out_shape=jax.ShapeDtypeStruct(parts.shape, parts.dtype),
        in_specs=[pl.BlockSpec(memory_space=pltpu.VMEM)],
        out_specs=pl.BlockSpec(memory_space=pltpu.VMEM),
        scratch_shapes=[
            pltpu.VMEM(parts.shape, parts.dtype),
            pltpu.VMEM(parts.shape[1:], parts.dtype),
            pltpu.SemaphoreType.DMA,
            pltpu.SemaphoreType.DMA,
            pltpu.SemaphoreType.DMA,
            pltpu.SemaphoreType.DMA,
        ],
        compiler_params=pltpu.CompilerParams(collective_id=collective_id, has_side_effects=True),
    )(parts)


HEAD_DIM = 72


highest = lax.Precision.HIGHEST
norm_eps = 1e-06


def modulate(rows, shift, scale):
    centred = rows - jnp.mean(rows, axis=-1, keepdims=True)
    normed = centred * lax.rsqrt(jnp.mean(centred * centred, axis=-1, keepdims=True) + norm_eps)
    return normed * (1.0 + scale) + shift


def gelu_tanh(values):
    return jax.nn.gelu(values, approximate=True)


def widen(rows):
    return lax.all_gather(rows, "tp", axis=1, tiled=True)


def narrow(terms):
    return lax.psum_scatter(
        terms.astype(jnp.bfloat16), "tp", scatter_dimension=1, tiled=True
    ).astype(jnp.float32)

FIRSTS = ("z", "y")
MAIN = 1024
CHUNK = 896
LEFT = 3968


def shuffle_matrix(width):
    place = jnp.arange(width, dtype=jnp.int32)
    tail = place - MAIN
    block = jnp.where(place < MAIN, place // 16, tail // 2)
    row = jnp.where(place < MAIN, place % 16, 16 + tail % 2)
    fsdp = ((block // 8) % 4) * 16 + ((block // 2) % 4) * 4 + (block % 2) * 2 + block // 32
    source = fsdp * 18 + row
    return (jnp.arange(width, dtype=jnp.int32)[:, None] == source[None, :]).astype(jnp.bfloat16)


def shuffled(rows, matrix):
    return jnp.einsum("...d,de->...e", rows, matrix, preferred_element_type=jnp.float32).astype(jnp.bfloat16)


def shuffled_wide(rows, matrix):
    return jnp.einsum("...d,de->...e", rows, matrix.astype(jnp.float32), precision=highest)


def straight(rows, matrix):
    return jnp.einsum("...e,de->...d", rows, matrix, preferred_element_type=jnp.float32).astype(jnp.bfloat16)


def straight_wide(rows, matrix):
    return jnp.einsum("...e,de->...d", rows, matrix.astype(jnp.float32), precision=highest)


def pack_rows(all_rows):
    main, tail = all_rows[:16], all_rows[16:]
    tail = jnp.pad(tail, ((0, 0), (0, 8 * CHUNK - tail.shape[1]))).reshape(16, CHUNK)
    whole = jnp.concatenate([tail, main], axis=1)
    return whole[:, :LEFT], whole[:, LEFT:]


def unpack_rows(left, right, width):
    whole = jnp.concatenate([left, right], axis=1)
    return jnp.concatenate([whole[:, CHUNK:], whole[:, :CHUNK].reshape(2, 8 * CHUNK)[:, :width]], axis=0)


def unpack_all(left, right, width):
    left, right = left.reshape(MAIN, -1), right.reshape(MAIN, -1)
    tail = left[:, :CHUNK].reshape(128, 8 * CHUNK)[:, :width]
    third = width // 3
    most = third - (right.shape[1] - third)
    one = jnp.concatenate([left[:, CHUNK : CHUNK + third], tail[:, :third]], axis=0)
    two = jnp.concatenate(
        [
            jnp.concatenate([left[:, CHUNK + third :], right[:, : right.shape[1] - third]], axis=1),
            tail[:, third : 2 * third],
        ],
        axis=0,
    )
    three = jnp.concatenate([right[:, right.shape[1] - third :], tail[:, 2 * third :]], axis=0)
    return one, two, three


def pack_all(grads):
    whole = jnp.concatenate(grads, axis=1)
    main, tail = whole[:MAIN], whole[MAIN:]
    tail = jnp.pad(tail, ((0, 0), (0, 8 * CHUNK - tail.shape[1]))).reshape(MAIN, CHUNK)
    whole = jnp.concatenate([tail, main], axis=1)
    shape = (2, 4, 4, 2, 16)
    return whole[:, :LEFT].reshape(*shape, LEFT), whole[:, LEFT:].reshape(*shape, -1)


def attend_forward(pieces):
    queries, keys, values = pieces
    factor = queries.shape[-1] ** (-0.5)
    scores = jnp.einsum("lhe,mhe->hlm", queries, keys, preferred_element_type=jnp.float32) * factor
    peak = jnp.max(scores, axis=-1, keepdims=True)
    raised = jnp.exp(scores - peak)
    total = jnp.sum(raised, axis=-1, keepdims=True)
    weights = (raised / total).astype(jnp.bfloat16)
    mixed = jnp.einsum("hlm,mhe->lhe", weights, values, preferred_element_type=jnp.float32)
    return (mixed.astype(jnp.bfloat16), (peak + jnp.log(total))[..., 0])


def attend_backward(pieces):
    queries, keys, values, log_total, grad_mixed = pieces
    factor = queries.shape[-1] ** (-0.5)
    scores = jnp.einsum("lhe,mhe->hlm", queries, keys, preferred_element_type=jnp.float32) * factor
    probs = jnp.exp(scores - log_total[..., None])
    grad_probs = jnp.einsum("lhe,mhe->hlm", grad_mixed, values, preferred_element_type=jnp.float32)
    inner = jnp.sum(probs * grad_probs, axis=-1, keepdims=True)
    grad_scores = (probs * (grad_probs - inner)).astype(jnp.bfloat16)
    grad_queries = (
        jnp.einsum("hlm,mhe->lhe", grad_scores, keys, preferred_element_type=jnp.float32) * factor
    ).astype(jnp.bfloat16)
    grad_keys = (
        jnp.einsum("hlm,lhe->mhe", grad_scores, queries, preferred_element_type=jnp.float32)
        * factor
    ).astype(jnp.bfloat16)
    grad_values = jnp.einsum(
        "hlm,lhe->mhe", probs.astype(jnp.bfloat16), grad_mixed, preferred_element_type=jnp.float32
    ).astype(jnp.bfloat16)
    return (grad_queries, grad_keys, grad_values)


def local(
    latents,
    condition,
    counts,
    order,
    w_ada,
    b_ada,
    w_qkv,
    b_qv,
    w_proj,
    b_proj,
    w_up,
    b_up,
    w_down,
    b_down,
    cotangent,
):
    slots = latents.shape[0]
    latent_count = condition.shape[0]
    group = lax.axis_index("fsdp")
    ranks = jnp.arange(counts.shape[0], dtype=jnp.int32)
    held = jnp.sum(jnp.where(ranks == group, counts, 0))
    before = jnp.sum(jnp.where(ranks < group, counts, 0))
    slot_rank = jnp.arange(slots, dtype=jnp.int32)
    live = (slot_rank < held).astype(jnp.float32)
    place = jnp.clip(before + slot_rank, 0, latent_count - 1)
    numbers = jnp.arange(latent_count, dtype=jnp.int32)
    owner = jnp.sum(jnp.where(numbers[None, :] == place[:, None], order[None, :], 0), axis=1)
    offsets = jnp.cumsum(counts) - counts
    every = jnp.clip(offsets[:, None] + slot_rank[None, :], 0, latent_count - 1).reshape(-1)
    owners = jnp.sum(jnp.where(numbers[None, :] == every[:, None], order[None, :], 0), axis=1)
    choose_all = (numbers[None, :] == owners[:, None]).astype(jnp.bfloat16)
    groups = counts.shape[0]
    devices = groups * 2
    matrix = shuffle_matrix(latents.shape[2])
    soft_cond = jax.nn.silu(condition.astype(jnp.float32))
    ada_local = w_ada.astype(jnp.float32)
    mod_part = jnp.einsum("nd,dke->nke", soft_cond, ada_local, precision=highest) + b_ada
    mod_low = mod_part.astype(jnp.bfloat16).reshape(latent_count, -1)
    mod_send = jnp.dot(choose_all, mod_low, preferred_element_type=jnp.float32).astype(jnp.bfloat16)
    columns = mod_part.shape[2]
    mod_send = jnp.pad(mod_send.reshape(groups, slots, -1), ((0, 0), (0, 16 - slots), (0, 128 - 6 * columns)))
    mod_got = exchange(mod_send, True, devices, 1)[:, :slots, : 6 * columns]
    slot_mod = jnp.transpose(mod_got.reshape(devices, slots, 6, columns), (1, 2, 0, 3)).reshape(slots, 6, -1)
    slot_mod = shuffled(slot_mod, matrix).astype(jnp.float32)
    shift_one = slot_mod[:, 0:1]
    scale_one = slot_mod[:, 1:2]
    gate_one = slot_mod[:, 2:3]
    shift_two = slot_mod[:, 3:4]
    scale_two = slot_mod[:, 4:5]
    gate_two = slot_mod[:, 5:6]
    rows = shuffled(latents, matrix).astype(jnp.float32)
    cotangent = shuffled(cotangent, matrix)
    b_proj, b_down = shuffled_wide(jnp.stack([b_proj, b_down]), matrix)
    own_rows = jnp.concatenate([w_qkv[0], w_qkv[1], w_qkv[2], w_proj.T, w_up, w_down.T], axis=1)
    width = own_rows.shape[1]
    head_part = w_qkv.shape[2]
    left, right = gather_blocks(FIRSTS, pack_rows(own_rows), 2)
    inner_all, up_all, down_all = unpack_all(left, right, width)
    qkv_all, proj_all = inner_all[:, : 3 * head_part], inner_all[:, 3 * head_part :]
    normed_one = widen(modulate(rows, shift_one, scale_one).astype(jnp.bfloat16))
    length = normed_one.shape[1]
    head_dim = HEAD_DIM
    head_count = head_part // head_dim
    bias_three = jnp.stack([b_qv[0], jnp.zeros_like(b_qv[0]), b_qv[1]])
    triple = (
        jnp.einsum("bld,de->ble", normed_one, qkv_all, preferred_element_type=jnp.float32)
        + bias_three.reshape(-1)
    ).astype(jnp.bfloat16)
    triple = [triple[..., i * head_part : (i + 1) * head_part] for i in range(3)]
    heads_shape = (slots, length, head_count, head_dim)
    queries = triple[0].reshape(heads_shape)
    keys = triple[1].reshape(heads_shape)
    values = triple[2].reshape(heads_shape)
    attended_heads, log_total = lax.map(attend_forward, (queries, keys, values))
    attended = attended_heads.reshape(slots, length, head_part)
    branch = (
        narrow(jnp.einsum("ble,de->bld", attended, proj_all, preferred_element_type=jnp.float32))
        + b_proj
    )
    middle = rows + gate_one * branch
    normed_two = widen(modulate(middle, shift_two, scale_two).astype(jnp.bfloat16))
    upper = jnp.einsum("bld,df->blf", normed_two, up_all, preferred_element_type=jnp.float32) + b_up
    acted = gelu_tanh(upper).astype(jnp.bfloat16)
    down = (
        narrow(jnp.einsum("blf,df->bld", acted, down_all, preferred_element_type=jnp.float32))
        + b_down
    )
    alive = live[:, None, None]
    block_output = straight(((middle + gate_two * down) * alive).astype(jnp.bfloat16), matrix)
    grad_rows = cotangent.astype(jnp.float32) * alive
    grad_gate_two = jnp.sum(grad_rows * down, axis=1, keepdims=True)
    down_low = (gate_two * grad_rows).astype(jnp.bfloat16)
    grad_b_down = jnp.sum(down_low.astype(jnp.float32), axis=(0, 1))
    down_wide = widen(down_low)
    up_use, down_use = (up_all, down_all)
    grad_acted = jnp.einsum("bld,df->blf", down_wide, down_use, preferred_element_type=jnp.float32)
    grad_upper = jax.vjp(gelu_tanh, upper)[1](grad_acted)[0]
    upper_low = grad_upper.astype(jnp.bfloat16)
    grad_b_up_local = jnp.sum(upper_low.astype(jnp.float32), axis=(0, 1))
    grad_w_down = jnp.einsum("bld,blf->df", down_wide, acted, preferred_element_type=jnp.float32)
    grad_w_up = jnp.einsum("bld,blf->df", normed_two, upper_low, preferred_element_type=jnp.float32)
    grad_normed_two = narrow(
        jnp.einsum("blf,df->bld", upper_low, up_use, preferred_element_type=jnp.float32)
    )
    grad_middle_norm, grad_shift_two, grad_scale_two = jax.vjp(
        modulate, middle, shift_two, scale_two
    )[1](grad_normed_two)
    grad_middle = grad_rows + grad_middle_norm
    grad_gate_one = jnp.sum(grad_middle * branch, axis=1, keepdims=True)
    branch_low = (gate_one * grad_middle).astype(jnp.bfloat16)
    grad_b_proj = jnp.sum(branch_low.astype(jnp.float32), axis=(0, 1))
    branch_wide = widen(branch_low)
    qkv_use, proj_use = (qkv_all, proj_all)
    grad_attended = jnp.einsum(
        "bld,de->ble", branch_wide, proj_use, preferred_element_type=jnp.float32
    ).astype(jnp.bfloat16)
    grad_w_proj = jnp.einsum(
        "bld,ble->de", branch_wide, attended, preferred_element_type=jnp.float32
    )
    grad_queries, grad_keys, grad_values = lax.map(
        attend_backward, (queries, keys, values, log_total, grad_attended.reshape(heads_shape))
    )
    flat_shape = (slots, length, head_part)
    grad_triple = jnp.concatenate(
        [
            grad_queries.reshape(flat_shape),
            grad_keys.reshape(flat_shape),
            grad_values.reshape(flat_shape),
        ],
        axis=-1,
    )
    grad_b_qv_local = jnp.stack(
        [
            jnp.sum(grad_queries.astype(jnp.float32), axis=(0, 1)).reshape(-1),
            jnp.sum(grad_values.astype(jnp.float32), axis=(0, 1)).reshape(-1),
        ]
    )
    grad_w_qkv = jnp.einsum(
        "bld,ble->de", normed_one, grad_triple, preferred_element_type=jnp.float32
    )
    grad_normed_one = narrow(
        jnp.einsum("ble,de->bld", grad_triple, qkv_use, preferred_element_type=jnp.float32)
    )
    grad_rows_norm, grad_shift_one, grad_scale_one = jax.vjp(modulate, rows, shift_one, scale_one)[
        1
    ](grad_normed_one)
    grad_latents = straight_wide(grad_middle + grad_rows_norm, matrix)
    packed = pack_all(
        [grads.astype(jnp.bfloat16) for grads in (grad_w_qkv, grad_w_proj, grad_w_up, grad_w_down)]
    )
    summed = unpack_rows(*scatter_blocks(FIRSTS, packed, 3), width)
    grad_w_qkv = jnp.stack([summed[:, i * head_part : (i + 1) * head_part] for i in range(3)])
    grad_w_proj = summed[:, 3 * head_part : 4 * head_part].T
    up_part = w_up.shape[1]
    grad_w_up = summed[:, 4 * head_part : 4 * head_part + up_part]
    grad_w_down = summed[:, 4 * head_part + up_part :].T
    grad_mod = jnp.concatenate(
        [
            grad_shift_one,
            grad_scale_one,
            grad_gate_one,
            grad_shift_two,
            grad_scale_two,
            grad_gate_two,
        ],
        axis=1,
    )
    grad_mod = straight_wide(grad_mod, matrix).reshape(slots, 6, devices, columns)
    grad_send = jnp.transpose(grad_mod, (2, 0, 1, 3)).reshape(devices, slots, 6 * columns)
    grad_send = jnp.pad(grad_send, ((0, 0), (0, 8 - slots), (0, 128 - 6 * columns)))
    grad_got = exchange(grad_send, False, devices, 4)[:, :slots, : 6 * columns]
    grad_got = jnp.sum(grad_got.reshape(groups, 2, slots, 6 * columns), axis=1).reshape(groups * slots, -1)
    alive_all = (slot_rank[None, :] < counts[:, None]).reshape(-1, 1)
    grad_mod_part = jnp.einsum(
        "sn,se->ne",
        choose_all.astype(jnp.float32),
        jnp.where(alive_all, grad_got, 0.0),
        precision=highest,
    ).reshape(latent_count, 6, columns)
    grad_b_ada = jnp.sum(grad_mod_part, axis=0)
    grad_w_ada = jnp.einsum("nd,nke->dke", soft_cond, grad_mod_part, precision=highest)
    grad_soft_part = jnp.einsum("nke,dke->nd", grad_mod_part, ada_local, precision=highest)
    tensor_rank = lax.axis_index("tp")
    zero_index = jnp.zeros((), jnp.int32)
    up_half = grad_b_up_local.shape[0]
    qv_place = lax.dynamic_update_slice(
        jnp.zeros((2, head_part * lax.axis_size("tp")), jnp.float32),
        grad_b_qv_local,
        (zero_index, tensor_rank * head_part),
    )
    up_place = lax.dynamic_update_slice(
        jnp.zeros((up_half * lax.axis_size("tp"),), jnp.float32),
        grad_b_up_local,
        (tensor_rank * up_half,),
    )
    sums = [grad_soft_part, grad_b_proj, grad_b_down, qv_place, up_place]
    flat = jnp.concatenate([each.reshape(-1) for each in sums])
    flat = jnp.pad(flat, (0, devices * 1024 - flat.shape[0])).reshape(devices, 8, 128)
    flat = total_everywhere(flat, 5).reshape(-1)
    parts, start = [], 0
    for each in sums:
        parts.append(flat[start : start + each.size].reshape(each.shape))
        start += each.size
    grad_soft, grad_b_proj, grad_b_down, qv_full, up_full = parts
    grad_b_proj, grad_b_down = straight_wide(jnp.stack([grad_b_proj, grad_b_down]), matrix)
    grad_b_qv = lax.dynamic_slice_in_dim(qv_full, tensor_rank * head_part, head_part, 1)
    grad_b_up = lax.dynamic_slice_in_dim(up_full, tensor_rank * up_half, up_half, 0)
    grad_condition = jax.vjp(jax.nn.silu, condition.astype(jnp.float32))[1](grad_soft)[0]
    return (
        block_output,
        grad_latents,
        grad_condition,
        grad_w_ada,
        grad_b_ada,
        grad_w_qkv,
        grad_b_qv,
        grad_w_proj,
        grad_b_proj,
        grad_w_up,
        grad_b_up,
        grad_w_down,
        grad_b_down,
    )


def solution(mesh):
    in_specs = (
        P("fsdp", "tp", None),
        P(),
        P(),
        P(),
        P(None, None, ("fsdp", "tp")),
        P(None, ("fsdp", "tp")),
        P(None, "fsdp", "tp"),
        P(None, "tp"),
        P("tp", "fsdp"),
        P(),
        P("fsdp", "tp"),
        P("tp"),
        P("tp", "fsdp"),
        P(),
        P("fsdp", "tp", None),
    )
    out_specs = (
        P("fsdp", "tp", None),
        P("fsdp", "tp", None),
        P(),
        P(None, None, ("fsdp", "tp")),
        P(None, ("fsdp", "tp")),
        P(None, "fsdp", "tp"),
        P(None, "tp"),
        P("tp", "fsdp"),
        P(),
        P("fsdp", "tp"),
        P("tp"),
        P("tp", "fsdp"),
        P(),
    )
    return jax.shard_map(local, mesh=mesh, in_specs=in_specs, out_specs=out_specs, check_vma=False)
```

```python
import functools

import jax
import jax.numpy as jnp
from jax import lax
from jax.experimental import pallas as pl
from jax.experimental.pallas import tpu as pltpu
from jax.sharding import PartitionSpec as P

MESH = pl.DeviceIdType.MESH
OFFS = (0, 3, 1, 2)
WIDTHS = (2304, 2304, 2304, 896)
PIECES = (
    (3, 0, 896, "z"),
    (0, 0, 1152, "z"),
    (0, 1152, 1152, "y"),
    (1, 0, 1152, "z"),
    (1, 1152, 1152, "y"),
    (2, 0, 1152, "z"),
    (2, 1152, 1152, "y"),
)


highest = lax.Precision.HIGHEST
norm_eps = 1e-06


def place_of():
    f = lax.axis_index("fsdp")
    return f // 16, (f // 4) % 4, (f // 2) % 2, f % 2, lax.axis_index("tp")


def peers(z, y, x, c, t):
    def at(z, y, x, c):
        return (z * 16 + y * 4 + x * 2 + c, t)

    return {
        "z": (at((z + 3) % 4, y, x, c), at((z + 1) % 4, y, x, c)),
        "y": (at(z, (y + 3) % 4, x, c), at(z, (y + 1) % 4, x, c)),
        "x": at(z, y, 1 - x, c),
        "c": at(z, y, x, 1 - c),
    }


def greet(near):
    barrier = pltpu.get_barrier_semaphore()
    group = (*near["z"], *near["y"], near["x"], near["c"])
    for peer in group:
        pl.semaphore_signal(barrier, inc=1, device_id=peer, device_id_type=MESH)
    pl.semaphore_wait(barrier, len(group))


def gather_kernel(*refs):
    n, m = len(PIECES), len(WIDTHS)
    ins, outs = refs[:m], refs[m : 2 * m]
    local_sem, send_sem, recv_sem, core_send, core_recv = refs[2 * m :]
    z, y, x, c, t = place_of()
    near = peers(z, y, x, c, t)
    greet(near)
    started = []

    def spot(p, u, v, core=c):
        return core * 32 + (u * 8 + v * 2 if PIECES[p][3] == "z" else v * 8 + u * 2)

    def block(p, at, count=1):
        r, low, width, first = PIECES[p]
        return outs[r].at[pl.ds(at, count), :, pl.ds(low, width)]

    def remote(src, dst, ssem, rsem, peer):
        return pltpu.make_async_remote_copy(
            src_ref=src, dst_ref=dst, send_sem=ssem, recv_sem=rsem, device_id=peer, device_id_type=MESH
        )

    def send(p, k, ref, peer, src=None):
        cp = remote(ref if src is None else src, ref, send_sem.at[p, k], recv_sem.at[p, k], peer)
        cp.start()
        started.append(cp)

    def arrive(p, k, ref):
        remote(ref, ref, send_sem.at[p, k], recv_sem.at[p, k], near["x"]).wait_recv()

    def share(p, k, ref):
        cp = remote(ref, ref, core_send.at[p, k], core_recv.at[p, k], near["c"])
        cp.start()
        started.append(cp)

    def axes(p):
        if PIECES[p][3] == "z":
            return z, y, near["z"], near["y"]
        return y, z, near["y"], near["z"]

    locals_ = []
    for p in range(n):
        r, low, width, first = PIECES[p]
        mine = ins[r].at[:, :, pl.ds(low, width)]
        own = block(p, c * 32 + z * 8 + y * 2 + x)
        send(p, 0, own, near["x"], mine)
        cp = pltpu.make_async_copy(mine, own, local_sem.at[p])
        cp.start()
        locals_.append(cp)
    for p in range(n):
        u, v, one, two = axes(p)
        locals_[p].wait()
        arrive(p, 0, block(p, c * 32 + z * 8 + y * 2 + 1 - x))
        pair = block(p, spot(p, u, v), 2)
        send(p, 1, pair, one[1])
        send(p, 2, pair, one[0])
        share(p, 0, pair)
    for p in range(n):
        u, v, one, two = axes(p)
        pair = block(p, spot(p, u, v), 2)
        send(p, 5, pair, two[1])
        send(p, 6, pair, two[0])
    for p in range(n):
        u, v, one, two = axes(p)
        for k, way in ((1, 1), (2, 0)):
            uu = (u + OFFS[k]) % 4
            pair = block(p, spot(p, uu, v), 2)
            arrive(p, k, pair)
            send(p, 2 + k, block(p, spot(p, uu, v) + 1 - way), one[way])
            send(p, 5 + 4 * k, pair, two[1])
            send(p, 6 + 4 * k, pair, two[0])
            share(p, 4 * k, pair)
    for p in range(n):
        u, v, one, two = axes(p)
        uu = (u + 2) % 4
        arrive(p, 3, block(p, spot(p, uu, v) + 0))
        arrive(p, 4, block(p, spot(p, uu, v) + 1))
        pair = block(p, spot(p, uu, v), 2)
        send(p, 17, pair, two[1])
        send(p, 18, pair, two[0])
        share(p, 12, pair)
    for k in range(4):
        for p in range(n):
            u, v, one, two = axes(p)
            uu = (u + OFFS[k]) % 4
            for side, way in ((1, 1), (2, 0)):
                vv = (v + OFFS[side]) % 4
                pair = block(p, spot(p, uu, vv), 2)
                arrive(p, 4 + 4 * k + side, pair)
                send(p, 6 + 4 * k + side, block(p, spot(p, uu, vv) + 1 - way), two[way])
                share(p, 4 * k + side, pair)
    for k in range(4):
        for p in range(n):
            u, v, one, two = axes(p)
            uu, vv = (u + OFFS[k]) % 4, (v + 2) % 4
            arrive(p, 7 + 4 * k, block(p, spot(p, uu, vv) + 0))
            arrive(p, 8 + 4 * k, block(p, spot(p, uu, vv) + 1))
            share(p, 4 * k + 3, block(p, spot(p, uu, vv), 2))
    for p in range(n):
        for k in range(16):
            ref = block(p, (1 - c) * 32 + 2 * k, 2)
            remote(ref, ref, core_send.at[p, k], core_recv.at[p, k], near["c"]).wait_recv()
    for cp in started:
        cp.wait_send()


def gather_blocks(parts, collective_id):
    n, m = len(PIECES), len(WIDTHS)
    return pl.pallas_call(
        gather_kernel,
        out_shape=[jax.ShapeDtypeStruct((64, 16, width), jnp.bfloat16) for width in WIDTHS],
        in_specs=[pl.BlockSpec(memory_space=pl.ANY)] * m,
        out_specs=[pl.BlockSpec(memory_space=pl.ANY)] * m,
        scratch_shapes=[
            pltpu.SemaphoreType.DMA((n,)),
            pltpu.SemaphoreType.DMA((n, 21)),
            pltpu.SemaphoreType.DMA((n, 21)),
            pltpu.SemaphoreType.DMA((n, 16)),
            pltpu.SemaphoreType.DMA((n, 16)),
        ],
        compiler_params=pltpu.CompilerParams(collective_id=collective_id, has_side_effects=True),
    )(*parts)


def add_into(dst, *srcs):
    width = dst.shape[-1]

    def step(i, carry):
        cols = pl.ds(pl.multiple_of(i * 128, 128), 128)
        lead = (slice(None),) * (len(dst.shape) - 1)
        total = srcs[0][(*lead, cols)].astype(jnp.float32)
        for src in srcs[1:]:
            total = total + src[(*lead, cols)].astype(jnp.float32)
        dst[(*lead, cols)] = total.astype(dst.dtype)
        return carry

    lax.fori_loop(0, width // 128, step, 0)


def scatter_kernel(*refs):
    n, m = len(PIECES), len(WIDTHS)
    grads, outs = refs[:m], refs[m : 2 * m]
    refs = refs[2 * m :]
    twins, sums, inner, mids, outer, ends, last = (refs[i * n : (i + 1) * n] for i in range(7))
    send_sem, recv_sem, core_send, core_recv = refs[7 * n :]
    z, y, x, c, t = place_of()
    near = peers(z, y, x, c, t)
    greet(near)
    started = []

    def remote(src, dst, ssem, rsem, peer):
        return pltpu.make_async_remote_copy(
            src_ref=src, dst_ref=dst, send_sem=ssem, recv_sem=rsem, device_id=peer, device_id_type=MESH
        )

    def axes(p):
        if PIECES[p][3] == "z":
            return z, y, near["z"], near["y"]
        return y, z, near["y"], near["z"]

    def spot(p, u, v):
        return u * 8 + v * 2 if PIECES[p][3] == "z" else v * 8 + u * 2

    def grad(p, at, count):
        r, low, width, first = PIECES[p]
        return grads[r].at[pl.ds(at, count), :, pl.ds(low, width)]

    def total(p, at, count):
        return sums[p].at[pl.ds(at, count)]

    def send(p, k, src, dst, peer):
        cp = remote(src, dst, send_sem.at[p, k], recv_sem.at[p, k], peer)
        cp.start()
        started.append(cp)

    def arrive(p, k, ref):
        remote(ref, ref, send_sem.at[p, k], recv_sem.at[p, k], near["x"]).wait_recv()

    order = (3, 2, 1, 0)
    sides = (3, 2, 1, 0)
    for side in sides:
        for k in order:
            for p in range(n):
                u, v, one, two = axes(p)
                at = spot(p, (u + OFFS[k]) % 4, (v + OFFS[side]) % 4)
                j = 4 * k + side
                cp = remote(
                    grad(p, (1 - c) * 32 + at, 2), twins[p].at[pl.ds(at, 2)], core_send.at[p, j], core_recv.at[p, j], near["c"]
                )
                cp.start()
                started.append(cp)

    def combine(p, k, side):
        u, v, one, two = axes(p)
        at = spot(p, (u + OFFS[k]) % 4, (v + OFFS[side]) % 4)
        j = 4 * k + side
        twin = twins[p].at[pl.ds(at, 2)]
        remote(twin, twin, core_send.at[p, j], core_recv.at[p, j], near["c"]).wait_recv()
        add_into(total(p, at, 2), grad(p, c * 32 + at, 2), twin)

    for k in order:
        for p in range(n):
            u, v, one, two = axes(p)
            combine(p, k, 3)
            src = sums[p].at[pl.ds(spot(p, (u + OFFS[k]) % 4, (v + 2) % 4), 2)]
            send(p, 6 * k, src.at[0], inner[p].at[k, 0], two[1])
            send(p, 6 * k + 1, src.at[1], inner[p].at[k, 1], two[0])
    for k in order:
        for p in range(n):
            u, v, one, two = axes(p)
            combine(p, k, 2)
            src = sums[p].at[pl.ds(spot(p, (u + OFFS[k]) % 4, (v + 1) % 4), 2)]
            send(p, 6 * k + 2, src.at[1], inner[p].at[k, 2], two[1])
            combine(p, k, 1)
            src = sums[p].at[pl.ds(spot(p, (u + OFFS[k]) % 4, (v + 3) % 4), 2)]
            send(p, 6 * k + 4, src.at[0], inner[p].at[k, 4], two[0])
    for k in order:
        for p in range(n):
            u, v, one, two = axes(p)
            arrive(p, 6 * k, inner[p].at[k, 0])
            src = sums[p].at[spot(p, (u + OFFS[k]) % 4, (v + 1) % 4) + 0]
            add_into(src, src, inner[p].at[k, 0])
            send(p, 6 * k + 3, src, inner[p].at[k, 3], two[1])
            arrive(p, 6 * k + 1, inner[p].at[k, 1])
            src = sums[p].at[spot(p, (u + OFFS[k]) % 4, (v + 3) % 4) + 1]
            add_into(src, src, inner[p].at[k, 1])
            send(p, 6 * k + 5, src, inner[p].at[k, 5], two[0])
    for k in order:
        for p in range(n):
            combine(p, k, 0)
    for k in order:
        for p in range(n):
            u, v, one, two = axes(p)
            own = sums[p].at[pl.ds(spot(p, (u + OFFS[k]) % 4, v), 2)]
            for j in range(2, 6):
                arrive(p, 6 * k + j, inner[p].at[k, j])
            add_into(mids[p].at[k, 0], own.at[0], inner[p].at[k, 3], inner[p].at[k, 4])
            add_into(mids[p].at[k, 1], own.at[1], inner[p].at[k, 2], inner[p].at[k, 5])
            if k == 3:
                send(p, 24, mids[p].at[3, 0], outer[p].at[0], one[1])
                send(p, 25, mids[p].at[3, 1], outer[p].at[1], one[0])
            if k == 2:
                send(p, 26, mids[p].at[2, 1], outer[p].at[2], one[1])
            if k == 1:
                send(p, 28, mids[p].at[1, 0], outer[p].at[4], one[0])
    for p in range(n):
        u, v, one, two = axes(p)
        arrive(p, 24, outer[p].at[0])
        add_into(mids[p].at[2, 0], mids[p].at[2, 0], outer[p].at[0])
        send(p, 27, mids[p].at[2, 0], outer[p].at[3], one[1])
        arrive(p, 25, outer[p].at[1])
        add_into(mids[p].at[1, 1], mids[p].at[1, 1], outer[p].at[1])
        send(p, 29, mids[p].at[1, 1], outer[p].at[5], one[0])
    for p in range(n):
        for j in range(2, 6):
            arrive(p, 24 + j, outer[p].at[j])
        add_into(ends[p].at[0], mids[p].at[0, 0], outer[p].at[3], outer[p].at[4])
        add_into(ends[p].at[1], mids[p].at[0, 1], outer[p].at[2], outer[p].at[5])
        send(p, 30, ends[p].at[1 - x], last[p], near["x"])
    for p in range(n):
        arrive(p, 30, last[p])
        r, low, width, first = PIECES[p]
        add_into(outs[r].at[:, pl.ds(low, width)], ends[p].at[x], last[p])
    for cp in started:
        cp.wait_send()


def scatter_blocks(parts, collective_id):
    n, m = len(PIECES), len(WIDTHS)

    def room(*lead):
        return [pltpu.VMEM(lead + (16, piece[2]), jnp.bfloat16) for piece in PIECES]

    return pl.pallas_call(
        scatter_kernel,
        out_shape=[jax.ShapeDtypeStruct((16, width), jnp.float32) for width in WIDTHS],
        in_specs=[pl.BlockSpec(memory_space=pltpu.VMEM)] * m,
        out_specs=[pl.BlockSpec(memory_space=pltpu.VMEM)] * m,
        scratch_shapes=[
            *room(32),
            *room(32),
            *room(4, 6),
            *room(4, 2),
            *room(6),
            *room(2),
            *room(),
            pltpu.SemaphoreType.DMA((n, 31)),
            pltpu.SemaphoreType.DMA((n, 31)),
            pltpu.SemaphoreType.DMA((n, 16)),
            pltpu.SemaphoreType.DMA((n, 16)),
        ],
        compiler_params=pltpu.CompilerParams(
            collective_id=collective_id, has_side_effects=True, vmem_limit_bytes=60 * 1024 * 1024
        ),
    )(*parts)


def everyone():
    f, t = lax.axis_index("fsdp"), lax.axis_index("tp")
    me = f * 2 + t
    count = lax.axis_size("fsdp") * lax.axis_size("tp")

    def peer(i):
        other = lax.rem(me + i, count)
        return other, (other // 2, other % 2)

    return me, count, peer


def greet_all(count, peer):
    barrier = pltpu.get_barrier_semaphore()

    def hello(i, carry):
        pl.semaphore_signal(barrier, inc=1, device_id=peer(i)[1], device_id_type=MESH)
        return carry

    lax.fori_loop(1, count, hello, 0)
    pl.semaphore_wait(barrier, count - 1)


def spread(count, peer, source, target, send_sem, recv_sem):
    def go(i, carry):
        other, where = peer(i)
        pltpu.make_async_remote_copy(
            src_ref=source(other),
            dst_ref=target,
            send_sem=send_sem,
            recv_sem=recv_sem,
            device_id=where,
            device_id_type=MESH,
        ).start()
        return carry

    lax.fori_loop(1, count, go, 0)


def settle(count, buffer, sem):
    ref = buffer.at[pl.ds(0, count - 1)]
    pltpu.make_async_copy(ref, ref, sem).wait()


def exchange_kernel(halve, in_ref, out_ref, send_sem, recv_sem):
    me, count, peer = everyone()
    greet_all(count, peer)

    def source(other):
        return in_ref.at[other // 2 if halve else other]

    spread(count, peer, source, out_ref.at[me], send_sem, recv_sem)
    out_ref[me] = source(me)[...]
    settle(count, out_ref, recv_sem)
    settle(count, out_ref, send_sem)


def exchange(parts, halve, count, collective_id):
    return pl.pallas_call(
        functools.partial(exchange_kernel, halve),
        out_shape=jax.ShapeDtypeStruct((count,) + parts.shape[1:], parts.dtype),
        in_specs=[pl.BlockSpec(memory_space=pltpu.VMEM)],
        out_specs=pl.BlockSpec(memory_space=pltpu.VMEM),
        scratch_shapes=[pltpu.SemaphoreType.DMA, pltpu.SemaphoreType.DMA],
        compiler_params=pltpu.CompilerParams(collective_id=collective_id, has_side_effects=True),
    )(parts)


def total_kernel(in_ref, out_ref, held, mine, send_one, recv_one, send_two, recv_two):
    me, count, peer = everyone()
    greet_all(count, peer)
    spread(count, peer, lambda other: in_ref.at[other], held.at[me], send_one, recv_one)
    held[me] = in_ref[me]
    settle(count, held, recv_one)

    def add(i, total):
        return total + held[i]

    total = lax.fori_loop(0, count, add, jnp.zeros(mine.shape, jnp.float32))
    mine[...] = total
    out_ref[me] = total
    spread(count, peer, lambda other: mine, out_ref.at[me], send_two, recv_two)
    settle(count, out_ref, recv_two)
    settle(count, held, send_one)
    settle(count, out_ref, send_two)


def total_everywhere(parts, collective_id):
    return pl.pallas_call(
        total_kernel,
        out_shape=jax.ShapeDtypeStruct(parts.shape, parts.dtype),
        in_specs=[pl.BlockSpec(memory_space=pltpu.VMEM)],
        out_specs=pl.BlockSpec(memory_space=pltpu.VMEM),
        scratch_shapes=[
            pltpu.VMEM(parts.shape, parts.dtype),
            pltpu.VMEM(parts.shape[1:], parts.dtype),
            pltpu.SemaphoreType.DMA,
            pltpu.SemaphoreType.DMA,
            pltpu.SemaphoreType.DMA,
            pltpu.SemaphoreType.DMA,
        ],
        compiler_params=pltpu.CompilerParams(collective_id=collective_id, has_side_effects=True),
    )(parts)


GATE_ROWS = 8
HEAD_LANES = 128


def one_hot(shape, rule):
    first = lax.broadcasted_iota(jnp.int32, shape, 0)
    second = lax.broadcasted_iota(jnp.int32, shape, 1)
    return jnp.where(rule(first, second), 1.0, 0.0).astype(jnp.bfloat16)


def dot(a, b, ca=1, cb=0):
    return lax.dot_general(a, b, (((ca,), (cb,)), ((), ())), preferred_element_type=jnp.float32)


def normed(rows):
    centred = rows - jnp.mean(rows, axis=-1, keepdims=True)
    inverse = lax.rsqrt(jnp.mean(centred * centred, axis=-1, keepdims=True) + norm_eps)
    return centred * inverse, inverse


def norm_back(grad, unit, inverse):
    first = jnp.mean(grad, axis=-1, keepdims=True)
    second = jnp.mean(grad * unit, axis=-1, keepdims=True)
    return inverse * (grad - first - unit * second)


def gelu_slope(u):
    a, b = 0.7978845608028654, 0.044715
    wave = jnp.tanh(a * (u + b * (u * u * u)))
    return 0.5 * (1.0 + wave) + 0.5 * u * (1.0 - wave * wave) * (a * (1.0 + 3.0 * b * (u * u)))


def gelu_value(u):
    a, b = 0.7978845608028654, 0.044715
    return 0.5 * u * (1.0 + jnp.tanh(a * (u + b * (u * u * u))))


def columns_loop(count, body):
    def step(i, carry):
        body(pl.ds(pl.multiple_of(i * 256, 256), 256))
        return carry

    lax.fori_loop(0, count, step, 0)


def middle_kernel(*refs):
    (lat, cot, mods, bias_d, bias_qkv, bias_up, w1, w2, w3, wt) = refs[:10]
    (out, grad_lat, g1, g2, g3, gt, grad_mod, grad_bd, grad_bqkv, grad_bup) = refs[10:20]
    (
        tail_w, tail_g, wide1, wideg, wide2, wideb, flip1, flipg, flip2, flipb,
        narrow_send, narrow_recv, part, qkvp, mixp, probs, gattp, gqkvp, qk, gqkv, att,
        upper, acted, gup, middle, branch, down_keep, unit2, send_sem, recv_sem,
    ) = refs[20:]
    slots = lat.shape[0]
    z, y, x, c, t = place_of()
    partner = (lax.axis_index("fsdp"), 1 - t)
    barrier = pltpu.get_barrier_semaphore()
    pl.semaphore_signal(barrier, inc=1, device_id=partner, device_id_type=MESH)
    pl.semaphore_wait(barrier, 1)

    def remote(k, src, dst):
        return pltpu.make_async_remote_copy(
            src_ref=src, dst_ref=dst, send_sem=send_sem.at[k], recv_sem=recv_sem.at[k],
            device_id=partner, device_id_type=MESH,
        )

    def widen_start(k, wide):
        remote(k, wide.at[:, t], wide.at[:, t]).start()

    def widen_end(k, wide):
        remote(k, wide.at[:, 1 - t], wide.at[:, 1 - t]).wait()
        return wide[...].reshape(256, wide.shape[-1])

    def narrow_start(k, n):
        for s in range(slots):
            narrow_send[n, s] = part[s, 1 - t].astype(jnp.bfloat16)
        remote(k, narrow_send.at[n], narrow_recv.at[n]).start()

    def narrow_end(k, n):
        remote(k, narrow_send.at[n], narrow_recv.at[n]).wait()

    def narrowed(n, s):
        return part[s, t].astype(jnp.bfloat16).astype(jnp.float32) + narrow_recv[n, s].astype(jnp.float32)

    def mod(s, k):
        return mods[s, k : k + 1, :]

    for s in range(slots):
        unit, inverse = normed(lat[s].astype(jnp.float32))
        wide1[s, t] = (unit * (1.0 + mod(s, 1)) + mod(s, 0)).astype(jnp.bfloat16)
    widen_start(0, wide1)
    for s in range(slots):
        grad = cot[s].astype(jnp.float32) * mod(s, 6)
        wideg[s, t] = (mod(s, 5) * grad).astype(jnp.bfloat16)
    widen_start(1, wideg)
    grad_bd[1:2] = sum(jnp.sum(wideg[s, t].astype(jnp.float32), axis=0, keepdims=True) for s in range(slots))

    for j in range(8):
        pick = one_hot((128, 1024), lambda a, b: b == (a // 2) * 16 + (a % 2) * 8 + j)
        tail_w[:, 896 * j : 896 * j + 896] = dot(pick, wt[...].reshape(1024, 896)).astype(jnp.bfloat16)

    h1 = widen_end(0, wide1)
    flip1[...] = h1.T

    def project(rows, w, cols, offset):
        return dot(rows[:, :1024], w[:, :, cols].reshape(1024, 256)) + dot(
            rows[:, 1024:], tail_w[:, pl.ds(pl.multiple_of(offset + cols.start, 256), 256)]
        )

    def to_qkv(cols):
        flat = project(wide1[...].reshape(256, 1152), w1, cols, 0) + bias_qkv[:, cols]
        qk[:, cols] = flat.astype(jnp.bfloat16)

    columns_loop(9, to_qkv)
    for i, lane in enumerate((0, 576, 1152)):
        low = lane // 128 * 128
        spread_heads = one_hot(
            (640, 1024), lambda a, b: (a - (lane - low) == (b // 128) * 72 + b % 128) & (b % 128 < 72)
        )
        qkvp[i] = dot(qk[:, low : low + 640], spread_heads).astype(jnp.bfloat16)

    factor = 72 ** (-0.5)

    def attend(i, carry):
        rows = pl.ds(pl.multiple_of(i * 128, 128), 128)
        for h in range(8):
            lanes = slice(128 * h, 128 * h + 128)
            q, k, v = qkvp[0, rows, lanes], qkvp[1, rows, lanes], qkvp[2, rows, lanes]
            scores = dot(q, k, 1, 1) * factor
            raised = jnp.exp(scores - jnp.max(scores, axis=-1, keepdims=True))
            prob = raised / jnp.sum(raised, axis=-1, keepdims=True)
            probs[i, h] = prob
            mixp[rows, lanes] = dot(prob.astype(jnp.bfloat16), v).astype(jnp.bfloat16)
        return carry

    lax.fori_loop(0, slots, attend, 0)
    join = one_hot((1024, 640), lambda a, b: (b - 64 == (a // 128) * 72 + a % 128) & (a % 128 < 72))
    att[...] = dot(mixp[...], join).astype(jnp.bfloat16)

    def back_to_width(rows, w, cols, tail_cols, add):
        total = dot(rows, w[:, :, cols].reshape(1024, -1), 1, 1)
        tail = dot(rows, tail_w[:, tail_cols], 1, 1)
        main = part.at[:, :, :, 0:1024]
        rest = part.at[:, :, :, 1024:1152]
        total, tail = total.reshape(slots, 2, 64, 1024), tail.reshape(slots, 2, 64, 128)
        main[...] = main[...] + total if add else total
        rest[...] = rest[...] + tail if add else tail

    back_to_width(att[...], w1, slice(1664, 2304), slice(1664, 2304), False)
    narrow_start(2, 0)
    narrow_end(2, 0)
    for s in range(slots):
        piece = narrowed(0, s) + bias_d[0:1]
        branch[s] = piece
        rows = lat[s].astype(jnp.float32) + mod(s, 2) * piece
        middle[s] = rows
        unit, inverse = normed(rows)
        wide2[s, t] = (unit * (1.0 + mod(s, 4)) + mod(s, 3)).astype(jnp.bfloat16)
    widen_start(3, wide2)
    gd = widen_end(1, wideg)
    flipg[...] = gd.T
    h2 = widen_end(3, wide2)
    flip2[...] = h2.T

    def feed(cols):
        up = project(wide2[...].reshape(256, 1152), w2, cols, 2304) + bias_up[:, cols]
        upper[:, cols] = up
        acted[:, cols] = gelu_value(up).astype(jnp.bfloat16)

    columns_loop(9, feed)
    back_to_width(acted[...], w3, slice(0, 2304), slice(4608, 6912), False)
    narrow_start(4, 1)
    for s in range(slots):
        down_keep[s] = part[s, t]

    def feed_back(cols):
        grad = project(wideg[...].reshape(256, 1152), w3, cols, 4608)
        low = (grad * gelu_slope(upper[:, cols])).astype(jnp.bfloat16)
        gup[:, cols] = low
        grad_bup[:, cols] = jnp.sum(low.astype(jnp.float32), axis=0, keepdims=True)

    columns_loop(9, feed_back)

    back_to_width(gup[...], w2, slice(0, 2304), slice(2304, 4608), False)
    narrow_start(5, 2)

    def weight_grad(flip, rows, cols, g, offset):
        made = dot(flip[...], rows[:, cols]).astype(jnp.bfloat16)
        g[:, :, cols] = made[:1024].reshape(64, 16, 256)
        tail_g[:, pl.ds(pl.multiple_of(offset + cols.start, 256), 256)] = made[1024:]

    columns_loop(9, lambda cols: weight_grad(flipg, acted, cols, g3, 4608))
    columns_loop(9, lambda cols: weight_grad(flip2, gup, cols, g2, 2304))

    narrow_end(4, 1)
    for s in range(slots):
        grad = cot[s].astype(jnp.float32) * mod(s, 6)
        down = down_keep[s].astype(jnp.bfloat16).astype(jnp.float32) + narrow_recv[1, s].astype(jnp.float32)
        down = down + bias_d[1:2]
        out[s] = ((middle[s] + mod(s, 5) * down) * mod(s, 6)).astype(jnp.bfloat16)
        grad_mod[s, 5:6] = jnp.sum(grad * down, axis=0, keepdims=True)
    narrow_end(5, 2)
    for s in range(slots):
        grad = cot[s].astype(jnp.float32) * mod(s, 6)
        gh = narrowed(2, s)
        unit, inverse = normed(middle[s])
        grad_mod[s, 3:4] = jnp.sum(gh, axis=0, keepdims=True)
        grad_mod[s, 4:5] = jnp.sum(gh * unit, axis=0, keepdims=True)
        gm = grad + norm_back(gh * (1.0 + mod(s, 4)), unit, inverse)
        grad_mod[s, 2:3] = jnp.sum(gm * branch[s], axis=0, keepdims=True)
        middle[s] = gm
        wideb[s, t] = (mod(s, 2) * gm).astype(jnp.bfloat16)
    widen_start(6, wideb)
    grad_bd[0:1] = sum(jnp.sum(wideb[s, t].astype(jnp.float32), axis=0, keepdims=True) for s in range(slots))
    gb = widen_end(6, wideb)
    flipb[...] = gb.T
    gatt = dot(gb[:, :1024], w1[:, :, 1664:2304].reshape(1024, 640)) + dot(gb[:, 1024:], tail_w[:, 1664:2304])
    gattp[...] = dot(gatt.astype(jnp.bfloat16), join, 1, 1).astype(jnp.bfloat16)

    def attend_back(i, carry):
        rows = pl.ds(pl.multiple_of(i * 128, 128), 128)
        for h in range(8):
            lanes = slice(128 * h, 128 * h + 128)
            q, k, v = qkvp[0, rows, lanes], qkvp[1, rows, lanes], qkvp[2, rows, lanes]
            ga = gattp[rows, lanes]
            prob = probs[i, h]
            grad = dot(ga, v, 1, 1)
            inner = jnp.sum(prob * grad, axis=-1, keepdims=True)
            gs = (prob * (grad - inner)).astype(jnp.bfloat16)
            gqkvp[0, rows, lanes] = (dot(gs, k) * factor).astype(jnp.bfloat16)
            gqkvp[1, rows, lanes] = (dot(gs, q, 0, 0) * factor).astype(jnp.bfloat16)
            gqkvp[2, rows, lanes] = dot(prob.astype(jnp.bfloat16), ga, 0, 0).astype(jnp.bfloat16)
        return carry

    lax.fori_loop(0, slots, attend_back, 0)
    gqkv[...] = jnp.zeros_like(gqkv)
    for i, lane in enumerate((0, 576, 1152)):
        low = lane // 128 * 128
        gather_heads = one_hot(
            (1024, 640), lambda a, b: (b - (lane - low) == (a // 128) * 72 + a % 128) & (a % 128 < 72)
        )
        piece = dot(gqkvp[i], gather_heads).astype(jnp.bfloat16)
        gqkv[:, low : low + 640] = gqkv[:, low : low + 640] + piece
    grad_bqkv[...] = jnp.sum(gqkv[...].astype(jnp.float32), axis=0, keepdims=True)
    back_to_width(gqkv[...], w1, slice(0, 1792), slice(0, 1792), False)
    narrow_start(7, 3)

    columns_loop(6, lambda cols: weight_grad(flip1, gqkv, cols, g1, 0))
    for low, high in ((1536, 1664), (1664, 1792), (1792, 2304)):
        made = 0.0
        if low < 1792:
            made = made + dot(flip1[...], gqkv[:, low:high])
        if high > 1664:
            made = made + dot(flipb[...], att[:, low - 1664 : high - 1664])
        made = made.astype(jnp.bfloat16)
        g1[:, :, low:high] = made[:1024].reshape(64, 16, high - low)
        tail_g[:, low:high] = made[1024:]
    tail_g[:, 6912:] = jnp.zeros((128, 256), jnp.bfloat16)
    total = jnp.zeros((1024, 896), jnp.float32)
    for j in range(8):
        pick = one_hot((1024, 128), lambda a, b: a == (b // 2) * 16 + (b % 2) * 8 + j)
        total = total + dot(pick, tail_g[:, 896 * j : 896 * j + 896])
    gt[...] = total.astype(jnp.bfloat16).reshape(64, 16, 896)

    narrow_end(7, 3)
    for s in range(slots):
        gh = narrowed(3, s)
        unit, inverse = normed(lat[s].astype(jnp.float32))
        grad_mod[s, 0:1] = jnp.sum(gh, axis=0, keepdims=True)
        grad_mod[s, 1:2] = jnp.sum(gh * unit, axis=0, keepdims=True)
        grad_lat[s] = middle[s] + norm_back(gh * (1.0 + mod(s, 1)), unit, inverse)
        grad_mod[s, 6:8] = jnp.zeros((2, 1152), jnp.float32)


def middle_block(args, collective_id):
    f32, bf = jnp.float32, jnp.bfloat16
    vmem = pl.BlockSpec(memory_space=pltpu.VMEM)
    shape = jax.ShapeDtypeStruct
    return pl.pallas_call(
        middle_kernel,
        out_shape=[
            shape((2, 64, 1152), bf), shape((2, 64, 1152), f32),
            shape((64, 16, 2304), bf), shape((64, 16, 2304), bf), shape((64, 16, 2304), bf), shape((64, 16, 896), bf),
            shape((2, 8, 1152), f32), shape((2, 1152), f32), shape((1, 1792), f32), shape((1, 2304), f32),
        ],
        in_specs=[vmem] * len(args),
        out_specs=[vmem] * 10,
        scratch_shapes=[
            pltpu.VMEM((128, 7168), bf), pltpu.VMEM((128, 7168), bf),
            *[pltpu.VMEM((2, 2, 64, 1152), bf)] * 4,
            *[pltpu.VMEM((1152, 256), bf)] * 4,
            pltpu.VMEM((4, 2, 64, 1152), bf), pltpu.VMEM((4, 2, 64, 1152), bf),
            pltpu.VMEM((2, 2, 64, 1152), f32),
            pltpu.VMEM((3, 256, 1024), bf), pltpu.VMEM((256, 1024), bf), pltpu.VMEM((2, 8, 128, 128), f32),
            pltpu.VMEM((256, 1024), bf), pltpu.VMEM((3, 256, 1024), bf),
            pltpu.VMEM((256, 2304), bf), pltpu.VMEM((256, 1792), bf), pltpu.VMEM((256, 640), bf),
            pltpu.VMEM((256, 2304), f32), pltpu.VMEM((256, 2304), bf), pltpu.VMEM((256, 2304), bf),
            *[pltpu.VMEM((2, 64, 1152), f32)] * 4,
            pltpu.SemaphoreType.DMA((8,)), pltpu.SemaphoreType.DMA((8,)),
        ],
        compiler_params=pltpu.CompilerParams(
            collective_id=collective_id, has_side_effects=True, vmem_limit_bytes=62 * 1024 * 1024
        ),
    )(*args)


MAIN = 1024
CHUNK = 896


def shuffle_matrix(width):
    place = jnp.arange(width, dtype=jnp.int32)
    tail = place - MAIN
    block = jnp.where(place < MAIN, place // 16, tail // 2)
    row = jnp.where(place < MAIN, place % 16, 16 + tail % 2)
    fsdp = ((block // 8) % 4) * 16 + ((block // 2) % 4) * 4 + (block % 2) * 2 + block // 32
    source = fsdp * 18 + row
    return (jnp.arange(width, dtype=jnp.int32)[:, None] == source[None, :]).astype(jnp.bfloat16)


def shuffled(rows, matrix):
    return jnp.einsum("...d,de->...e", rows, matrix, preferred_element_type=jnp.float32).astype(jnp.bfloat16)


def shuffled_wide(rows, matrix):
    return jnp.einsum("...d,de->...e", rows, matrix.astype(jnp.float32), precision=highest)


def straight(rows, matrix):
    return jnp.einsum("...e,de->...d", rows, matrix, preferred_element_type=jnp.float32).astype(jnp.bfloat16)


def straight_wide(rows, matrix):
    return jnp.einsum("...e,de->...d", rows, matrix.astype(jnp.float32), precision=highest)


def pack_rows(all_rows):
    third = all_rows.shape[1] // 3
    main, tail = all_rows[:16], all_rows[16:]
    tail = jnp.pad(tail, ((0, 0), (0, 8 * CHUNK - tail.shape[1]))).reshape(1, 16, CHUNK)
    return [*(main[None, :, i * third : (i + 1) * third] for i in range(3)), tail]


def unpack_rows(one, two, three, tail):
    width = one.shape[1] * 3
    main = jnp.concatenate([one, two, three], axis=1)
    return jnp.concatenate([main, tail.reshape(2, 8 * CHUNK)[:, :width]], axis=0)


def local(
    latents,
    condition,
    counts,
    order,
    w_ada,
    b_ada,
    w_qkv,
    b_qv,
    w_proj,
    b_proj,
    w_up,
    b_up,
    w_down,
    b_down,
    cotangent,
):
    slots = latents.shape[0]
    latent_count = condition.shape[0]
    group = lax.axis_index("fsdp")
    ranks = jnp.arange(counts.shape[0], dtype=jnp.int32)
    held = jnp.sum(jnp.where(ranks == group, counts, 0))
    before = jnp.sum(jnp.where(ranks < group, counts, 0))
    slot_rank = jnp.arange(slots, dtype=jnp.int32)
    live = (slot_rank < held).astype(jnp.float32)
    place = jnp.clip(before + slot_rank, 0, latent_count - 1)
    numbers = jnp.arange(latent_count, dtype=jnp.int32)
    owner = jnp.sum(jnp.where(numbers[None, :] == place[:, None], order[None, :], 0), axis=1)
    offsets = jnp.cumsum(counts) - counts
    every = jnp.clip(offsets[:, None] + slot_rank[None, :], 0, latent_count - 1).reshape(-1)
    owners = jnp.sum(jnp.where(numbers[None, :] == every[:, None], order[None, :], 0), axis=1)
    choose_all = (numbers[None, :] == owners[:, None]).astype(jnp.bfloat16)
    groups = counts.shape[0]
    devices = groups * 2
    matrix = shuffle_matrix(latents.shape[2])
    soft_cond = jax.nn.silu(condition.astype(jnp.float32))
    ada_local = w_ada.astype(jnp.float32)
    mod_part = jnp.einsum("nd,dke->nke", soft_cond, ada_local, precision=highest) + b_ada
    mod_low = mod_part.astype(jnp.bfloat16).reshape(latent_count, -1)
    mod_send = jnp.dot(choose_all, mod_low, preferred_element_type=jnp.float32).astype(jnp.bfloat16)
    columns = mod_part.shape[2]
    mod_send = jnp.pad(mod_send.reshape(groups, slots, -1), ((0, 0), (0, 16 - slots), (0, 128 - 6 * columns)))
    mod_got = exchange(mod_send, True, devices, 1)[:, :slots, : 6 * columns]
    slot_mod = jnp.transpose(mod_got.reshape(devices, slots, 6, columns), (1, 2, 0, 3)).reshape(slots, 6, -1)
    slot_mod = shuffled(slot_mod, matrix).astype(jnp.float32)
    rows = shuffled(latents, matrix)
    cotangent = shuffled(cotangent, matrix)
    bias_d = shuffled_wide(jnp.stack([b_proj, b_down]), matrix)
    own_rows = jnp.concatenate([w_qkv[0], w_qkv[1], w_qkv[2], w_proj.T, w_up, w_down.T], axis=1)
    width = own_rows.shape[1]
    head_part = w_qkv.shape[2]
    weights = gather_blocks(pack_rows(own_rows), 2)
    mods = jnp.concatenate(
        [slot_mod, jnp.broadcast_to(live[:, None, None], (slots, 2, slot_mod.shape[2]))], axis=1
    )
    nothing = jnp.zeros_like(b_qv[0])
    bias_qkv = jnp.concatenate([b_qv[0], nothing, b_qv[1], nothing])[None]
    block_output, grad_latents, *grads, grad_mod, grad_bd, grad_bqkv, grad_bup = middle_block(
        (rows, cotangent, mods, bias_d, bias_qkv, b_up[None], *weights), 6
    )
    block_output = straight(block_output, matrix)
    grad_latents = straight_wide(grad_latents, matrix)
    grad_b_qv_local = jnp.stack([grad_bqkv[0, :head_part], grad_bqkv[0, 2 * head_part : 3 * head_part]])
    grad_b_up_local = grad_bup[0]
    grad_b_proj, grad_b_down = grad_bd[0], grad_bd[1]
    summed = unpack_rows(*scatter_blocks(grads, 3))
    grad_w_qkv = jnp.stack([summed[:, i * head_part : (i + 1) * head_part] for i in range(3)])
    grad_w_proj = summed[:, 3 * head_part : 4 * head_part].T
    up_part = w_up.shape[1]
    grad_w_up = summed[:, 4 * head_part : 4 * head_part + up_part]
    grad_w_down = summed[:, 4 * head_part + up_part :].T
    grad_mod = grad_mod[:, :6]
    grad_mod = straight_wide(grad_mod, matrix).reshape(slots, 6, devices, columns)
    grad_send = jnp.transpose(grad_mod, (2, 0, 1, 3)).reshape(devices, slots, 6 * columns)
    grad_send = jnp.pad(grad_send, ((0, 0), (0, 8 - slots), (0, 128 - 6 * columns)))
    grad_got = exchange(grad_send, False, devices, 4)[:, :slots, : 6 * columns]
    grad_got = jnp.sum(grad_got.reshape(groups, 2, slots, 6 * columns), axis=1).reshape(groups * slots, -1)
    alive_all = (slot_rank[None, :] < counts[:, None]).reshape(-1, 1)
    grad_mod_part = jnp.einsum(
        "sn,se->ne",
        choose_all.astype(jnp.float32),
        jnp.where(alive_all, grad_got, 0.0),
        precision=highest,
    ).reshape(latent_count, 6, columns)
    grad_b_ada = jnp.sum(grad_mod_part, axis=0)
    grad_w_ada = jnp.einsum("nd,nke->dke", soft_cond, grad_mod_part, precision=highest)
    grad_soft_part = jnp.einsum("nke,dke->nd", grad_mod_part, ada_local, precision=highest)
    tensor_rank = lax.axis_index("tp")
    zero_index = jnp.zeros((), jnp.int32)
    up_half = grad_b_up_local.shape[0]
    qv_place = lax.dynamic_update_slice(
        jnp.zeros((2, head_part * lax.axis_size("tp")), jnp.float32),
        grad_b_qv_local,
        (zero_index, tensor_rank * head_part),
    )
    up_place = lax.dynamic_update_slice(
        jnp.zeros((up_half * lax.axis_size("tp"),), jnp.float32),
        grad_b_up_local,
        (tensor_rank * up_half,),
    )
    sums = [grad_soft_part, grad_b_proj, grad_b_down, qv_place, up_place]
    flat = jnp.concatenate([each.reshape(-1) for each in sums])
    flat = jnp.pad(flat, (0, devices * 1024 - flat.shape[0])).reshape(devices, 8, 128)
    flat = total_everywhere(flat, 5).reshape(-1)
    parts, start = [], 0
    for each in sums:
        parts.append(flat[start : start + each.size].reshape(each.shape))
        start += each.size
    grad_soft, grad_b_proj, grad_b_down, qv_full, up_full = parts
    grad_b_proj, grad_b_down = straight_wide(jnp.stack([grad_b_proj, grad_b_down]), matrix)
    grad_b_qv = lax.dynamic_slice_in_dim(qv_full, tensor_rank * head_part, head_part, 1)
    grad_b_up = lax.dynamic_slice_in_dim(up_full, tensor_rank * up_half, up_half, 0)
    grad_condition = jax.vjp(jax.nn.silu, condition.astype(jnp.float32))[1](grad_soft)[0]
    return (
        block_output,
        grad_latents,
        grad_condition,
        grad_w_ada,
        grad_b_ada,
        grad_w_qkv,
        grad_b_qv,
        grad_w_proj,
        grad_b_proj,
        grad_w_up,
        grad_b_up,
        grad_w_down,
        grad_b_down,
    )


def solution(mesh):
    in_specs = (
        P("fsdp", "tp", None),
        P(),
        P(),
        P(),
        P(None, None, ("fsdp", "tp")),
        P(None, ("fsdp", "tp")),
        P(None, "fsdp", "tp"),
        P(None, "tp"),
        P("tp", "fsdp"),
        P(),
        P("fsdp", "tp"),
        P("tp"),
        P("tp", "fsdp"),
        P(),
        P("fsdp", "tp", None),
    )
    out_specs = (
        P("fsdp", "tp", None),
        P("fsdp", "tp", None),
        P(),
        P(None, None, ("fsdp", "tp")),
        P(None, ("fsdp", "tp")),
        P(None, "fsdp", "tp"),
        P(None, "tp"),
        P("tp", "fsdp"),
        P(),
        P("fsdp", "tp"),
        P("tp"),
        P("tp", "fsdp"),
        P(),
    )
    return jax.shard_map(local, mesh=mesh, in_specs=in_specs, out_specs=out_specs, check_vma=False)
```

```python
import functools

import jax
import jax.numpy as jnp
from jax import lax
from jax.experimental import pallas as pl
from jax.experimental.pallas import tpu as pltpu
from jax.sharding import PartitionSpec as P

MESH = pl.DeviceIdType.MESH
OFFS = (0, 3, 1, 2)
WIDTHS = (2304, 2304, 2304, 896)
PIECES = (
    (3, 0, 896, "z"),
    (0, 0, 1152, "z"),
    (0, 1152, 1152, "y"),
    (1, 0, 1152, "z"),
    (1, 1152, 1152, "y"),
    (2, 0, 1152, "z"),
    (2, 1152, 1152, "y"),
)
ONE, TWO, THREE = (0, 1, 2), (3, 4), (5, 6)
ALL = ONE + TWO + THREE
BACK = (3, 2, 1, 0)


highest = lax.Precision.HIGHEST
norm_eps = 1e-06


def place_of():
    f = lax.axis_index("fsdp")
    return f // 16, (f // 4) % 4, (f // 2) % 2, f % 2, lax.axis_index("tp")


def peers(z, y, x, c, t):
    def at(z, y, x, c):
        return (z * 16 + y * 4 + x * 2 + c, t)

    return {
        "z": (at((z + 3) % 4, y, x, c), at((z + 1) % 4, y, x, c)),
        "y": (at(z, (y + 3) % 4, x, c), at(z, (y + 1) % 4, x, c)),
        "x": at(z, y, 1 - x, c),
        "c": at(z, y, x, 1 - c),
        "t": (z * 16 + y * 4 + x * 2 + c, 1 - t),
    }


def greet(near):
    barrier = pltpu.get_barrier_semaphore()
    group = (*near["z"], *near["y"], near["x"], near["c"], near["t"])
    for peer in group:
        pl.semaphore_signal(barrier, inc=1, device_id=peer, device_id_type=MESH)
    pl.semaphore_wait(barrier, len(group))


def add_into(dst, *srcs):
    width = dst.shape[-1]

    def step(i, carry):
        cols = pl.ds(pl.multiple_of(i * 128, 128), 128)
        lead = (slice(None),) * (len(dst.shape) - 1)
        total = srcs[0][(*lead, cols)].astype(jnp.float32)
        for src in srcs[1:]:
            total = total + src[(*lead, cols)].astype(jnp.float32)
        dst[(*lead, cols)] = total.astype(dst.dtype)
        return carry

    lax.fori_loop(0, width // 128, step, 0)


def everyone():
    f, t = lax.axis_index("fsdp"), lax.axis_index("tp")
    me = f * 2 + t
    count = lax.axis_size("fsdp") * lax.axis_size("tp")

    def peer(i):
        other = lax.rem(me + i, count)
        return other, (other // 2, other % 2)

    return me, count, peer


def greet_all(count, peer):
    barrier = pltpu.get_barrier_semaphore()

    def hello(i, carry):
        pl.semaphore_signal(barrier, inc=1, device_id=peer(i)[1], device_id_type=MESH)
        return carry

    lax.fori_loop(1, count, hello, 0)
    pl.semaphore_wait(barrier, count - 1)


def spread(count, peer, source, target, send_sem, recv_sem):
    def go(i, carry):
        other, where = peer(i)
        pltpu.make_async_remote_copy(
            src_ref=source(other),
            dst_ref=target,
            send_sem=send_sem,
            recv_sem=recv_sem,
            device_id=where,
            device_id_type=MESH,
        ).start()
        return carry

    lax.fori_loop(1, count, go, 0)


def settle(count, buffer, sem):
    ref = buffer.at[pl.ds(0, count - 1)]
    pltpu.make_async_copy(ref, ref, sem).wait()


def exchange_kernel(halve, in_ref, out_ref, send_sem, recv_sem):
    me, count, peer = everyone()
    greet_all(count, peer)

    def source(other):
        return in_ref.at[other // 2 if halve else other]

    spread(count, peer, source, out_ref.at[me], send_sem, recv_sem)
    out_ref[me] = source(me)[...]
    settle(count, out_ref, recv_sem)
    settle(count, out_ref, send_sem)


def exchange(parts, halve, count, collective_id):
    return pl.pallas_call(
        functools.partial(exchange_kernel, halve),
        out_shape=jax.ShapeDtypeStruct((count,) + parts.shape[1:], parts.dtype),
        in_specs=[pl.BlockSpec(memory_space=pltpu.VMEM)],
        out_specs=pl.BlockSpec(memory_space=pltpu.VMEM),
        scratch_shapes=[pltpu.SemaphoreType.DMA, pltpu.SemaphoreType.DMA],
        compiler_params=pltpu.CompilerParams(collective_id=collective_id, has_side_effects=True),
    )(parts)


def total_kernel(in_ref, out_ref, held, mine, send_one, recv_one, send_two, recv_two):
    me, count, peer = everyone()
    greet_all(count, peer)
    spread(count, peer, lambda other: in_ref.at[other], held.at[me], send_one, recv_one)
    held[me] = in_ref[me]
    settle(count, held, recv_one)

    def add(i, total):
        return total + held[i]

    total = lax.fori_loop(0, count, add, jnp.zeros(mine.shape, jnp.float32))
    mine[...] = total
    out_ref[me] = total
    spread(count, peer, lambda other: mine, out_ref.at[me], send_two, recv_two)
    settle(count, out_ref, recv_two)
    settle(count, held, send_one)
    settle(count, out_ref, send_two)


def total_everywhere(parts, collective_id):
    return pl.pallas_call(
        total_kernel,
        out_shape=jax.ShapeDtypeStruct(parts.shape, parts.dtype),
        in_specs=[pl.BlockSpec(memory_space=pltpu.VMEM)],
        out_specs=pl.BlockSpec(memory_space=pltpu.VMEM),
        scratch_shapes=[
            pltpu.VMEM(parts.shape, parts.dtype),
            pltpu.VMEM(parts.shape[1:], parts.dtype),
            pltpu.SemaphoreType.DMA,
            pltpu.SemaphoreType.DMA,
            pltpu.SemaphoreType.DMA,
            pltpu.SemaphoreType.DMA,
        ],
        compiler_params=pltpu.CompilerParams(collective_id=collective_id, has_side_effects=True),
    )(parts)


GATE_ROWS = 8
HEAD_LANES = 128


def one_hot(shape, rule):
    first = lax.broadcasted_iota(jnp.int32, shape, 0)
    second = lax.broadcasted_iota(jnp.int32, shape, 1)
    return jnp.where(rule(first, second), 1.0, 0.0).astype(jnp.bfloat16)


def dot(a, b, ca=1, cb=0):
    return lax.dot_general(a, b, (((ca,), (cb,)), ((), ())), preferred_element_type=jnp.float32)


def normed(rows):
    centred = rows - jnp.mean(rows, axis=-1, keepdims=True)
    inverse = lax.rsqrt(jnp.mean(centred * centred, axis=-1, keepdims=True) + norm_eps)
    return centred * inverse, inverse


def norm_back(grad, unit, inverse):
    first = jnp.mean(grad, axis=-1, keepdims=True)
    second = jnp.mean(grad * unit, axis=-1, keepdims=True)
    return inverse * (grad - first - unit * second)


def gelu_slope(u):
    a, b = 0.7978845608028654, 0.044715
    wave = jnp.tanh(a * (u + b * (u * u * u)))
    return 0.5 * (1.0 + wave) + 0.5 * u * (1.0 - wave * wave) * (a * (1.0 + 3.0 * b * (u * u)))


def gelu_value(u):
    a, b = 0.7978845608028654, 0.044715
    return 0.5 * u * (1.0 + jnp.tanh(a * (u + b * (u * u * u))))


def columns_loop(count, body):
    def step(i, carry):
        body(pl.ds(pl.multiple_of(i * 256, 256), 256))
        return carry

    lax.fori_loop(0, count, step, 0)


def block_kernel(*refs):
    n, m = len(PIECES), len(WIDTHS)
    (lat, cot, mods, bias_d, bias_qkv, bias_up), ins = refs[:6], refs[6 : 6 + m]
    refs = refs[6 + m :]
    (out, grad_lat), outs, (grad_mod, grad_bd, grad_bqkv, grad_bup) = refs[:2], refs[2 : 2 + m], refs[2 + m : 6 + m]
    refs = refs[6 + m :]
    ws, twins = refs[:m], refs[m : 2 * m]
    refs = refs[2 * m :]
    inner, outer, last = (refs[i * n : (i + 1) * n] for i in range(3))
    (
        tail_w, tail_g, wide1, wideg, wide2, wideb, flip1, flipg, flip2, flipb,
        narrow_send, narrow_recv, part, qkvp, probs, gattp, qk, gqkv, att,
        upper, acted, gup, middle, branch, down_keep, send_sem, recv_sem,
        local_sem, way_send, core_send, way_recv, core_recv, back_recv, back_core,
    ) = refs[3 * n :]
    w1, w2, w3, wt = ws
    slots = lat.shape[0]
    z, y, x, c, t = place_of()
    near = peers(z, y, x, c, t)
    partner = near["t"]
    greet(near)
    pending = {p: [] for p in range(n)}

    def far(src, dst, ssem, rsem, peer):
        return pltpu.make_async_remote_copy(
            src_ref=src, dst_ref=dst, send_sem=ssem, recv_sem=rsem, device_id=peer, device_id_type=MESH
        )

    def axes(p):
        if PIECES[p][3] == "z":
            return z, y, near["z"], near["y"]
        return y, z, near["y"], near["z"]

    def spot(p, u, v, core=c):
        return core * 32 + (u * 8 + v * 2 if PIECES[p][3] == "z" else v * 8 + u * 2)

    def block(p, at, count=1, of=ws):
        r, low, width, first = PIECES[p]
        return of[r].at[pl.ds(at, count), :, pl.ds(low, width)]

    def push(p, k, ref, peer, src=None):
        cp = far(ref if src is None else src, ref, way_send.at[p, k], way_recv.at[p, k], peer)
        cp.start()
        pending[p].append(cp)

    def arrive(p, k, ref):
        far(ref, ref, way_send.at[p, k], way_recv.at[p, k], near["x"]).wait_recv()

    def share(p, k, ref):
        cp = far(ref, ref, core_send.at[p, k], core_recv.at[p, k], near["c"])
        cp.start()
        pending[p].append(cp)

    def gather_begin(p):
        r, low, width, first = PIECES[p]
        mine = ins[r].at[:, :, pl.ds(low, width)]
        own = block(p, c * 32 + z * 8 + y * 2 + x)
        push(p, 0, own, near["x"], mine)
        pltpu.make_async_copy(mine, own, local_sem.at[p]).start()

    def gather_x(p):
        u, v, one, two = axes(p)
        r, low, width, first = PIECES[p]
        own = block(p, c * 32 + z * 8 + y * 2 + x)
        pltpu.make_async_copy(ins[r].at[:, :, pl.ds(low, width)], own, local_sem.at[p]).wait()
        arrive(p, 0, block(p, c * 32 + z * 8 + y * 2 + 1 - x))
        pair = block(p, spot(p, u, v), 2)
        push(p, 1, pair, one[1])
        push(p, 2, pair, one[0])
        share(p, 0, pair)

    def gather_first(p):
        u, v, one, two = axes(p)
        for k, way in ((1, 1), (2, 0)):
            uu = (u + OFFS[k]) % 4
            pair = block(p, spot(p, uu, v), 2)
            arrive(p, k, pair)
            push(p, 2 + k, block(p, spot(p, uu, v) + 1 - way), one[way])
            share(p, 4 * k, pair)

    def gather_first_end(p):
        u, v, one, two = axes(p)
        uu = (u + 2) % 4
        arrive(p, 3, block(p, spot(p, uu, v)))
        arrive(p, 4, block(p, spot(p, uu, v) + 1))
        share(p, 12, block(p, spot(p, uu, v), 2))

    def gather_second(p, ks):
        u, v, one, two = axes(p)
        for k in ks:
            pair = block(p, spot(p, (u + OFFS[k]) % 4, v), 2)
            push(p, 5 + 4 * k, pair, two[1])
            push(p, 6 + 4 * k, pair, two[0])

    def gather_relay(p, ks):
        u, v, one, two = axes(p)
        for k in ks:
            uu = (u + OFFS[k]) % 4
            for side, way in ((1, 1), (2, 0)):
                vv = (v + OFFS[side]) % 4
                pair = block(p, spot(p, uu, vv), 2)
                arrive(p, 4 + 4 * k + side, pair)
                push(p, 6 + 4 * k + side, block(p, spot(p, uu, vv) + 1 - way), two[way])
                share(p, 4 * k + side, pair)

    def gather_end(p, ks):
        u, v, one, two = axes(p)
        for k in ks:
            uu, vv = (u + OFFS[k]) % 4, (v + 2) % 4
            arrive(p, 7 + 4 * k, block(p, spot(p, uu, vv)))
            arrive(p, 8 + 4 * k, block(p, spot(p, uu, vv) + 1))
            share(p, 4 * k + 3, block(p, spot(p, uu, vv), 2))

    def gather_core(p):
        for k in range(16):
            ref = block(p, (1 - c) * 32 + 2 * k, 2)
            far(ref, ref, core_send.at[p, k], core_recv.at[p, k], near["c"]).wait_recv()

    def sent(p):
        for cp in pending[p]:
            cp.wait_send()
        pending[p].clear()

    def back(p, k, src, dst, peer):
        cp = far(src, dst, way_send.at[p, k], back_recv.at[p, k], peer)
        cp.start()
        pending[p].append(cp)

    def came(p, k, ref):
        far(ref, ref, way_send.at[p, k], back_recv.at[p, k], near["x"]).wait_recv()

    def twin_of(p, at):
        return block(p, at, 2, twins)

    def scatter_twin(p):
        u, v, one, two = axes(p)
        for side in BACK:
            for k in BACK:
                at = spot(p, (u + OFFS[k]) % 4, (v + OFFS[side]) % 4, 0)
                j = 4 * k + side
                cp = far(block(p, (1 - c) * 32 + at, 2), twin_of(p, at), core_send.at[p, j], back_core.at[p, j], near["c"])
                cp.start()
                pending[p].append(cp)

    def combine(p, k, side):
        u, v, one, two = axes(p)
        at = spot(p, (u + OFFS[k]) % 4, (v + OFFS[side]) % 4, 0)
        j = 4 * k + side
        twin = twin_of(p, at)
        far(twin, twin, core_send.at[p, j], back_core.at[p, j], near["c"]).wait_recv()
        own = block(p, c * 32 + at, 2)
        add_into(own, own, twin)
        return c * 32 + at

    def scatter_relay(p, ks):
        u, v, one, two = axes(p)
        for k in ks:
            at = combine(p, k, 3)
            back(p, 6 * k, block(p, at), inner[p].at[k, pl.ds(0, 1)], two[1])
            back(p, 6 * k + 1, block(p, at + 1), inner[p].at[k, pl.ds(1, 1)], two[0])

    def scatter_direct(p, ks):
        u, v, one, two = axes(p)
        for k in ks:
            at = combine(p, k, 2)
            back(p, 6 * k + 2, block(p, at + 1), inner[p].at[k, pl.ds(2, 1)], two[1])
            at = combine(p, k, 1)
            back(p, 6 * k + 4, block(p, at), inner[p].at[k, pl.ds(4, 1)], two[0])

    def scatter_on(p, ks):
        u, v, one, two = axes(p)
        for k in ks:
            for j, side, way in ((0, 2, 1), (1, 1, 0)):
                came(p, 6 * k + j, inner[p].at[k, pl.ds(j, 1)])
                own = block(p, spot(p, (u + OFFS[k]) % 4, (v + OFFS[side]) % 4) + j)
                add_into(own, own, inner[p].at[k, pl.ds(j, 1)])
                back(p, 6 * k + 3 + 2 * j, own, inner[p].at[k, pl.ds(3 + 2 * j, 1)], two[way])

    def scatter_middle(p, ks):
        u, v, one, two = axes(p)
        for k in ks:
            at = combine(p, k, 0)
            for j in range(2, 6):
                came(p, 6 * k + j, inner[p].at[k, pl.ds(j, 1)])
            held = [inner[p].at[k, pl.ds(j, 1)] for j in range(6)]
            add_into(block(p, at), block(p, at), held[3], held[4])
            add_into(block(p, at + 1), block(p, at + 1), held[2], held[5])
            if k == 3:
                back(p, 24, block(p, at), outer[p].at[pl.ds(0, 1)], one[1])
                back(p, 25, block(p, at + 1), outer[p].at[pl.ds(1, 1)], one[0])
            if k == 2:
                back(p, 26, block(p, at + 1), outer[p].at[pl.ds(2, 1)], one[1])
            if k == 1:
                back(p, 28, block(p, at), outer[p].at[pl.ds(4, 1)], one[0])

    def scatter_outer(p):
        u, v, one, two = axes(p)
        for j, side, way in ((0, 2, 1), (1, 1, 0)):
            came(p, 24 + j, outer[p].at[pl.ds(j, 1)])
            own = block(p, spot(p, (u + OFFS[side]) % 4, v) + j)
            add_into(own, own, outer[p].at[pl.ds(j, 1)])
            back(p, 27 + 2 * j, own, outer[p].at[pl.ds(3 + 2 * j, 1)], one[way])

    def scatter_x(p):
        u, v, one, two = axes(p)
        for j in range(2, 6):
            came(p, 24 + j, outer[p].at[pl.ds(j, 1)])
        held = [outer[p].at[pl.ds(j, 1)] for j in range(6)]
        at = spot(p, u, v)
        add_into(block(p, at), block(p, at), held[3], held[4])
        add_into(block(p, at + 1), block(p, at + 1), held[2], held[5])
        back(p, 30, block(p, at + 1 - x), last[p], near["x"])

    def scatter_end(p):
        r, low, width, first = PIECES[p]
        u, v, one, two = axes(p)
        came(p, 30, last[p])
        add_into(outs[r].at[:, :, pl.ds(low, width)], block(p, spot(p, u, v) + x), last[p])

    def each(step, group, *rest):
        for p in group:
            step(p, *rest)

    def remote(k, src, dst):
        return far(src, dst, send_sem.at[k], recv_sem.at[k], partner)

    def widen_start(k, wide):
        remote(k, wide.at[:, t], wide.at[:, t]).start()

    def widen_end(k, wide):
        remote(k, wide.at[:, 1 - t], wide.at[:, 1 - t]).wait()
        return wide[...].reshape(256, wide.shape[-1])

    def narrow_start(k, n):
        for s in range(slots):
            narrow_send[n, s] = part[s, 1 - t].astype(jnp.bfloat16)
        remote(k, narrow_send.at[n], narrow_recv.at[n]).start()

    def narrow_end(k, n):
        remote(k, narrow_send.at[n], narrow_recv.at[n]).wait()

    def narrowed(n, s):
        return part[s, t].astype(jnp.bfloat16).astype(jnp.float32) + narrow_recv[n, s].astype(jnp.float32)

    def mod(s, k):
        return mods[s, k : k + 1, :]

    each(gather_begin, ALL)
    for s in range(slots):
        unit, inverse = normed(lat[s].astype(jnp.float32))
        wide1[s, t] = (unit * (1.0 + mod(s, 1)) + mod(s, 0)).astype(jnp.bfloat16)
    widen_start(0, wide1)
    for s in range(slots):
        grad = cot[s].astype(jnp.float32) * mod(s, 6)
        wideg[s, t] = (mod(s, 5) * grad).astype(jnp.bfloat16)
    widen_start(1, wideg)
    grad_bd[1:2] = sum(jnp.sum(wideg[s, t].astype(jnp.float32), axis=0, keepdims=True) for s in range(slots))

    each(gather_x, ALL)
    each(gather_first, ONE)
    each(gather_second, ONE, (0, 1, 2))
    each(gather_first, TWO + THREE)
    each(gather_first_end, ONE)
    each(gather_second, ONE, (3,))
    for k in range(4):
        each(gather_relay, ONE, (k,))
    each(gather_first_end, TWO)
    each(gather_second, TWO, range(4))
    each(gather_end, ONE, range(4))
    each(gather_core, ONE)
    for j in range(8):
        pick = one_hot((128, 1024), lambda a, b: b == (a // 2) * 16 + (a % 2) * 8 + j)
        tail_w[:, 896 * j : 896 * j + 896] = dot(pick, wt[...].reshape(1024, 896)).astype(jnp.bfloat16)

    h1 = widen_end(0, wide1)
    flip1[...] = h1.T

    def project(rows, w, cols, offset):
        return dot(rows[:, :1024], w[:, :, cols].reshape(1024, 256)) + dot(
            rows[:, 1024:], tail_w[:, pl.ds(pl.multiple_of(offset + cols.start, 256), 256)]
        )

    def to_qkv(cols):
        flat = project(wide1[...].reshape(256, 1152), w1, cols, 0) + bias_qkv[:, cols]
        qk[:, cols] = flat.astype(jnp.bfloat16)

    columns_loop(9, to_qkv)
    for k in range(4):
        each(gather_relay, TWO, (k,))
    each(gather_first_end, THREE)
    each(gather_second, THREE, range(4))
    for i, lane in enumerate((0, 576, 1152)):
        low = lane // 128 * 128
        spread_heads = one_hot(
            (640, 1024), lambda a, b: (a - (lane - low) == (b // 128) * 72 + b % 128) & (b % 128 < 72)
        )
        qkvp[i] = dot(qk[:, low : low + 640], spread_heads).astype(jnp.bfloat16)

    factor = 72 ** (-0.5)

    def attend(i, carry):
        rows = pl.ds(pl.multiple_of(i * 128, 128), 128)
        for h in range(8):
            lanes = slice(128 * h, 128 * h + 128)
            q, k, v = qkvp[0, rows, lanes], qkvp[1, rows, lanes], qkvp[2, rows, lanes]
            scores = dot(q, k, 1, 1) * factor
            raised = jnp.exp(scores - jnp.max(scores, axis=-1, keepdims=True))
            prob = raised / jnp.sum(raised, axis=-1, keepdims=True)
            probs[i, h] = prob
            gattp[rows, lanes] = dot(prob.astype(jnp.bfloat16), v).astype(jnp.bfloat16)
        return carry

    lax.fori_loop(0, slots, attend, 0)
    each(gather_end, TWO, range(4))
    for k in range(4):
        each(gather_relay, THREE, (k,))
    join = one_hot((1024, 640), lambda a, b: (b - 64 == (a // 128) * 72 + a % 128) & (a % 128 < 72))
    att[...] = dot(gattp[...], join).astype(jnp.bfloat16)

    def back_to_width(rows, w, cols, tail_cols, add):
        total = dot(rows, w[:, :, cols].reshape(1024, -1), 1, 1)
        tail = dot(rows, tail_w[:, tail_cols], 1, 1)
        main = part.at[:, :, :, 0:1024]
        rest = part.at[:, :, :, 1024:1152]
        total, tail = total.reshape(slots, 2, 64, 1024), tail.reshape(slots, 2, 64, 128)
        main[...] = main[...] + total if add else total
        rest[...] = rest[...] + tail if add else tail

    back_to_width(att[...], w1, slice(1664, 2304), slice(1664, 2304), False)
    narrow_start(2, 0)
    narrow_end(2, 0)
    for s in range(slots):
        piece = narrowed(0, s) + bias_d[0:1]
        branch[s] = piece
        rows = lat[s].astype(jnp.float32) + mod(s, 2) * piece
        middle[s] = rows
        unit, inverse = normed(rows)
        wide2[s, t] = (unit * (1.0 + mod(s, 4)) + mod(s, 3)).astype(jnp.bfloat16)
    widen_start(3, wide2)
    gd = widen_end(1, wideg)
    flipg[...] = gd.T
    each(gather_core, TWO)
    each(gather_end, THREE, range(4))
    h2 = widen_end(3, wide2)
    flip2[...] = h2.T

    def feed(cols):
        up = project(wide2[...].reshape(256, 1152), w2, cols, 2304) + bias_up[:, cols]
        upper[:, cols] = up
        acted[:, cols] = gelu_value(up).astype(jnp.bfloat16)

    columns_loop(9, feed)
    each(gather_core, THREE)
    back_to_width(acted[...], w3, slice(0, 2304), slice(4608, 6912), False)
    narrow_start(4, 1)
    for s in range(slots):
        down_keep[s] = part[s, t]

    def feed_back(cols):
        grad = project(wideg[...].reshape(256, 1152), w3, cols, 4608)
        low = (grad * gelu_slope(upper[:, cols])).astype(jnp.bfloat16)
        gup[:, cols] = low
        grad_bup[:, cols] = jnp.sum(low.astype(jnp.float32), axis=0, keepdims=True)

    columns_loop(9, feed_back)

    back_to_width(gup[...], w2, slice(0, 2304), slice(2304, 4608), False)
    narrow_start(5, 2)

    def weight_grad(flip, rows, cols, g, offset):
        made = dot(flip[...], rows[:, cols]).astype(jnp.bfloat16)
        g[:, :, cols] = made[:1024].reshape(64, 16, 256)
        tail_g[:, pl.ds(pl.multiple_of(offset + cols.start, 256), 256)] = made[1024:]

    each(sent, THREE)
    columns_loop(9, lambda cols: weight_grad(flipg, acted, cols, w3, 4608))
    each(scatter_twin, THREE)

    narrow_end(4, 1)
    for s in range(slots):
        grad = cot[s].astype(jnp.float32) * mod(s, 6)
        down = down_keep[s].astype(jnp.bfloat16).astype(jnp.float32) + narrow_recv[1, s].astype(jnp.float32)
        down = down + bias_d[1:2]
        out[s] = ((middle[s] + mod(s, 5) * down) * mod(s, 6)).astype(jnp.bfloat16)
        grad_mod[s, 5:6] = jnp.sum(grad * down, axis=0, keepdims=True)
    narrow_end(5, 2)
    for s in range(slots):
        grad = cot[s].astype(jnp.float32) * mod(s, 6)
        gh = narrowed(2, s)
        unit, inverse = normed(middle[s])
        grad_mod[s, 3:4] = jnp.sum(gh, axis=0, keepdims=True)
        grad_mod[s, 4:5] = jnp.sum(gh * unit, axis=0, keepdims=True)
        gm = grad + norm_back(gh * (1.0 + mod(s, 4)), unit, inverse)
        grad_mod[s, 2:3] = jnp.sum(gm * branch[s], axis=0, keepdims=True)
        middle[s] = gm
        wideb[s, t] = (mod(s, 2) * gm).astype(jnp.bfloat16)
    widen_start(6, wideb)
    each(scatter_relay, THREE, BACK)
    each(sent, TWO)
    columns_loop(9, lambda cols: weight_grad(flip2, gup, cols, w2, 2304))
    each(scatter_twin, TWO)
    each(scatter_direct, THREE, BACK)
    grad_bd[0:1] = sum(jnp.sum(wideb[s, t].astype(jnp.float32), axis=0, keepdims=True) for s in range(slots))
    gb = widen_end(6, wideb)
    flipb[...] = gb.T
    gatt = dot(gb[:, :1024], w1[:, :, 1664:2304].reshape(1024, 640)) + dot(gb[:, 1024:], tail_w[:, 1664:2304])
    each(scatter_on, THREE, BACK)
    each(scatter_relay, TWO, BACK)
    gattp[...] = dot(gatt.astype(jnp.bfloat16), join, 1, 1).astype(jnp.bfloat16)

    def attend_back(i, carry):
        rows = pl.ds(pl.multiple_of(i * 128, 128), 128)
        for h in range(8):
            lanes = slice(128 * h, 128 * h + 128)
            q, k, v = qkvp[0, rows, lanes], qkvp[1, rows, lanes], qkvp[2, rows, lanes]
            ga = gattp[rows, lanes]
            prob = probs[i, h]
            grad = dot(ga, v, 1, 1)
            inner = jnp.sum(prob * grad, axis=-1, keepdims=True)
            gs = (prob * (grad - inner)).astype(jnp.bfloat16)
            qkvp[0, rows, lanes] = (dot(gs, k) * factor).astype(jnp.bfloat16)
            qkvp[1, rows, lanes] = (dot(gs, q, 0, 0) * factor).astype(jnp.bfloat16)
            qkvp[2, rows, lanes] = dot(prob.astype(jnp.bfloat16), ga, 0, 0).astype(jnp.bfloat16)
        return carry

    attend_back(0, 0)
    each(scatter_direct, TWO, BACK)
    each(scatter_middle, THREE, BACK)
    attend_back(1, 0)
    each(scatter_on, TWO, BACK)
    gqkv[...] = jnp.zeros_like(gqkv)
    for i, lane in enumerate((0, 576, 1152)):
        low = lane // 128 * 128
        gather_heads = one_hot(
            (1024, 640), lambda a, b: (b - (lane - low) == (a // 128) * 72 + a % 128) & (a % 128 < 72)
        )
        piece = dot(qkvp[i], gather_heads).astype(jnp.bfloat16)
        gqkv[:, low : low + 640] = gqkv[:, low : low + 640] + piece
    grad_bqkv[...] = jnp.sum(gqkv[...].astype(jnp.float32), axis=0, keepdims=True)
    back_to_width(gqkv[...], w1, slice(0, 1792), slice(0, 1792), False)
    narrow_start(7, 3)

    each(scatter_middle, TWO, BACK)
    each(scatter_outer, THREE)
    each(sent, ONE)
    columns_loop(6, lambda cols: weight_grad(flip1, gqkv, cols, w1, 0))
    for low, high in ((1536, 1664), (1664, 1792), (1792, 2304)):
        made = 0.0
        if low < 1792:
            made = made + dot(flip1[...], gqkv[:, low:high])
        if high > 1664:
            made = made + dot(flipb[...], att[:, low - 1664 : high - 1664])
        made = made.astype(jnp.bfloat16)
        w1[:, :, low:high] = made[:1024].reshape(64, 16, high - low)
        tail_g[:, low:high] = made[1024:]
    tail_g[:, 6912:] = jnp.zeros((128, 256), jnp.bfloat16)
    total = jnp.zeros((1024, 896), jnp.float32)
    for j in range(8):
        pick = one_hot((1024, 128), lambda a, b: a == (b // 2) * 16 + (b % 2) * 8 + j)
        total = total + dot(pick, tail_g[:, 896 * j : 896 * j + 896])
    wt[...] = total.astype(jnp.bfloat16).reshape(64, 16, 896)
    each(scatter_twin, ONE)
    each(scatter_x, THREE)
    each(scatter_outer, TWO)
    each(scatter_relay, ONE, BACK)

    narrow_end(7, 3)
    for s in range(slots):
        gh = narrowed(3, s)
        unit, inverse = normed(lat[s].astype(jnp.float32))
        grad_mod[s, 0:1] = jnp.sum(gh, axis=0, keepdims=True)
        grad_mod[s, 1:2] = jnp.sum(gh * unit, axis=0, keepdims=True)
        grad_lat[s] = middle[s] + norm_back(gh * (1.0 + mod(s, 1)), unit, inverse)
        grad_mod[s, 6:8] = jnp.zeros((2, 1152), jnp.float32)
    each(scatter_x, TWO)
    each(scatter_direct, ONE, BACK)
    each(scatter_end, THREE)
    each(scatter_on, ONE, BACK)
    each(scatter_end, TWO)
    each(scatter_middle, ONE, BACK)
    each(scatter_outer, ONE)
    each(scatter_x, ONE)
    each(scatter_end, ONE)
    each(sent, ALL)


def whole_block(args, weights, collective_id):
    f32, bf = jnp.float32, jnp.bfloat16
    m = len(WIDTHS)
    vmem = pl.BlockSpec(memory_space=pltpu.VMEM)
    shape = jax.ShapeDtypeStruct
    n = len(PIECES)

    def room(*lead):
        return [pltpu.VMEM(lead + (16, piece[2]), bf) for piece in PIECES]

    dma = pltpu.SemaphoreType.DMA
    return pl.pallas_call(
        block_kernel,
        out_shape=[
            shape((2, 64, 1152), bf), shape((2, 64, 1152), f32),
            *[shape((1, 16, width), f32) for width in WIDTHS],
            shape((2, 8, 1152), f32), shape((2, 1152), f32), shape((1, 1792), f32), shape((1, 2304), f32),
        ],
        in_specs=[vmem] * (len(args) + m),
        out_specs=[vmem] * (6 + m),
        scratch_shapes=[
            *[pltpu.VMEM((64, 16, width), bf) for width in WIDTHS],
            *[pltpu.VMEM((32, 16, width), bf) for width in WIDTHS],
            *room(4, 6), *room(6), *room(1),
            pltpu.VMEM((128, 7168), bf), pltpu.VMEM((128, 7168), bf),
            *[pltpu.VMEM((2, 2, 64, 1152), bf)] * 4,
            *[pltpu.VMEM((1152, 256), bf)] * 4,
            pltpu.VMEM((4, 2, 64, 1152), bf), pltpu.VMEM((4, 2, 64, 1152), bf),
            pltpu.VMEM((2, 2, 64, 1152), f32),
            pltpu.VMEM((3, 256, 1024), bf), pltpu.VMEM((2, 8, 128, 128), f32), pltpu.VMEM((256, 1024), bf),
            pltpu.VMEM((256, 2304), bf), pltpu.VMEM((256, 1792), bf), pltpu.VMEM((256, 640), bf),
            pltpu.VMEM((256, 2304), f32), pltpu.VMEM((256, 2304), bf), pltpu.VMEM((256, 2304), bf),
            *[pltpu.VMEM((2, 64, 1152), f32)] * 3,
            dma((8,)), dma((8,)),
            dma((n,)), dma((n, 31)), dma((n, 16)), dma((n, 21)), dma((n, 16)), dma((n, 31)), dma((n, 16)),
        ],
        compiler_params=pltpu.CompilerParams(
            collective_id=collective_id, has_side_effects=True, vmem_limit_bytes=63 * 1024 * 1024
        ),
    )(*args, *weights)


MAIN = 1024
CHUNK = 896


def shuffle_matrix(width):
    place = jnp.arange(width, dtype=jnp.int32)
    tail = place - MAIN
    block = jnp.where(place < MAIN, place // 16, tail // 2)
    row = jnp.where(place < MAIN, place % 16, 16 + tail % 2)
    fsdp = ((block // 8) % 4) * 16 + ((block // 2) % 4) * 4 + (block % 2) * 2 + block // 32
    source = fsdp * 18 + row
    return (jnp.arange(width, dtype=jnp.int32)[:, None] == source[None, :]).astype(jnp.bfloat16)


def shuffled(rows, matrix):
    return jnp.einsum("...d,de->...e", rows, matrix, preferred_element_type=jnp.float32).astype(jnp.bfloat16)


def shuffled_wide(rows, matrix):
    return jnp.einsum("...d,de->...e", rows, matrix.astype(jnp.float32), precision=highest)


def straight(rows, matrix):
    return jnp.einsum("...e,de->...d", rows, matrix, preferred_element_type=jnp.float32).astype(jnp.bfloat16)


def straight_wide(rows, matrix):
    return jnp.einsum("...e,de->...d", rows, matrix.astype(jnp.float32), precision=highest)


def pack_rows(all_rows):
    third = all_rows.shape[1] // 3
    main, tail = all_rows[:16], all_rows[16:]
    tail = jnp.pad(tail, ((0, 0), (0, 8 * CHUNK - tail.shape[1]))).reshape(1, 16, CHUNK)
    return [*(main[None, :, i * third : (i + 1) * third] for i in range(3)), tail]


def unpack_rows(one, two, three, tail):
    width = one.shape[1] * 3
    main = jnp.concatenate([one, two, three], axis=1)
    return jnp.concatenate([main, tail.reshape(2, 8 * CHUNK)[:, :width]], axis=0)


def local(
    latents,
    condition,
    counts,
    order,
    w_ada,
    b_ada,
    w_qkv,
    b_qv,
    w_proj,
    b_proj,
    w_up,
    b_up,
    w_down,
    b_down,
    cotangent,
):
    slots = latents.shape[0]
    latent_count = condition.shape[0]
    group = lax.axis_index("fsdp")
    ranks = jnp.arange(counts.shape[0], dtype=jnp.int32)
    held = jnp.sum(jnp.where(ranks == group, counts, 0))
    before = jnp.sum(jnp.where(ranks < group, counts, 0))
    slot_rank = jnp.arange(slots, dtype=jnp.int32)
    live = (slot_rank < held).astype(jnp.float32)
    place = jnp.clip(before + slot_rank, 0, latent_count - 1)
    numbers = jnp.arange(latent_count, dtype=jnp.int32)
    owner = jnp.sum(jnp.where(numbers[None, :] == place[:, None], order[None, :], 0), axis=1)
    offsets = jnp.cumsum(counts) - counts
    every = jnp.clip(offsets[:, None] + slot_rank[None, :], 0, latent_count - 1).reshape(-1)
    owners = jnp.sum(jnp.where(numbers[None, :] == every[:, None], order[None, :], 0), axis=1)
    choose_all = (numbers[None, :] == owners[:, None]).astype(jnp.bfloat16)
    groups = counts.shape[0]
    devices = groups * 2
    matrix = shuffle_matrix(latents.shape[2])
    soft_cond = jax.nn.silu(condition.astype(jnp.float32))
    ada_local = w_ada.astype(jnp.float32)
    mod_part = jnp.einsum("nd,dke->nke", soft_cond, ada_local, precision=highest) + b_ada
    mod_low = mod_part.astype(jnp.bfloat16).reshape(latent_count, -1)
    mod_send = jnp.dot(choose_all, mod_low, preferred_element_type=jnp.float32).astype(jnp.bfloat16)
    columns = mod_part.shape[2]
    mod_send = jnp.pad(mod_send.reshape(groups, slots, -1), ((0, 0), (0, 16 - slots), (0, 128 - 6 * columns)))
    mod_got = exchange(mod_send, True, devices, 1)[:, :slots, : 6 * columns]
    slot_mod = jnp.transpose(mod_got.reshape(devices, slots, 6, columns), (1, 2, 0, 3)).reshape(slots, 6, -1)
    slot_mod = shuffled(slot_mod, matrix).astype(jnp.float32)
    rows = shuffled(latents, matrix)
    cotangent = shuffled(cotangent, matrix)
    bias_d = shuffled_wide(jnp.stack([b_proj, b_down]), matrix)
    own_rows = jnp.concatenate([w_qkv[0], w_qkv[1], w_qkv[2], w_proj.T, w_up, w_down.T], axis=1)
    width = own_rows.shape[1]
    head_part = w_qkv.shape[2]
    weights = pack_rows(own_rows)
    mods = jnp.concatenate(
        [slot_mod, jnp.broadcast_to(live[:, None, None], (slots, 2, slot_mod.shape[2]))], axis=1
    )
    nothing = jnp.zeros_like(b_qv[0])
    bias_qkv = jnp.concatenate([b_qv[0], nothing, b_qv[1], nothing])[None]
    block_output, grad_latents, *grads, grad_mod, grad_bd, grad_bqkv, grad_bup = whole_block(
        (rows, cotangent, mods, bias_d, bias_qkv, b_up[None]), weights, 2
    )
    block_output = straight(block_output, matrix)
    grad_latents = straight_wide(grad_latents, matrix)
    grad_b_qv_local = jnp.stack([grad_bqkv[0, :head_part], grad_bqkv[0, 2 * head_part : 3 * head_part]])
    grad_b_up_local = grad_bup[0]
    grad_b_proj, grad_b_down = grad_bd[0], grad_bd[1]
    summed = unpack_rows(*(each[0] for each in grads))
    grad_w_qkv = jnp.stack([summed[:, i * head_part : (i + 1) * head_part] for i in range(3)])
    grad_w_proj = summed[:, 3 * head_part : 4 * head_part].T
    up_part = w_up.shape[1]
    grad_w_up = summed[:, 4 * head_part : 4 * head_part + up_part]
    grad_w_down = summed[:, 4 * head_part + up_part :].T
    grad_mod = grad_mod[:, :6]
    grad_mod = straight_wide(grad_mod, matrix).reshape(slots, 6, devices, columns)
    grad_send = jnp.transpose(grad_mod, (2, 0, 1, 3)).reshape(devices, slots, 6 * columns)
    grad_send = jnp.pad(grad_send, ((0, 0), (0, 8 - slots), (0, 128 - 6 * columns)))
    grad_got = exchange(grad_send, False, devices, 4)[:, :slots, : 6 * columns]
    grad_got = jnp.sum(grad_got.reshape(groups, 2, slots, 6 * columns), axis=1).reshape(groups * slots, -1)
    alive_all = (slot_rank[None, :] < counts[:, None]).reshape(-1, 1)
    grad_mod_part = jnp.einsum(
        "sn,se->ne",
        choose_all.astype(jnp.float32),
        jnp.where(alive_all, grad_got, 0.0),
        precision=highest,
    ).reshape(latent_count, 6, columns)
    grad_b_ada = jnp.sum(grad_mod_part, axis=0)
    grad_w_ada = jnp.einsum("nd,nke->dke", soft_cond, grad_mod_part, precision=highest)
    grad_soft_part = jnp.einsum("nke,dke->nd", grad_mod_part, ada_local, precision=highest)
    tensor_rank = lax.axis_index("tp")
    zero_index = jnp.zeros((), jnp.int32)
    up_half = grad_b_up_local.shape[0]
    qv_place = lax.dynamic_update_slice(
        jnp.zeros((2, head_part * lax.axis_size("tp")), jnp.float32),
        grad_b_qv_local,
        (zero_index, tensor_rank * head_part),
    )
    up_place = lax.dynamic_update_slice(
        jnp.zeros((up_half * lax.axis_size("tp"),), jnp.float32),
        grad_b_up_local,
        (tensor_rank * up_half,),
    )
    sums = [grad_soft_part, grad_b_proj, grad_b_down, qv_place, up_place]
    flat = jnp.concatenate([each.reshape(-1) for each in sums])
    flat = jnp.pad(flat, (0, devices * 1024 - flat.shape[0])).reshape(devices, 8, 128)
    flat = total_everywhere(flat, 5).reshape(-1)
    parts, start = [], 0
    for each in sums:
        parts.append(flat[start : start + each.size].reshape(each.shape))
        start += each.size
    grad_soft, grad_b_proj, grad_b_down, qv_full, up_full = parts
    grad_b_proj, grad_b_down = straight_wide(jnp.stack([grad_b_proj, grad_b_down]), matrix)
    grad_b_qv = lax.dynamic_slice_in_dim(qv_full, tensor_rank * head_part, head_part, 1)
    grad_b_up = lax.dynamic_slice_in_dim(up_full, tensor_rank * up_half, up_half, 0)
    grad_condition = jax.vjp(jax.nn.silu, condition.astype(jnp.float32))[1](grad_soft)[0]
    return (
        block_output,
        grad_latents,
        grad_condition,
        grad_w_ada,
        grad_b_ada,
        grad_w_qkv,
        grad_b_qv,
        grad_w_proj,
        grad_b_proj,
        grad_w_up,
        grad_b_up,
        grad_w_down,
        grad_b_down,
    )


def solution(mesh):
    in_specs = (
        P("fsdp", "tp", None),
        P(),
        P(),
        P(),
        P(None, None, ("fsdp", "tp")),
        P(None, ("fsdp", "tp")),
        P(None, "fsdp", "tp"),
        P(None, "tp"),
        P("tp", "fsdp"),
        P(),
        P("fsdp", "tp"),
        P("tp"),
        P("tp", "fsdp"),
        P(),
        P("fsdp", "tp", None),
    )
    out_specs = (
        P("fsdp", "tp", None),
        P("fsdp", "tp", None),
        P(),
        P(None, None, ("fsdp", "tp")),
        P(None, ("fsdp", "tp")),
        P(None, "fsdp", "tp"),
        P(None, "tp"),
        P("tp", "fsdp"),
        P(),
        P("fsdp", "tp"),
        P("tp"),
        P("tp", "fsdp"),
        P(),
    )
    return jax.shard_map(local, mesh=mesh, in_specs=in_specs, out_specs=out_specs, check_vma=False)
```

```python
import jax
import jax.numpy as jnp
import numpy as np
from jax import lax
from jax.experimental import pallas as pl
from jax.experimental.pallas import tpu as pltpu
from jax.sharding import PartitionSpec as P

MESH = pl.DeviceIdType.MESH
OFFS = (0, 3, 1, 2)
WIDTHS = (2304, 2304, 2304, 896)
PIECES = (
    (3, 0, 896, "z"),
    (0, 0, 1152, "z"),
    (0, 1152, 1152, "y"),
    (1, 0, 1152, "z"),
    (1, 1152, 1152, "y"),
    (2, 0, 1152, "z"),
    (2, 1152, 1152, "y"),
)
ONE, TWO, THREE = (0, 1, 2), (3, 4), (5, 6)
ALL = ONE + TWO + THREE
BACK = (3, 2, 1, 0)


highest = lax.Precision.HIGHEST
norm_eps = 1e-06


def place_of():
    f = lax.axis_index("fsdp")
    return f // 16, (f // 4) % 4, (f // 2) % 2, f % 2, lax.axis_index("tp")


def peers(z, y, x, c, t):
    def at(z, y, x, c):
        return (z * 16 + y * 4 + x * 2 + c, t)

    return {
        "z": (at((z + 3) % 4, y, x, c), at((z + 1) % 4, y, x, c)),
        "y": (at(z, (y + 3) % 4, x, c), at(z, (y + 1) % 4, x, c)),
        "x": at(z, y, 1 - x, c),
        "c": at(z, y, x, 1 - c),
        "t": (z * 16 + y * 4 + x * 2 + c, 1 - t),
    }


def ring_peer(i):
    f, t = lax.axis_index("fsdp"), lax.axis_index("tp")
    other = (f % 4 * 2 + t + i) % RING
    return other, (f // 4 * 4 + other // 2, other % 2)


def plane_peer(i):
    f, t = lax.axis_index("fsdp"), lax.axis_index("tp")
    other = (f // 4 + i) % PLANE
    return other, (other * 4 + f % 4, t)


def greet():
    barrier = pltpu.get_barrier_semaphore()

    def hello(peer):
        def go(i, carry):
            pl.semaphore_signal(barrier, inc=1, device_id=peer(i)[1], device_id_type=MESH)
            return carry

        return go

    lax.fori_loop(1, PLANE, hello(plane_peer), 0)
    lax.fori_loop(1, RING, hello(ring_peer), 0)
    pl.semaphore_wait(barrier, PLANE + RING - 2)


def add_into(dst, *srcs):
    for i in range(dst.shape[0]):
        total = srcs[0][i].astype(jnp.float32)
        for src in srcs[1:]:
            total = total + src[i].astype(jnp.float32)
        dst[i] = total.astype(dst.dtype)


PLANE, RING = 16, 8


def one_hot(shape, rule):
    first = lax.broadcasted_iota(jnp.int32, shape, 0)
    second = lax.broadcasted_iota(jnp.int32, shape, 1)
    return jnp.where(rule(first, second), 1.0, 0.0).astype(jnp.bfloat16)


def dot(a, b, ca=1, cb=0):
    return lax.dot_general(a, b, (((ca,), (cb,)), ((), ())), preferred_element_type=jnp.float32)


def normed(rows):
    centred = rows - jnp.mean(rows, axis=-1, keepdims=True)
    inverse = lax.rsqrt(jnp.mean(centred * centred, axis=-1, keepdims=True) + norm_eps)
    return centred * inverse, inverse


def norm_back(grad, unit, inverse):
    first = jnp.mean(grad, axis=-1, keepdims=True)
    second = jnp.mean(grad * unit, axis=-1, keepdims=True)
    return inverse * (grad - first - unit * second)


def gelu_slope(u):
    a, b = 0.7978845608028654, 0.044715
    wave = jnp.tanh(a * (u + b * (u * u * u)))
    return 0.5 * (1.0 + wave) + 0.5 * u * (1.0 - wave * wave) * (a * (1.0 + 3.0 * b * (u * u)))


def gelu_value(u):
    a, b = 0.7978845608028654, 0.044715
    return 0.5 * u * (1.0 + jnp.tanh(a * (u + b * (u * u * u))))


def columns_loop(count, body, first=0):
    def step(i, carry):
        body(pl.ds(pl.multiple_of(i * 256, 256), 256))
        return carry

    lax.fori_loop(first, count, step, 0)


def block_kernel(*refs):
    n, m = len(PIECES), len(WIDTHS)
    (lat_in, cot_in, live, bias_in, bias_qkv, bias_up, mod_send, choose, ada, rows_at, lanes_at, kinds), ins = (
        refs[:12],
        refs[12 : 12 + m],
    )
    refs = refs[12 + m :]
    (out, grad_lat), outs, (table_grad, tiles) = refs[:2], refs[2 : 2 + m], refs[2 + m : 4 + m]
    refs = refs[4 + m :]
    ws, twins = refs[:m], refs[m : 2 * m]
    refs = refs[2 * m :]
    inner, outer, last = (refs[i * n : (i + 1) * n] for i in range(3))
    (
        tail_w, tail_g, wide1, wideg, wide2, wideb, flip_one, flip_two,
        narrow_send, narrow_recv, part, qkvp, probs, gattp, gqkv, att,
        upper, acted, gup, middle, branch, down_keep, send_sem, recv_sem,
        local_sem, way_send, core_send, way_recv, core_recv, back_recv, back_core,
        mods, grad_mod, grad_bd, grad_bqkv, grad_bup,
        mod_plane, mod_turn, mod_ring, turn_send, turn_ring, turn_plane_send, turn_plane,
        tile_send, tile_plane, tile_part, tile_ring, small_send, small_recv, lat, cot, bias_d,
    ) = refs[3 * n :]
    w1, w2, w3, wt = ws
    flip1 = flipg = flip_one
    flip2 = flipb = flip_two
    qk = gup
    slots = lat.shape[0]
    z, y, x, c, t = place_of()
    near = peers(z, y, x, c, t)
    partner = near["t"]
    greet()
    pending = {p: [] for p in range(n)}

    def far(src, dst, ssem, rsem, peer):
        return pltpu.make_async_remote_copy(
            src_ref=src, dst_ref=dst, send_sem=ssem, recv_sem=rsem, device_id=peer, device_id_type=MESH
        )

    def axes(p):
        if PIECES[p][3] == "z":
            return z, y, near["z"], near["y"]
        return y, z, near["y"], near["z"]

    def spot(p, u, v, core=c):
        return core * 32 + (u * 8 + v * 2 if PIECES[p][3] == "z" else v * 8 + u * 2)

    def block(p, at, count=1, of=ws):
        r, low, width, first = PIECES[p]
        return of[r].at[pl.ds(at, count), :, pl.ds(low, width)]

    def push(p, k, ref, peer, src=None):
        cp = far(ref if src is None else src, ref, way_send.at[p, k], way_recv.at[p, k], peer)
        cp.start()
        pending[p].append(cp)

    def arrive(p, k, ref):
        far(ref, ref, way_send.at[p, k], way_recv.at[p, k], near["x"]).wait_recv()

    def share(p, k, ref):
        cp = far(ref, ref, core_send.at[p, k], core_recv.at[p, k], near["c"])
        cp.start()
        pending[p].append(cp)

    def gather_begin(p):
        r, low, width, first = PIECES[p]
        mine = ins[r].at[:, :, pl.ds(low, width)]
        own = block(p, c * 32 + z * 8 + y * 2 + x)
        push(p, 0, own, near["x"], mine)
        pltpu.make_async_copy(mine, own, local_sem.at[p]).start()

    def gather_x(p):
        u, v, one, two = axes(p)
        r, low, width, first = PIECES[p]
        own = block(p, c * 32 + z * 8 + y * 2 + x)
        pltpu.make_async_copy(ins[r].at[:, :, pl.ds(low, width)], own, local_sem.at[p]).wait()
        arrive(p, 0, block(p, c * 32 + z * 8 + y * 2 + 1 - x))
        pair = block(p, spot(p, u, v), 2)
        push(p, 1, pair, one[1])
        push(p, 2, pair, one[0])
        share(p, 0, pair)

    def gather_first(p):
        u, v, one, two = axes(p)
        for k, way in ((1, 1), (2, 0)):
            uu = (u + OFFS[k]) % 4
            pair = block(p, spot(p, uu, v), 2)
            arrive(p, k, pair)
            push(p, 2 + k, block(p, spot(p, uu, v) + 1 - way), one[way])
            share(p, 4 * k, pair)

    def gather_first_end(p):
        u, v, one, two = axes(p)
        uu = (u + 2) % 4
        arrive(p, 3, block(p, spot(p, uu, v)))
        arrive(p, 4, block(p, spot(p, uu, v) + 1))
        share(p, 12, block(p, spot(p, uu, v), 2))

    def gather_second(p, ks):
        u, v, one, two = axes(p)
        for k in ks:
            pair = block(p, spot(p, (u + OFFS[k]) % 4, v), 2)
            push(p, 5 + 4 * k, pair, two[1])
            push(p, 6 + 4 * k, pair, two[0])

    def gather_relay(p, ks):
        u, v, one, two = axes(p)
        for k in ks:
            uu = (u + OFFS[k]) % 4
            for side, way in ((1, 1), (2, 0)):
                vv = (v + OFFS[side]) % 4
                pair = block(p, spot(p, uu, vv), 2)
                arrive(p, 4 + 4 * k + side, pair)
                push(p, 6 + 4 * k + side, block(p, spot(p, uu, vv) + 1 - way), two[way])
                share(p, 4 * k + side, pair)

    def gather_end(p, ks):
        u, v, one, two = axes(p)
        for k in ks:
            uu, vv = (u + OFFS[k]) % 4, (v + 2) % 4
            arrive(p, 7 + 4 * k, block(p, spot(p, uu, vv)))
            arrive(p, 8 + 4 * k, block(p, spot(p, uu, vv) + 1))
            share(p, 4 * k + 3, block(p, spot(p, uu, vv), 2))

    def gather_core(p):
        for k in range(16):
            ref = block(p, (1 - c) * 32 + 2 * k, 2)
            far(ref, ref, core_send.at[p, k], core_recv.at[p, k], near["c"]).wait_recv()

    def sent(p):
        for cp in pending[p]:
            cp.wait_send()
        pending[p].clear()

    def back(p, k, src, dst, peer):
        cp = far(src, dst, way_send.at[p, k], back_recv.at[p, k], peer)
        cp.start()
        pending[p].append(cp)

    def came(p, k, ref):
        far(ref, ref, way_send.at[p, k], back_recv.at[p, k], near["x"]).wait_recv()

    def twin_of(p, at):
        return block(p, at, 2, twins)

    def scatter_twin(p):
        u, v, one, two = axes(p)
        for side in BACK:
            for k in BACK:
                at = spot(p, (u + OFFS[k]) % 4, (v + OFFS[side]) % 4, 0)
                j = 4 * k + side
                cp = far(block(p, (1 - c) * 32 + at, 2), twin_of(p, at), core_send.at[p, j], back_core.at[p, j], near["c"])
                cp.start()
                pending[p].append(cp)

    def combine(p, k, side):
        u, v, one, two = axes(p)
        at = spot(p, (u + OFFS[k]) % 4, (v + OFFS[side]) % 4, 0)
        j = 4 * k + side
        twin = twin_of(p, at)
        far(twin, twin, core_send.at[p, j], back_core.at[p, j], near["c"]).wait_recv()
        own = block(p, c * 32 + at, 2)
        add_into(own, own, twin)
        return c * 32 + at

    def scatter_relay(p, ks):
        u, v, one, two = axes(p)
        for k in ks:
            at = combine(p, k, 3)
            back(p, 6 * k, block(p, at), inner[p].at[k, pl.ds(0, 1)], two[1])
            back(p, 6 * k + 1, block(p, at + 1), inner[p].at[k, pl.ds(1, 1)], two[0])

    def scatter_direct(p, ks):
        u, v, one, two = axes(p)
        for k in ks:
            at = combine(p, k, 2)
            back(p, 6 * k + 2, block(p, at + 1), inner[p].at[k, pl.ds(2, 1)], two[1])
            at = combine(p, k, 1)
            back(p, 6 * k + 4, block(p, at), inner[p].at[k, pl.ds(4, 1)], two[0])

    def scatter_on(p, ks):
        u, v, one, two = axes(p)
        for k in ks:
            for j, side, way in ((0, 2, 1), (1, 1, 0)):
                came(p, 6 * k + j, inner[p].at[k, pl.ds(j, 1)])
                own = block(p, spot(p, (u + OFFS[k]) % 4, (v + OFFS[side]) % 4) + j)
                add_into(own, own, inner[p].at[k, pl.ds(j, 1)])
                back(p, 6 * k + 3 + 2 * j, own, inner[p].at[k, pl.ds(3 + 2 * j, 1)], two[way])

    def scatter_middle(p, ks):
        u, v, one, two = axes(p)
        for k in ks:
            at = combine(p, k, 0)
            for j in range(2, 6):
                came(p, 6 * k + j, inner[p].at[k, pl.ds(j, 1)])
            held = [inner[p].at[k, pl.ds(j, 1)] for j in range(6)]
            add_into(block(p, at), block(p, at), held[3], held[4])
            add_into(block(p, at + 1), block(p, at + 1), held[2], held[5])
            if k == 3:
                back(p, 24, block(p, at), outer[p].at[pl.ds(0, 1)], one[1])
                back(p, 25, block(p, at + 1), outer[p].at[pl.ds(1, 1)], one[0])
            if k == 2:
                back(p, 26, block(p, at + 1), outer[p].at[pl.ds(2, 1)], one[1])
            if k == 1:
                back(p, 28, block(p, at), outer[p].at[pl.ds(4, 1)], one[0])

    def scatter_outer(p):
        u, v, one, two = axes(p)
        for j, side, way in ((0, 2, 1), (1, 1, 0)):
            came(p, 24 + j, outer[p].at[pl.ds(j, 1)])
            own = block(p, spot(p, (u + OFFS[side]) % 4, v) + j)
            add_into(own, own, outer[p].at[pl.ds(j, 1)])
            back(p, 27 + 2 * j, own, outer[p].at[pl.ds(3 + 2 * j, 1)], one[way])

    def scatter_x(p):
        u, v, one, two = axes(p)
        for j in range(2, 6):
            came(p, 24 + j, outer[p].at[pl.ds(j, 1)])
        held = [outer[p].at[pl.ds(j, 1)] for j in range(6)]
        at = spot(p, u, v)
        add_into(block(p, at), block(p, at), held[3], held[4])
        add_into(block(p, at + 1), block(p, at + 1), held[2], held[5])
        back(p, 30, block(p, at + 1 - x), last[p], near["x"])

    def scatter_end(p):
        r, low, width, first = PIECES[p]
        u, v, one, two = axes(p)
        came(p, 30, last[p])
        add_into(outs[r].at[:, :, pl.ds(low, width)], block(p, spot(p, u, v) + x), last[p])

    def spread(k, peer, count, source, target):
        def go(i, carry):
            other, where = peer(i)
            far(source(other), target, small_send.at[k], small_recv.at[k], where).start()
            return carry

        lax.fori_loop(1, count, go, 0)

    def settle(k, count, buffer):
        ref = buffer.at[pl.ds(0, count - 1)]
        pltpu.make_async_copy(ref, ref, small_recv.at[k]).wait()

    def settle_sent(k, count, buffer):
        ref = buffer.at[pl.ds(0, count - 1)]
        pltpu.make_async_copy(ref, ref, small_send.at[k]).wait()

    plane_me = lax.axis_index("fsdp") // 4
    ring_me = lax.axis_index("fsdp") % 4 * 2 + t

    def exact(a, b, ca=1, cb=0):
        return lax.dot_general(
            a, b, (((ca,), (cb,)), ((), ())), precision=highest, preferred_element_type=jnp.float32
        )

    def table_plane():
        mod_plane[plane_me] = mod_send[plane_me]
        spread(0, plane_peer, PLANE, lambda other: mod_send.at[other], mod_plane.at[plane_me])

    def table_ring():
        settle(0, PLANE, mod_plane)
        pick = one_hot((64, 256), lambda a, b: b == (a % 16) * 16 + a // 16)
        turned = dot(pick, mod_plane[...].reshape(256, 128)).astype(jnp.bfloat16)
        mod_turn[...] = turned.reshape(4, 16, 128)
        mod_ring[ring_me] = mod_turn[ring_me // 2]
        spread(1, ring_peer, RING, lambda other: mod_turn.at[other // 2], mod_ring.at[ring_me])

    def table_end():
        settle(1, RING, mod_ring)
        wide = dot(mod_ring[...].reshape(128, 128), rows_at[...], 0, 0)
        wide = (wide * lanes_at[...].astype(jnp.float32)).astype(jnp.bfloat16)
        both = dot(kinds[...], wide)
        mods[0] = both[:8]
        mods[1] = both[8:]

    def turn_ring_start():
        both = jnp.concatenate([grad_mod[0], grad_mod[1]], axis=0)
        wide = exact(kinds[...].astype(jnp.float32), both, 0, 0) * lanes_at[...].astype(jnp.float32)
        turn_send[...] = exact(rows_at[...].astype(jnp.float32), wide, 1, 1).reshape(RING, PLANE, 128)
        turn_ring[ring_me] = turn_send[ring_me]
        spread(2, ring_peer, RING, lambda other: turn_send.at[other], turn_ring.at[ring_me])

    def turn_plane_start():
        settle(2, RING, turn_ring)
        whole = jnp.concatenate([turn_ring[2 * r] + turn_ring[2 * r + 1] for r in range(4)], axis=0)
        pick = one_hot((128, 64), lambda a, b: (b == (a % 8) * 16 + a // 8) & (a % 8 < 4))
        turn_plane_send[...] = exact(pick.astype(jnp.float32), whole).reshape(PLANE, 8, 128)
        turn_plane[plane_me] = turn_plane_send[plane_me]
        spread(3, plane_peer, PLANE, lambda other: turn_plane_send.at[other], turn_plane.at[plane_me])

    def tiles_plane():
        settle(3, PLANE, turn_plane)
        found = turn_plane[...].reshape(128, 128)
        lane = lax.broadcasted_iota(jnp.int32, (96, 128), 1)
        table = jnp.where(lane < 54, exact(choose[0], found), exact(choose[1], found))
        table_grad[...] = table
        soft = exact(table, ada[...].astype(jnp.float32))
        for i in range(12):
            for j in range(9):
                tile_send[i * 9 + j] = soft[8 * i : 8 * i + 8, 128 * j : 128 * j + 128]
        tile_send[108:] = jnp.zeros((20, 8, 128), jnp.float32)

        def line(row, value):
            tile_send[108 + row // 8, row % 8 : row % 8 + 1, :] = value

        for j in range(9):
            line(j, grad_bd[0:1, 128 * j : 128 * j + 128])
            line(9 + j, grad_bd[1:2, 128 * j : 128 * j + 128])
        for half in range(2):
            for j in range(14):
                line(18 + 32 * half + j, jnp.where(t == half, grad_bqkv[:, 128 * j : 128 * j + 128], 0.0))
            for j in range(18):
                line(32 + 32 * half + j, jnp.where(t == half, grad_bup[:, 128 * j : 128 * j + 128], 0.0))
        tile_plane[plane_me] = tile_send[pl.ds(plane_me * 8, 8)]
        spread(4, plane_peer, PLANE, lambda other: tile_send.at[pl.ds(other * 8, 8)], tile_plane.at[plane_me])

    def tiles_ring():
        settle(4, PLANE, tile_plane)
        total = tile_plane[0]
        for i in range(1, PLANE):
            total = total + tile_plane[i]
        tile_part[...] = total
        tile_ring[ring_me] = tile_part[ring_me]
        spread(5, ring_peer, RING, lambda other: tile_part.at[other], tile_ring.at[ring_me])

    def tiles_back():
        settle(5, RING, tile_ring)
        total = tile_ring[0]
        for i in range(1, RING):
            total = total + tile_ring[i]
        own = tiles.at[plane_me * 8 + ring_me]
        own[...] = total
        spread(6, ring_peer, RING, lambda other: own, own)

    def tiles_out():
        settle(6, RING, tiles)
        own = tiles.at[pl.ds(plane_me * 8, 8)]
        spread(7, plane_peer, PLANE, lambda other: own, own)

    def tiles_end():
        ref = tiles.at[pl.ds(0, 8 * PLANE - 8)]
        pltpu.make_async_copy(ref, ref, small_recv.at[7]).wait()
        settle_sent(0, PLANE, mod_plane)
        settle_sent(1, RING, mod_ring)
        settle_sent(2, RING, turn_ring)
        settle_sent(3, PLANE, turn_plane)
        settle_sent(4, PLANE, tile_plane)
        settle_sent(5, RING, tile_ring)
        settle_sent(6, RING, tiles)
        pltpu.make_async_copy(ref, ref, small_send.at[7]).wait()

    def each(step, group, *rest):
        for p in group:
            step(p, *rest)

    def remote(k, src, dst):
        return far(src, dst, send_sem.at[k], recv_sem.at[k], partner)

    def widen_start(k, wide):
        remote(k, wide.at[:, t], wide.at[:, t]).start()

    def widen_end(k, wide):
        remote(k, wide.at[:, 1 - t], wide.at[:, 1 - t]).wait()
        return wide[...].reshape(256, wide.shape[-1])

    def narrow_start(k, n):
        for s in range(slots):
            narrow_send[n, s] = part[s, 1 - t].astype(jnp.bfloat16)
        remote(k, narrow_send.at[n], narrow_recv.at[n]).start()

    def narrow_end(k, n):
        remote(k, narrow_send.at[n], narrow_recv.at[n]).wait()

    def narrowed(n, s):
        return part[s, t].astype(jnp.bfloat16).astype(jnp.float32) + narrow_recv[n, s].astype(jnp.float32)

    def mod(s, k):
        return live[s] if k == 6 else mods[s, k : k + 1, :]

    table_plane()
    each(gather_begin, ALL)
    each(gather_x, ALL)
    table_ring()
    each(gather_first, ONE)
    each(gather_second, ONE, (0, 1, 2))
    each(gather_first, TWO + THREE)
    table_end()
    def chosen(i):
        place = lax.broadcasted_iota(jnp.int32, (1, 128), 1)
        if i < 8:
            place = place + 128 * i
            number, row = place // 16, place % 16
        else:
            number, row = place // 2, 16 + place % 2
        group = (number // 8) % 4 * 16 + (number // 2) % 4 * 4 + number % 2 * 2 + number // 32
        source = group * 18 + row
        return jnp.where(lax.broadcasted_iota(jnp.int32, (1152, 128), 0) == source, 1.0, 0.0).astype(jnp.bfloat16)

    def thirds(rows):
        high = rows.astype(jnp.bfloat16)
        rest = rows - high.astype(jnp.float32)
        middle_part = rest.astype(jnp.bfloat16)
        low = (rest - middle_part.astype(jnp.float32)).astype(jnp.bfloat16)
        return high, middle_part, low

    def unshuffled(parts):
        total = None
        for i in range(9):
            pick = chosen(i)
            for part_rows in parts:
                term = dot(part_rows[:, 128 * i : 128 * i + 128], pick, 1, 1)
                total = term if total is None else total + term
        return total

    both_rows = jnp.concatenate([lat_in[0], lat_in[1], cot_in[0], cot_in[1]], axis=0)
    bias_parts = thirds(bias_in[...])
    for i in range(9):
        pick = chosen(i)
        lanes = slice(128 * i, 128 * i + 128)
        moved = dot(both_rows, pick).astype(jnp.bfloat16)
        for s in range(slots):
            lat[s, :, lanes] = moved[64 * s : 64 * s + 64]
            cot[s, :, lanes] = moved[128 + 64 * s : 192 + 64 * s]
        bias_d[:, lanes] = sum(dot(each_part, pick) for each_part in bias_parts)
    for s in range(slots):
        unit, inverse = normed(lat[s].astype(jnp.float32))
        wide1[s, t] = (unit * (1.0 + mod(s, 1)) + mod(s, 0)).astype(jnp.bfloat16)
    widen_start(0, wide1)
    for s in range(slots):
        grad = cot[s].astype(jnp.float32) * mod(s, 6)
        wideg[s, t] = (mod(s, 5) * grad).astype(jnp.bfloat16)
    widen_start(1, wideg)
    grad_bd[1:2] = sum(jnp.sum(wideg[s, t].astype(jnp.float32), axis=0, keepdims=True) for s in range(slots))

    each(gather_first_end, ONE)
    each(gather_second, ONE, (3,))
    for k in range(4):
        each(gather_relay, ONE, (k,))
    each(gather_first_end, TWO)
    each(gather_second, TWO, range(4))
    each(gather_first_end, THREE)
    each(gather_second, THREE, range(4))
    each(gather_end, ONE, range(4))
    each(gather_core, ONE)
    for j in range(8):
        pick = one_hot((128, 1024), lambda a, b: b == (a // 2) * 16 + (a % 2) * 8 + j)
        tail_w[:, 896 * j : 896 * j + 896] = dot(pick, wt[...].reshape(1024, 896)).astype(jnp.bfloat16)

    widen_end(0, wide1)

    def project(rows, w, cols, offset):
        return dot(rows[:, :1024], w[:, :, cols].reshape(1024, 256)) + dot(
            rows[:, 1024:], tail_w[:, pl.ds(pl.multiple_of(offset + cols.start, 256), 256)]
        )

    def to_qkv(cols):
        flat = project(wide1[...].reshape(256, 1152), w1, cols, 0) + bias_qkv[:, cols]
        qk[:, cols] = flat.astype(jnp.bfloat16)

    columns_loop(9, to_qkv)
    for k in range(4):
        each(gather_relay, TWO, (k,))
    for i, lane in enumerate((0, 576, 1152)):
        low = lane // 128 * 128
        spread_heads = one_hot(
            (640, 1024), lambda a, b: (a - (lane - low) == (b // 128) * 72 + b % 128) & (b % 128 < 72)
        )
        qkvp[i] = dot(qk[:, low : low + 640], spread_heads).astype(jnp.bfloat16)

    factor = 72 ** (-0.5)

    def attend(i, carry):
        rows = pl.ds(pl.multiple_of(i * 128, 128), 128)
        for h in range(8):
            lanes = slice(128 * h, 128 * h + 128)
            q, k, v = qkvp[0, rows, lanes], qkvp[1, rows, lanes], qkvp[2, rows, lanes]
            scores = dot(q, k, 1, 1) * factor
            raised = jnp.exp(scores - jnp.max(scores, axis=-1, keepdims=True))
            prob = raised / jnp.sum(raised, axis=-1, keepdims=True)
            probs[i, h] = prob
            gattp[rows, lanes] = dot(prob.astype(jnp.bfloat16), v).astype(jnp.bfloat16)
        return carry

    attend(0, 0)
    each(gather_end, TWO, (0, 1))
    attend(1, 0)
    each(gather_end, TWO, (2, 3))
    join = one_hot((1024, 640), lambda a, b: (b - 64 == (a // 128) * 72 + a % 128) & (a % 128 < 72))
    att[...] = dot(gattp[...], join).astype(jnp.bfloat16)

    def back_to_width(rows, w, cols, tail_cols, add):
        total = dot(rows, w[:, :, cols].reshape(1024, -1), 1, 1)
        tail = dot(rows, tail_w[:, tail_cols], 1, 1)
        main = part.at[:, :, :, 0:1024]
        rest = part.at[:, :, :, 1024:1152]
        total, tail = total.reshape(slots, 2, 64, 1024), tail.reshape(slots, 2, 64, 128)
        main[...] = main[...] + total if add else total
        rest[...] = rest[...] + tail if add else tail

    back_to_width(att[...], w1, slice(1664, 2304), slice(1664, 2304), False)
    narrow_start(2, 0)
    for k in range(2):
        each(gather_relay, THREE, (k,))
    narrow_end(2, 0)
    for s in range(slots):
        piece = narrowed(0, s) + bias_d[0:1]
        branch[s] = piece
        rows = lat[s].astype(jnp.float32) + mod(s, 2) * piece
        middle[s] = rows
        unit, inverse = normed(rows)
        wide2[s, t] = (unit * (1.0 + mod(s, 4)) + mod(s, 3)).astype(jnp.bfloat16)
    widen_start(3, wide2)
    for k in range(2, 4):
        each(gather_relay, THREE, (k,))
    gd = widen_end(1, wideg)
    flipg[...] = gd.T
    each(gather_core, TWO)
    h2 = widen_end(3, wide2)
    flip2[...] = h2.T

    def feed(cols):
        up = project(wide2[...].reshape(256, 1152), w2, cols, 2304) + bias_up[:, cols]
        upper[:, cols] = up
        acted[:, cols] = gelu_value(up).astype(jnp.bfloat16)

    for k, (first, stop) in enumerate(((0, 3), (3, 5), (5, 7), (7, 9))):
        columns_loop(stop, feed, first)
        each(gather_end, THREE, (k,))
    each(gather_core, THREE)
    back_to_width(acted[...], w3, slice(0, 2304), slice(4608, 6912), False)
    narrow_start(4, 1)
    for s in range(slots):
        down_keep[s] = part[s, t]

    def feed_back(cols):
        grad = project(wideg[...].reshape(256, 1152), w3, cols, 4608)
        low = (grad * gelu_slope(upper[:, cols])).astype(jnp.bfloat16)
        gup[:, cols] = low
        grad_bup[:, cols] = jnp.sum(low.astype(jnp.float32), axis=0, keepdims=True)

    columns_loop(9, feed_back)

    back_to_width(gup[...], w2, slice(0, 2304), slice(2304, 4608), False)
    narrow_start(5, 2)

    def weight_grad(flip, rows, cols, g, offset):
        made = dot(flip[...], rows[:, cols]).astype(jnp.bfloat16)
        g[:, :, cols] = made[:1024].reshape(64, 16, 256)
        tail_g[:, pl.ds(pl.multiple_of(offset + cols.start, 256), 256)] = made[1024:]

    each(sent, THREE)
    columns_loop(9, lambda cols: weight_grad(flipg, acted, cols, w3, 4608))
    each(scatter_twin, THREE)

    narrow_end(4, 1)
    for s in range(slots):
        grad = cot[s].astype(jnp.float32) * mod(s, 6)
        down = down_keep[s].astype(jnp.bfloat16).astype(jnp.float32) + narrow_recv[1, s].astype(jnp.float32)
        down = down + bias_d[1:2]
        wideg[s, t] = ((middle[s] + mod(s, 5) * down) * mod(s, 6)).astype(jnp.bfloat16)
        grad_mod[s, 5:6] = jnp.sum(grad * down, axis=0, keepdims=True)
    narrow_end(5, 2)
    for s in range(slots):
        grad = cot[s].astype(jnp.float32) * mod(s, 6)
        gh = narrowed(2, s)
        unit, inverse = normed(middle[s])
        grad_mod[s, 3:4] = jnp.sum(gh, axis=0, keepdims=True)
        grad_mod[s, 4:5] = jnp.sum(gh * unit, axis=0, keepdims=True)
        gm = grad + norm_back(gh * (1.0 + mod(s, 4)), unit, inverse)
        grad_mod[s, 2:3] = jnp.sum(gm * branch[s], axis=0, keepdims=True)
        middle[s] = gm
        wideb[s, t] = (mod(s, 2) * gm).astype(jnp.bfloat16)
    widen_start(6, wideb)
    each(scatter_relay, THREE, BACK)
    each(sent, TWO)
    columns_loop(9, lambda cols: weight_grad(flip2, gup, cols, w2, 2304))
    each(scatter_twin, TWO)
    each(scatter_direct, THREE, BACK)
    grad_bd[0:1] = sum(jnp.sum(wideb[s, t].astype(jnp.float32), axis=0, keepdims=True) for s in range(slots))
    flip1[...] = wide1[...].reshape(256, 1152).T
    gb = widen_end(6, wideb)
    flipb[...] = gb.T
    gatt = dot(gb[:, :1024], w1[:, :, 1664:2304].reshape(1024, 640)) + dot(gb[:, 1024:], tail_w[:, 1664:2304])
    each(scatter_on, THREE, BACK)
    each(scatter_relay, TWO, BACK)
    gattp[...] = dot(gatt.astype(jnp.bfloat16), join, 1, 1).astype(jnp.bfloat16)

    def attend_back(i, carry):
        rows = pl.ds(pl.multiple_of(i * 128, 128), 128)
        for h in range(8):
            lanes = slice(128 * h, 128 * h + 128)
            q, k, v = qkvp[0, rows, lanes], qkvp[1, rows, lanes], qkvp[2, rows, lanes]
            ga = gattp[rows, lanes]
            prob = probs[i, h]
            grad = dot(ga, v, 1, 1)
            inner = jnp.sum(prob * grad, axis=-1, keepdims=True)
            gs = (prob * (grad - inner)).astype(jnp.bfloat16)
            qkvp[0, rows, lanes] = (dot(gs, k) * factor).astype(jnp.bfloat16)
            qkvp[1, rows, lanes] = (dot(gs, q, 0, 0) * factor).astype(jnp.bfloat16)
            qkvp[2, rows, lanes] = dot(prob.astype(jnp.bfloat16), ga, 0, 0).astype(jnp.bfloat16)
        return carry

    attend_back(0, 0)
    each(scatter_direct, TWO, BACK)
    attend_back(1, 0)
    each(scatter_on, TWO, BACK)
    each(scatter_middle, THREE, BACK)
    gqkv[...] = jnp.zeros_like(gqkv)
    for i, lane in enumerate((0, 576, 1152)):
        low = lane // 128 * 128
        gather_heads = one_hot(
            (1024, 640), lambda a, b: (b - (lane - low) == (a // 128) * 72 + a % 128) & (a % 128 < 72)
        )
        piece = dot(qkvp[i], gather_heads).astype(jnp.bfloat16)
        gqkv[:, low : low + 640] = gqkv[:, low : low + 640] + piece
    grad_bqkv[...] = jnp.sum(gqkv[...].astype(jnp.float32), axis=0, keepdims=True)
    back_to_width(gqkv[...], w1, slice(0, 1792), slice(0, 1792), False)
    narrow_start(7, 3)

    each(scatter_middle, TWO, BACK)
    each(scatter_outer, THREE)
    each(sent, ONE)
    columns_loop(6, lambda cols: weight_grad(flip1, gqkv, cols, w1, 0))
    for low, high in ((1536, 1664), (1664, 1792), (1792, 2304)):
        made = 0.0
        if low < 1792:
            made = made + dot(flip1[...], gqkv[:, low:high])
        if high > 1664:
            made = made + dot(flipb[...], att[:, low - 1664 : high - 1664])
        made = made.astype(jnp.bfloat16)
        w1[:, :, low:high] = made[:1024].reshape(64, 16, high - low)
        tail_g[:, low:high] = made[1024:]
    tail_g[:, 6912:] = jnp.zeros((128, 256), jnp.bfloat16)
    total = jnp.zeros((1024, 896), jnp.float32)
    for j in range(8):
        pick = one_hot((1024, 128), lambda a, b: a == (b // 2) * 16 + (b % 2) * 8 + j)
        total = total + dot(pick, tail_g[:, 896 * j : 896 * j + 896])
    wt[...] = total.astype(jnp.bfloat16).reshape(64, 16, 896)
    each(scatter_twin, ONE)
    each(scatter_x, THREE)
    each(scatter_outer, TWO)
    each(scatter_relay, ONE, BACK)

    narrow_end(7, 3)
    for s in range(slots):
        gh = narrowed(3, s)
        unit, inverse = normed(lat[s].astype(jnp.float32))
        grad_mod[s, 0:1] = jnp.sum(gh, axis=0, keepdims=True)
        grad_mod[s, 1:2] = jnp.sum(gh * unit, axis=0, keepdims=True)
        middle[s] = middle[s] + norm_back(gh * (1.0 + mod(s, 1)), unit, inverse)
        grad_mod[s, 6:8] = jnp.zeros((2, 1152), jnp.float32)
    grad_bd[...] = unshuffled(thirds(grad_bd[...]))
    turn_ring_start()
    each(scatter_x, TWO)
    each(scatter_direct, ONE, BACK)
    turn_plane_start()
    each(scatter_end, THREE)
    each(scatter_on, ONE, BACK)
    tiles_plane()
    each(scatter_end, TWO)
    each(scatter_middle, ONE, (3, 2))
    tiles_ring()
    each(scatter_middle, ONE, (1, 0))
    tiles_back()
    grad_lat[...] = unshuffled(thirds(middle[...].reshape(128, 1152))).reshape(2, 64, 1152)
    done = jnp.concatenate([wideg[0, t], wideg[1, t]], axis=0)
    out[...] = unshuffled([done]).astype(jnp.bfloat16).reshape(2, 64, 1152)
    each(scatter_outer, ONE)
    tiles_out()
    each(scatter_x, ONE)
    each(scatter_end, ONE)
    tiles_end()
    each(sent, ALL)


def whole_block(args, weights, collective_id):
    f32, bf = jnp.float32, jnp.bfloat16
    m = len(WIDTHS)
    vmem = pl.BlockSpec(memory_space=pltpu.VMEM)
    shape = jax.ShapeDtypeStruct
    n = len(PIECES)

    def room(*lead):
        return [pltpu.VMEM(lead + (16, piece[2]), bf) for piece in PIECES]

    dma = pltpu.SemaphoreType.DMA
    return pl.pallas_call(
        block_kernel,
        out_shape=[
            shape((2, 64, 1152), bf), shape((2, 64, 1152), f32),
            *[shape((1, 16, width), f32) for width in WIDTHS],
            shape((96, 128), f32), shape((128, 8, 128), f32),
        ],
        in_specs=[vmem] * (len(args) + m),
        out_specs=[vmem] * (4 + m),
        scratch_shapes=[
            *[pltpu.VMEM((64, 16, width), bf) for width in WIDTHS],
            *[pltpu.VMEM((32, 16, width), bf) for width in WIDTHS],
            *room(4, 6), *room(6), *room(1),
            pltpu.VMEM((128, 7168), bf), pltpu.VMEM((128, 7168), bf),
            *[pltpu.VMEM((2, 2, 64, 1152), bf)] * 4,
            *[pltpu.VMEM((1152, 256), bf)] * 2,
            pltpu.VMEM((4, 2, 64, 1152), bf), pltpu.VMEM((4, 2, 64, 1152), bf),
            pltpu.VMEM((2, 2, 64, 1152), f32),
            pltpu.VMEM((3, 256, 1024), bf), pltpu.VMEM((2, 8, 128, 128), f32), pltpu.VMEM((256, 1024), bf),
            pltpu.VMEM((256, 1792), bf), pltpu.VMEM((256, 640), bf),
            pltpu.VMEM((256, 2304), f32), pltpu.VMEM((256, 2304), bf), pltpu.VMEM((256, 2304), bf),
            *[pltpu.VMEM((2, 64, 1152), f32)] * 3,
            dma((8,)), dma((8,)),
            dma((n,)), dma((n, 31)), dma((n, 16)), dma((n, 21)), dma((n, 16)), dma((n, 31)), dma((n, 16)),
            pltpu.VMEM((2, 8, 1152), f32), pltpu.VMEM((2, 8, 1152), f32),
            pltpu.VMEM((2, 1152), f32), pltpu.VMEM((1, 1792), f32), pltpu.VMEM((1, 2304), f32),
            pltpu.VMEM((16, 16, 128), bf), pltpu.VMEM((4, 16, 128), bf), pltpu.VMEM((8, 16, 128), bf),
            pltpu.VMEM((8, 16, 128), f32), pltpu.VMEM((8, 16, 128), f32),
            pltpu.VMEM((16, 8, 128), f32), pltpu.VMEM((16, 8, 128), f32),
            pltpu.VMEM((128, 8, 128), f32), pltpu.VMEM((16, 8, 8, 128), f32),
            pltpu.VMEM((8, 8, 128), f32), pltpu.VMEM((8, 8, 128), f32),
            dma((8,)), dma((8,)),
            pltpu.VMEM((2, 64, 1152), bf), pltpu.VMEM((2, 64, 1152), bf), pltpu.VMEM((2, 1152), f32),
        ],
        compiler_params=pltpu.CompilerParams(
            collective_id=collective_id, has_side_effects=True, vmem_limit_bytes=63 * 1024 * 1024
        ),
    )(*args, *weights)


MAIN = 1024
CHUNK = 896


def index_tables():
    place = np.arange(1152)
    tail = place - MAIN
    block = np.where(place < MAIN, place // 16, tail // 2)
    row = np.where(place < MAIN, place % 16, 16 + tail % 2)
    plane = (block // 8) % 4 * 4 + (block // 2) % 4
    ring = ((block % 2) * 2 + block // 32) * 2 + row // 9
    lane = np.arange(128)
    rows_at = (ring * PLANE + plane)[None, :] == lane[:, None]
    lanes_at = ((lane % 9)[:, None] == (row % 9)[None, :]) & (lane < 108)[:, None]
    kind = np.arange(16)
    kinds = (lane // 54 * 8 + lane % 54 // 9)[None, :] == kind[:, None]
    kinds = kinds & (lane < 108)[None, :]
    return [jnp.asarray(each.astype(np.float32), jnp.bfloat16) for each in (rows_at, lanes_at, kinds)]


def pack_rows(all_rows):
    third = all_rows.shape[1] // 3
    main, tail = all_rows[:16], all_rows[16:]
    tail = jnp.pad(tail, ((0, 0), (0, 8 * CHUNK - tail.shape[1]))).reshape(1, 16, CHUNK)
    return [*(main[None, :, i * third : (i + 1) * third] for i in range(3)), tail]


def unpack_rows(one, two, three, tail):
    width = one.shape[1] * 3
    main = jnp.concatenate([one, two, three], axis=1)
    return jnp.concatenate([main, tail.reshape(2, 8 * CHUNK)[:, :width]], axis=0)


def local(
    latents,
    condition,
    counts,
    order,
    w_ada,
    b_ada,
    w_qkv,
    b_qv,
    w_proj,
    b_proj,
    w_up,
    b_up,
    w_down,
    b_down,
    cotangent,
):
    slots = latents.shape[0]
    latent_count = condition.shape[0]
    group = lax.axis_index("fsdp")
    ranks = jnp.arange(counts.shape[0], dtype=jnp.int32)
    held = jnp.sum(jnp.where(ranks == group, counts, 0))
    before = jnp.sum(jnp.where(ranks < group, counts, 0))
    slot_rank = jnp.arange(slots, dtype=jnp.int32)
    live = (slot_rank < held).astype(jnp.float32)
    place = jnp.clip(before + slot_rank, 0, latent_count - 1)
    numbers = jnp.arange(latent_count, dtype=jnp.int32)
    owner = jnp.sum(jnp.where(numbers[None, :] == place[:, None], order[None, :], 0), axis=1)
    offsets = jnp.cumsum(counts) - counts
    every = jnp.clip(offsets[:, None] + slot_rank[None, :], 0, latent_count - 1).reshape(-1)
    owners = jnp.sum(jnp.where(numbers[None, :] == every[:, None], order[None, :], 0), axis=1)
    choose_all = (numbers[None, :] == owners[:, None]).astype(jnp.bfloat16)
    groups = counts.shape[0]
    devices = groups * 2
    soft_cond = jax.nn.silu(condition.astype(jnp.float32))
    ada_local = w_ada.astype(jnp.float32)
    mod_part = jnp.einsum("nd,dke->nke", soft_cond, ada_local, precision=highest) + b_ada
    mod_low = mod_part.astype(jnp.bfloat16).reshape(latent_count, -1)
    columns = mod_part.shape[2]
    mod_send = jnp.dot(choose_all, mod_low, preferred_element_type=jnp.float32).astype(jnp.bfloat16)
    mod_send = jnp.pad(
        mod_send.reshape(PLANE, 4, slots * 6 * columns), ((0, 0), (0, 12), (0, 128 - slots * 6 * columns))
    )
    alive_all = slot_rank[None, :] < counts[:, None]
    choose_two = jnp.where(
        (numbers[:, None, None] == owners.reshape(groups, slots)[None]) & alive_all[None], 1.0, 0.0
    )
    choose_two = jnp.transpose(choose_two, (2, 0, 1)).reshape(slots, latent_count, PLANE, 4)
    choose_two = jnp.pad(choose_two, ((0, 0), (0, 0), (0, 0), (0, 4))).reshape(slots, latent_count, 128)
    ada = jnp.transpose(w_ada.reshape(w_ada.shape[0], -1))
    ada = jnp.concatenate([ada, ada, jnp.zeros((128 - 2 * ada.shape[0], ada.shape[1]), ada.dtype)], axis=0)
    bias_d = jnp.stack([b_proj, b_down])
    own_rows = jnp.concatenate([w_qkv[0], w_qkv[1], w_qkv[2], w_proj.T, w_up, w_down.T], axis=1)
    width = own_rows.shape[1]
    head_part = w_qkv.shape[2]
    weights = pack_rows(own_rows)
    live_rows = jnp.broadcast_to(live[:, None, None], (slots, 1, latents.shape[2]))
    nothing = jnp.zeros_like(b_qv[0])
    bias_qkv = jnp.concatenate([b_qv[0], nothing, b_qv[1], nothing])[None]
    block_output, grad_latents, *grads, grad_table, tiles = whole_block(
        (latents, cotangent, live_rows, bias_d, bias_qkv, b_up[None], mod_send, choose_two, ada, *index_tables()),
        weights,
        2,
    )
    summed = unpack_rows(*(each[0] for each in grads))
    grad_w_qkv = jnp.stack([summed[:, i * head_part : (i + 1) * head_part] for i in range(3)])
    grad_w_proj = summed[:, 3 * head_part : 4 * head_part].T
    up_part = w_up.shape[1]
    grad_w_up = summed[:, 4 * head_part : 4 * head_part + up_part]
    grad_w_down = summed[:, 4 * head_part + up_part :].T
    used = 6 * columns
    grad_mod_part = (grad_table[:, :used] + grad_table[:, used : 2 * used]).reshape(latent_count, 6, columns)
    grad_b_ada = jnp.sum(grad_mod_part, axis=0)
    grad_w_ada = jnp.einsum("nd,nke->dke", soft_cond, grad_mod_part, precision=highest)
    grad_soft = jnp.transpose(tiles[:108].reshape(12, 9, 8, 128), (0, 2, 1, 3)).reshape(latent_count, -1)
    lines = tiles[108:].reshape(-1, 128)
    grad_b_proj, grad_b_down = lines[:9].reshape(-1), lines[9:18].reshape(-1)
    halves = lax.dynamic_slice_in_dim(lines, 18 + 32 * lax.axis_index("tp"), 32, 0)
    frame = halves[:14].reshape(-1)
    grad_b_qv = jnp.stack([frame[:head_part], frame[2 * head_part : 3 * head_part]])
    grad_b_up = halves[14:].reshape(-1)
    grad_condition = jax.vjp(jax.nn.silu, condition.astype(jnp.float32))[1](grad_soft)[0]
    return (
        block_output,
        grad_latents,
        grad_condition,
        grad_w_ada,
        grad_b_ada,
        grad_w_qkv,
        grad_b_qv,
        grad_w_proj,
        grad_b_proj,
        grad_w_up,
        grad_b_up,
        grad_w_down,
        grad_b_down,
    )


def solution(mesh):
    in_specs = (
        P("fsdp", "tp", None),
        P(),
        P(),
        P(),
        P(None, None, ("fsdp", "tp")),
        P(None, ("fsdp", "tp")),
        P(None, "fsdp", "tp"),
        P(None, "tp"),
        P("tp", "fsdp"),
        P(),
        P("fsdp", "tp"),
        P("tp"),
        P("tp", "fsdp"),
        P(),
        P("fsdp", "tp", None),
    )
    out_specs = (
        P("fsdp", "tp", None),
        P("fsdp", "tp", None),
        P(),
        P(None, None, ("fsdp", "tp")),
        P(None, ("fsdp", "tp")),
        P(None, "fsdp", "tp"),
        P(None, "tp"),
        P("tp", "fsdp"),
        P(),
        P("fsdp", "tp"),
        P("tp"),
        P("tp", "fsdp"),
        P(),
    )
    return jax.shard_map(local, mesh=mesh, in_specs=in_specs, out_specs=out_specs, check_vma=False)
```

```python
import jax
import jax.numpy as jnp
import numpy as np
from jax import lax
from jax.experimental import pallas as pl
from jax.experimental.pallas import tpu as pltpu
from jax.sharding import PartitionSpec as P

MESH = pl.DeviceIdType.MESH
OFFS = (0, 3, 1, 2)
WIDTHS = (2304, 2304, 2304, 896)
PIECES = (
    (3, 0, 896, "z"),
    (0, 0, 1152, "z"),
    (0, 1152, 1152, "y"),
    (1, 0, 1152, "z"),
    (1, 1152, 1152, "y"),
    (2, 0, 1152, "z"),
    (2, 1152, 1152, "y"),
)
ONE, TWO, THREE = (0, 1, 2), (3, 4), (5, 6)
ALL = ONE + TWO + THREE
BACK = (3, 2, 1, 0)


highest = lax.Precision.HIGHEST
norm_eps = 1e-06


def place_of():
    f = lax.axis_index("fsdp")
    return f // 16, (f // 4) % 4, (f // 2) % 2, f % 2, lax.axis_index("tp")


def peers(z, y, x, c, t):
    def at(z, y, x, c):
        return (z * 16 + y * 4 + x * 2 + c, t)

    return {
        "z": (at((z + 3) % 4, y, x, c), at((z + 1) % 4, y, x, c)),
        "y": (at(z, (y + 3) % 4, x, c), at(z, (y + 1) % 4, x, c)),
        "x": at(z, y, 1 - x, c),
        "c": at(z, y, x, 1 - c),
        "t": (z * 16 + y * 4 + x * 2 + c, 1 - t),
    }


def ring_peer(i):
    f, t = lax.axis_index("fsdp"), lax.axis_index("tp")
    other = (f % 4 * 2 + t + i) % RING
    return other, (f // 4 * 4 + other // 2, other % 2)


def plane_peer(i):
    f, t = lax.axis_index("fsdp"), lax.axis_index("tp")
    other = (f // 4 + i) % PLANE
    return other, (other * 4 + f % 4, t)


def greet():
    barrier = pltpu.get_barrier_semaphore()

    def hello(peer):
        def go(i, carry):
            pl.semaphore_signal(barrier, inc=1, device_id=peer(i)[1], device_id_type=MESH)
            return carry

        return go

    lax.fori_loop(1, PLANE, hello(plane_peer), 0)
    lax.fori_loop(1, RING, hello(ring_peer), 0)
    pl.semaphore_wait(barrier, PLANE + RING - 2)


def add_into(dst, *srcs):
    for i in range(dst.shape[0]):
        total = srcs[0][i].astype(jnp.float32)
        for src in srcs[1:]:
            total = total + src[i].astype(jnp.float32)
        dst[i] = total.astype(dst.dtype)


PLANE, RING = 16, 8


def one_hot(shape, rule):
    first = lax.broadcasted_iota(jnp.int32, shape, 0)
    second = lax.broadcasted_iota(jnp.int32, shape, 1)
    return jnp.where(rule(first, second), 1.0, 0.0).astype(jnp.bfloat16)


def dot(a, b, ca=1, cb=0):
    return lax.dot_general(a, b, (((ca,), (cb,)), ((), ())), preferred_element_type=jnp.float32)


def normed(rows):
    centred = rows - jnp.mean(rows, axis=-1, keepdims=True)
    inverse = lax.rsqrt(jnp.mean(centred * centred, axis=-1, keepdims=True) + norm_eps)
    return centred * inverse, inverse


def norm_back(grad, unit, inverse):
    first = jnp.mean(grad, axis=-1, keepdims=True)
    second = jnp.mean(grad * unit, axis=-1, keepdims=True)
    return inverse * (grad - first - unit * second)


def gelu_slope(u):
    a, b = 0.7978845608028654, 0.044715
    wave = jnp.tanh(a * (u + b * (u * u * u)))
    return 0.5 * (1.0 + wave) + 0.5 * u * (1.0 - wave * wave) * (a * (1.0 + 3.0 * b * (u * u)))


def gelu_value(u):
    a, b = 0.7978845608028654, 0.044715
    return 0.5 * u * (1.0 + jnp.tanh(a * (u + b * (u * u * u))))


def columns_loop(count, body, first=0):
    def step(i, carry):
        body(pl.ds(pl.multiple_of(i * 256, 256), 256))
        return carry

    lax.fori_loop(first, count, step, 0)


def block_kernel(*refs):
    n, m = len(PIECES), len(WIDTHS)
    (lat_in, cot_in, live, bias_in, bias_qkv, bias_up, mod_send, choose, ada, rows_at, lanes_at, kinds), ins = (
        refs[:12],
        refs[12 : 12 + m],
    )
    refs = refs[12 + m :]
    (out, grad_lat), outs, (table_grad, tiles) = refs[:2], refs[2 : 2 + m], refs[2 + m : 4 + m]
    refs = refs[4 + m :]
    ws, twins = refs[:m], refs[m : 2 * m]
    refs = refs[2 * m :]
    inner, outer, last = (refs[i * n : (i + 1) * n] for i in range(3))
    (
        tail_w, tail_g, wide1, wideg, wide2, wideb, flip_one, flip_two,
        narrow_send, narrow_recv, part, qkvp, probs, gattp, gqkv, att,
        upper, acted, gup, middle, branch, down_keep, send_sem, recv_sem,
        local_sem, way_send, core_send, way_recv, core_recv, back_recv, back_core,
        mods, grad_mod, grad_bd, grad_bqkv, grad_bup,
        mod_plane, mod_turn, mod_ring, turn_send, turn_ring, turn_plane_send, turn_plane,
        tile_send, tile_plane, tile_part, tile_ring, small_send, small_recv, lat, cot, bias_d,
    ) = refs[3 * n :]
    w1, w2, w3, wt = ws
    flip1 = flipg = flip_one
    flip2 = flipb = flip_two
    qk = gup
    slots = lat.shape[0]
    z, y, x, c, t = place_of()
    near = peers(z, y, x, c, t)
    partner = near["t"]
    greet()
    pending = {p: [] for p in range(n)}

    def far(src, dst, ssem, rsem, peer):
        return pltpu.make_async_remote_copy(
            src_ref=src, dst_ref=dst, send_sem=ssem, recv_sem=rsem, device_id=peer, device_id_type=MESH
        )

    def axes(p):
        if PIECES[p][3] == "z":
            return z, y, near["z"], near["y"]
        return y, z, near["y"], near["z"]

    def spot(p, u, v, core=c):
        return core * 32 + (u * 8 + v * 2 if PIECES[p][3] == "z" else v * 8 + u * 2)

    def block(p, at, count=1, of=ws):
        r, low, width, first = PIECES[p]
        return of[r].at[pl.ds(at, count), :, pl.ds(low, width)]

    def push(p, k, ref, peer, src=None):
        cp = far(ref if src is None else src, ref, way_send.at[p, k], way_recv.at[p, k], peer)
        cp.start()
        pending[p].append(cp)

    def arrive(p, k, ref):
        far(ref, ref, way_send.at[p, k], way_recv.at[p, k], near["x"]).wait_recv()

    def share(p, k, ref):
        cp = far(ref, ref, core_send.at[p, k], core_recv.at[p, k], near["c"])
        cp.start()
        pending[p].append(cp)

    def gather_begin(p):
        r, low, width, first = PIECES[p]
        mine = ins[r].at[:, :, pl.ds(low, width)]
        own = block(p, c * 32 + z * 8 + y * 2 + x)
        push(p, 0, own, near["x"], mine)
        pltpu.make_async_copy(mine, own, local_sem.at[p]).start()

    def gather_x(p):
        u, v, one, two = axes(p)
        r, low, width, first = PIECES[p]
        own = block(p, c * 32 + z * 8 + y * 2 + x)
        pltpu.make_async_copy(ins[r].at[:, :, pl.ds(low, width)], own, local_sem.at[p]).wait()
        arrive(p, 0, block(p, c * 32 + z * 8 + y * 2 + 1 - x))
        pair = block(p, spot(p, u, v), 2)
        push(p, 1, pair, one[1])
        push(p, 2, pair, one[0])
        share(p, 0, pair)

    def gather_first(p):
        u, v, one, two = axes(p)
        for k, way in ((1, 1), (2, 0)):
            uu = (u + OFFS[k]) % 4
            pair = block(p, spot(p, uu, v), 2)
            arrive(p, k, pair)
            push(p, 2 + k, block(p, spot(p, uu, v) + 1 - way), one[way])
            share(p, 4 * k, pair)

    def gather_first_end(p):
        u, v, one, two = axes(p)
        uu = (u + 2) % 4
        arrive(p, 3, block(p, spot(p, uu, v)))
        arrive(p, 4, block(p, spot(p, uu, v) + 1))
        share(p, 12, block(p, spot(p, uu, v), 2))

    def gather_second(p, ks):
        u, v, one, two = axes(p)
        for k in ks:
            pair = block(p, spot(p, (u + OFFS[k]) % 4, v), 2)
            push(p, 5 + 4 * k, pair, two[1])
            push(p, 6 + 4 * k, pair, two[0])

    def gather_relay(p, ks):
        u, v, one, two = axes(p)
        for k in ks:
            uu = (u + OFFS[k]) % 4
            for side, way in ((1, 1), (2, 0)):
                vv = (v + OFFS[side]) % 4
                pair = block(p, spot(p, uu, vv), 2)
                arrive(p, 4 + 4 * k + side, pair)
                push(p, 6 + 4 * k + side, block(p, spot(p, uu, vv) + 1 - way), two[way])
                share(p, 4 * k + side, pair)

    def gather_end(p, ks):
        u, v, one, two = axes(p)
        for k in ks:
            uu, vv = (u + OFFS[k]) % 4, (v + 2) % 4
            arrive(p, 7 + 4 * k, block(p, spot(p, uu, vv)))
            arrive(p, 8 + 4 * k, block(p, spot(p, uu, vv) + 1))
            share(p, 4 * k + 3, block(p, spot(p, uu, vv), 2))

    def gather_core(p):
        for k in range(16):
            ref = block(p, (1 - c) * 32 + 2 * k, 2)
            far(ref, ref, core_send.at[p, k], core_recv.at[p, k], near["c"]).wait_recv()

    def sent(p):
        for cp in pending[p]:
            cp.wait_send()
        pending[p].clear()

    def back(p, k, src, dst, peer):
        cp = far(src, dst, way_send.at[p, k], back_recv.at[p, k], peer)
        cp.start()
        pending[p].append(cp)

    def came(p, k, ref):
        far(ref, ref, way_send.at[p, k], back_recv.at[p, k], near["x"]).wait_recv()

    def twin_of(p, at):
        return block(p, at, 2, twins)

    def scatter_twin(p):
        u, v, one, two = axes(p)
        for side in BACK:
            for k in BACK:
                at = spot(p, (u + OFFS[k]) % 4, (v + OFFS[side]) % 4, 0)
                j = 4 * k + side
                cp = far(block(p, (1 - c) * 32 + at, 2), twin_of(p, at), core_send.at[p, j], back_core.at[p, j], near["c"])
                cp.start()
                pending[p].append(cp)

    def combine(p, k, side):
        u, v, one, two = axes(p)
        at = spot(p, (u + OFFS[k]) % 4, (v + OFFS[side]) % 4, 0)
        j = 4 * k + side
        twin = twin_of(p, at)
        far(twin, twin, core_send.at[p, j], back_core.at[p, j], near["c"]).wait_recv()
        own = block(p, c * 32 + at, 2)
        add_into(own, own, twin)
        return c * 32 + at

    def scatter_relay(p, ks):
        u, v, one, two = axes(p)
        for k in ks:
            at = combine(p, k, 3)
            back(p, 6 * k, block(p, at), inner[p].at[k, pl.ds(0, 1)], two[1])
            back(p, 6 * k + 1, block(p, at + 1), inner[p].at[k, pl.ds(1, 1)], two[0])

    def scatter_direct(p, ks):
        u, v, one, two = axes(p)
        for k in ks:
            at = combine(p, k, 2)
            back(p, 6 * k + 2, block(p, at + 1), inner[p].at[k, pl.ds(2, 1)], two[1])
            at = combine(p, k, 1)
            back(p, 6 * k + 4, block(p, at), inner[p].at[k, pl.ds(4, 1)], two[0])

    def scatter_on(p, ks):
        u, v, one, two = axes(p)
        for k in ks:
            for j, side, way in ((0, 2, 1), (1, 1, 0)):
                came(p, 6 * k + j, inner[p].at[k, pl.ds(j, 1)])
                own = block(p, spot(p, (u + OFFS[k]) % 4, (v + OFFS[side]) % 4) + j)
                add_into(own, own, inner[p].at[k, pl.ds(j, 1)])
                back(p, 6 * k + 3 + 2 * j, own, inner[p].at[k, pl.ds(3 + 2 * j, 1)], two[way])

    def scatter_middle(p, ks):
        u, v, one, two = axes(p)
        for k in ks:
            at = combine(p, k, 0)
            for j in range(2, 6):
                came(p, 6 * k + j, inner[p].at[k, pl.ds(j, 1)])
            held = [inner[p].at[k, pl.ds(j, 1)] for j in range(6)]
            add_into(block(p, at), block(p, at), held[3], held[4])
            add_into(block(p, at + 1), block(p, at + 1), held[2], held[5])
            if k == 3:
                back(p, 24, block(p, at), outer[p].at[pl.ds(0, 1)], one[1])
                back(p, 25, block(p, at + 1), outer[p].at[pl.ds(1, 1)], one[0])
            if k == 2:
                back(p, 26, block(p, at + 1), outer[p].at[pl.ds(2, 1)], one[1])
            if k == 1:
                back(p, 28, block(p, at), outer[p].at[pl.ds(4, 1)], one[0])

    def scatter_outer(p):
        u, v, one, two = axes(p)
        for j, side, way in ((0, 2, 1), (1, 1, 0)):
            came(p, 24 + j, outer[p].at[pl.ds(j, 1)])
            own = block(p, spot(p, (u + OFFS[side]) % 4, v) + j)
            add_into(own, own, outer[p].at[pl.ds(j, 1)])
            back(p, 27 + 2 * j, own, outer[p].at[pl.ds(3 + 2 * j, 1)], one[way])

    def scatter_x(p):
        u, v, one, two = axes(p)
        for j in range(2, 6):
            came(p, 24 + j, outer[p].at[pl.ds(j, 1)])
        held = [outer[p].at[pl.ds(j, 1)] for j in range(6)]
        at = spot(p, u, v)
        add_into(block(p, at), block(p, at), held[3], held[4])
        add_into(block(p, at + 1), block(p, at + 1), held[2], held[5])
        back(p, 30, block(p, at + 1 - x), last[p], near["x"])

    def scatter_end(p):
        r, low, width, first = PIECES[p]
        u, v, one, two = axes(p)
        came(p, 30, last[p])
        add_into(outs[r].at[:, :, pl.ds(low, width)], block(p, spot(p, u, v) + x), last[p])

    def spread(k, peer, count, source, target):
        def go(i, carry):
            other, where = peer(i)
            far(source(other), target, small_send.at[k], small_recv.at[k], where).start()
            return carry

        lax.fori_loop(1, count, go, 0)

    def settle(k, count, buffer):
        ref = buffer.at[pl.ds(0, count - 1)]
        pltpu.make_async_copy(ref, ref, small_recv.at[k]).wait()

    def settle_sent(k, count, buffer):
        ref = buffer.at[pl.ds(0, count - 1)]
        pltpu.make_async_copy(ref, ref, small_send.at[k]).wait()

    plane_me = lax.axis_index("fsdp") // 4
    ring_me = lax.axis_index("fsdp") % 4 * 2 + t

    def exact(a, b, ca=1, cb=0):
        return lax.dot_general(
            a, b, (((ca,), (cb,)), ((), ())), precision=highest, preferred_element_type=jnp.float32
        )

    def table_plane():
        mod_plane[plane_me] = mod_send[plane_me]
        spread(0, plane_peer, PLANE, lambda other: mod_send.at[other], mod_plane.at[plane_me])

    def table_ring():
        settle(0, PLANE, mod_plane)
        pick = one_hot((64, 256), lambda a, b: b == (a % 16) * 16 + a // 16)
        turned = dot(pick, mod_plane[...].reshape(256, 128)).astype(jnp.bfloat16)
        mod_turn[...] = turned.reshape(4, 16, 128)
        mod_ring[ring_me] = mod_turn[ring_me // 2]
        spread(1, ring_peer, RING, lambda other: mod_turn.at[other // 2], mod_ring.at[ring_me])

    def table_end():
        settle(1, RING, mod_ring)
        wide = dot(mod_ring[...].reshape(128, 128), rows_at[...], 0, 0)
        wide = (wide * lanes_at[...].astype(jnp.float32)).astype(jnp.bfloat16)
        both = dot(kinds[...], wide)
        mods[0] = both[:8]
        mods[1] = both[8:]

    def turn_ring_start():
        both = jnp.concatenate([grad_mod[0], grad_mod[1]], axis=0)
        wide = exact(kinds[...].astype(jnp.float32), both, 0, 0) * lanes_at[...].astype(jnp.float32)
        turn_send[...] = exact(rows_at[...].astype(jnp.float32), wide, 1, 1).reshape(RING, PLANE, 128)
        turn_ring[ring_me] = turn_send[ring_me]
        spread(2, ring_peer, RING, lambda other: turn_send.at[other], turn_ring.at[ring_me])

    def turn_plane_start():
        settle(2, RING, turn_ring)
        whole = jnp.concatenate([turn_ring[2 * r] + turn_ring[2 * r + 1] for r in range(4)], axis=0)
        pick = one_hot((128, 64), lambda a, b: (b == (a % 8) * 16 + a // 8) & (a % 8 < 4))
        turn_plane_send[...] = exact(pick.astype(jnp.float32), whole).reshape(PLANE, 8, 128)
        turn_plane[plane_me] = turn_plane_send[plane_me]
        spread(3, plane_peer, PLANE, lambda other: turn_plane_send.at[other], turn_plane.at[plane_me])

    def tiles_plane():
        settle(3, PLANE, turn_plane)
        found = turn_plane[...].reshape(128, 128)
        lane = lax.broadcasted_iota(jnp.int32, (96, 128), 1)
        table = jnp.where(lane < 54, exact(choose[0], found), exact(choose[1], found))
        table_grad[...] = table
        soft = exact(table, ada[...].astype(jnp.float32))
        for i in range(12):
            for j in range(9):
                tile_send[i * 9 + j] = soft[8 * i : 8 * i + 8, 128 * j : 128 * j + 128]
        tile_send[108:] = jnp.zeros((20, 8, 128), jnp.float32)

        def line(row, value):
            tile_send[108 + row // 8, row % 8 : row % 8 + 1, :] = value

        for j in range(9):
            line(j, grad_bd[0:1, 128 * j : 128 * j + 128])
            line(9 + j, grad_bd[1:2, 128 * j : 128 * j + 128])
        for half in range(2):
            for j in range(14):
                line(18 + 32 * half + j, jnp.where(t == half, grad_bqkv[:, 128 * j : 128 * j + 128], 0.0))
            for j in range(18):
                line(32 + 32 * half + j, jnp.where(t == half, grad_bup[:, 128 * j : 128 * j + 128], 0.0))
        tile_plane[plane_me] = tile_send[pl.ds(plane_me * 8, 8)]
        spread(4, plane_peer, PLANE, lambda other: tile_send.at[pl.ds(other * 8, 8)], tile_plane.at[plane_me])

    def tiles_ring():
        settle(4, PLANE, tile_plane)
        total = tile_plane[0]
        for i in range(1, PLANE):
            total = total + tile_plane[i]
        tile_part[...] = total
        tile_ring[ring_me] = tile_part[ring_me]
        spread(5, ring_peer, RING, lambda other: tile_part.at[other], tile_ring.at[ring_me])

    def tiles_back():
        settle(5, RING, tile_ring)
        total = tile_ring[0]
        for i in range(1, RING):
            total = total + tile_ring[i]
        own = tiles.at[plane_me * 8 + ring_me]
        own[...] = total
        spread(6, ring_peer, RING, lambda other: own, own)

    def tiles_out():
        settle(6, RING, tiles)
        own = tiles.at[pl.ds(plane_me * 8, 8)]
        spread(7, plane_peer, PLANE, lambda other: own, own)

    def tiles_end():
        ref = tiles.at[pl.ds(0, 8 * PLANE - 8)]
        pltpu.make_async_copy(ref, ref, small_recv.at[7]).wait()
        settle_sent(0, PLANE, mod_plane)
        settle_sent(1, RING, mod_ring)
        settle_sent(2, RING, turn_ring)
        settle_sent(3, PLANE, turn_plane)
        settle_sent(4, PLANE, tile_plane)
        settle_sent(5, RING, tile_ring)
        settle_sent(6, RING, tiles)
        pltpu.make_async_copy(ref, ref, small_send.at[7]).wait()

    def each(step, group, *rest):
        for p in group:
            step(p, *rest)

    def remote(k, src, dst):
        return far(src, dst, send_sem.at[k], recv_sem.at[k], partner)

    def widen_start(k, wide):
        remote(k, wide.at[:, t], wide.at[:, t]).start()

    def widen_end(k, wide):
        remote(k, wide.at[:, 1 - t], wide.at[:, 1 - t]).wait()
        return wide[...].reshape(256, wide.shape[-1])

    def narrow_start(k, n):
        for s in range(slots):
            narrow_send[n, s] = part[s, 1 - t].astype(jnp.bfloat16)
        remote(k, narrow_send.at[n], narrow_recv.at[n]).start()

    def narrow_end(k, n):
        remote(k, narrow_send.at[n], narrow_recv.at[n]).wait()

    def narrowed(n, s):
        return part[s, t].astype(jnp.bfloat16).astype(jnp.float32) + narrow_recv[n, s].astype(jnp.float32)

    def mod(s, k):
        return live[s] if k == 6 else mods[s, k : k + 1, :]

    table_plane()
    each(gather_begin, ALL)
    each(gather_x, ALL)
    table_ring()
    each(gather_first, ONE)
    each(gather_second, ONE, (0, 1, 2))
    each(gather_first, TWO + THREE)
    table_end()
    def chosen(i):
        place = lax.broadcasted_iota(jnp.int32, (1, 128), 1)
        if i < 8:
            place = place + 128 * i
            number, row = place // 16, place % 16
        else:
            number, row = place // 2, 16 + place % 2
        group = (number // 8) % 4 * 16 + (number // 2) % 4 * 4 + number % 2 * 2 + number // 32
        source = group * 18 + row
        return jnp.where(lax.broadcasted_iota(jnp.int32, (1152, 128), 0) == source, 1.0, 0.0).astype(jnp.bfloat16)

    def thirds(rows):
        high = rows.astype(jnp.bfloat16)
        rest = rows - high.astype(jnp.float32)
        middle_part = rest.astype(jnp.bfloat16)
        low = (rest - middle_part.astype(jnp.float32)).astype(jnp.bfloat16)
        return high, middle_part, low

    def unshuffled(parts):
        total = None
        for i in range(9):
            pick = chosen(i)
            for part_rows in parts:
                term = dot(part_rows[:, 128 * i : 128 * i + 128], pick, 1, 1)
                total = term if total is None else total + term
        return total

    both_rows = jnp.concatenate([lat_in[0], lat_in[1], cot_in[0], cot_in[1]], axis=0)
    bias_parts = thirds(bias_in[...])
    for i in range(9):
        pick = chosen(i)
        lanes = slice(128 * i, 128 * i + 128)
        moved = dot(both_rows, pick).astype(jnp.bfloat16)
        for s in range(slots):
            lat[s, :, lanes] = moved[64 * s : 64 * s + 64]
            cot[s, :, lanes] = moved[128 + 64 * s : 192 + 64 * s]
        bias_d[:, lanes] = sum(dot(each_part, pick) for each_part in bias_parts)
    for s in range(slots):
        unit, inverse = normed(lat[s].astype(jnp.float32))
        wide1[s, t] = (unit * (1.0 + mod(s, 1)) + mod(s, 0)).astype(jnp.bfloat16)
    widen_start(0, wide1)
    for s in range(slots):
        grad = cot[s].astype(jnp.float32) * mod(s, 6)
        wideg[s, t] = (mod(s, 5) * grad).astype(jnp.bfloat16)
    widen_start(1, wideg)
    grad_bd[1:2] = sum(jnp.sum(wideg[s, t].astype(jnp.float32), axis=0, keepdims=True) for s in range(slots))

    each(gather_first_end, ONE)
    each(gather_second, ONE, (3,))
    for k in range(4):
        each(gather_relay, ONE, (k,))
    each(gather_first_end, TWO)
    each(gather_second, TWO, range(4))
    each(gather_first_end, THREE)
    each(gather_second, THREE, range(4))
    each(gather_end, ONE, range(4))
    each(gather_core, ONE)
    turn = one_hot((256, 256), lambda a, b: b == (a % 32 // 2) * 16 + (a % 2) * 8 + a // 32)
    for i in range(4):
        turned = dot(turn, wt[16 * i : 16 * i + 16].reshape(256, 896)).astype(jnp.bfloat16)
        for j in range(8):
            tail_w[32 * i : 32 * i + 32, 896 * j : 896 * j + 896] = turned[32 * j : 32 * j + 32]

    widen_end(0, wide1)

    def project(rows, w, cols, offset):
        return dot(rows[:, :1024], w[:, :, cols].reshape(1024, 256)) + dot(
            rows[:, 1024:], tail_w[:, pl.ds(pl.multiple_of(offset + cols.start, 256), 256)]
        )

    def to_qkv(cols):
        flat = project(wide1[...].reshape(256, 1152), w1, cols, 0) + bias_qkv[:, cols]
        qk[:, cols] = flat.astype(jnp.bfloat16)

    columns_loop(9, to_qkv)
    for k in range(4):
        each(gather_relay, TWO, (k,))
    for i, lane in enumerate((0, 576, 1152)):
        low = lane // 128 * 128
        spread_heads = one_hot(
            (640, 1024), lambda a, b: (a - (lane - low) == (b // 128) * 72 + b % 128) & (b % 128 < 72)
        )
        qkvp[i] = dot(qk[:, low : low + 640], spread_heads).astype(jnp.bfloat16)

    factor = 72 ** (-0.5)

    def attend(i, carry):
        rows = pl.ds(pl.multiple_of(i * 128, 128), 128)
        for h in range(8):
            lanes = slice(128 * h, 128 * h + 128)
            q, k, v = qkvp[0, rows, lanes], qkvp[1, rows, lanes], qkvp[2, rows, lanes]
            scores = dot(q, k, 1, 1) * factor
            raised = jnp.exp(scores - jnp.max(scores, axis=-1, keepdims=True))
            prob = raised / jnp.sum(raised, axis=-1, keepdims=True)
            probs[i, h] = prob
            gattp[rows, lanes] = dot(prob.astype(jnp.bfloat16), v).astype(jnp.bfloat16)
        return carry

    attend(0, 0)
    each(gather_end, TWO, (0, 1))
    attend(1, 0)
    each(gather_end, TWO, (2, 3))
    join = one_hot((1024, 640), lambda a, b: (b - 64 == (a // 128) * 72 + a % 128) & (a % 128 < 72))
    att[...] = dot(gattp[...], join).astype(jnp.bfloat16)

    def back_to_width(rows, w, cols, tail_cols, add):
        total = dot(rows, w[:, :, cols].reshape(1024, -1), 1, 1)
        tail = dot(rows, tail_w[:, tail_cols], 1, 1)
        main = part.at[:, :, :, 0:1024]
        rest = part.at[:, :, :, 1024:1152]
        total, tail = total.reshape(slots, 2, 64, 1024), tail.reshape(slots, 2, 64, 128)
        main[...] = main[...] + total if add else total
        rest[...] = rest[...] + tail if add else tail

    back_to_width(att[...], w1, slice(1664, 2304), slice(1664, 2304), False)
    narrow_start(2, 0)
    for k in range(2):
        each(gather_relay, THREE, (k,))
    narrow_end(2, 0)
    for s in range(slots):
        piece = narrowed(0, s) + bias_d[0:1]
        branch[s] = piece
        rows = lat[s].astype(jnp.float32) + mod(s, 2) * piece
        middle[s] = rows
        unit, inverse = normed(rows)
        wide2[s, t] = (unit * (1.0 + mod(s, 4)) + mod(s, 3)).astype(jnp.bfloat16)
    widen_start(3, wide2)
    for k in range(2, 4):
        each(gather_relay, THREE, (k,))
    gd = widen_end(1, wideg)
    flipg[...] = gd.T
    each(gather_core, TWO)
    h2 = widen_end(3, wide2)
    flip2[...] = h2.T

    def feed(cols):
        up = project(wide2[...].reshape(256, 1152), w2, cols, 2304) + bias_up[:, cols]
        upper[:, cols] = up
        acted[:, cols] = gelu_value(up).astype(jnp.bfloat16)

    for k, (first, stop) in enumerate(((0, 3), (3, 5), (5, 7), (7, 9))):
        columns_loop(stop, feed, first)
        each(gather_end, THREE, (k,))
    each(gather_core, THREE)
    back_to_width(acted[...], w3, slice(0, 2304), slice(4608, 6912), False)
    narrow_start(4, 1)
    for s in range(slots):
        down_keep[s] = part[s, t]

    def feed_back(cols):
        grad = project(wideg[...].reshape(256, 1152), w3, cols, 4608)
        low = (grad * gelu_slope(upper[:, cols])).astype(jnp.bfloat16)
        gup[:, cols] = low
        grad_bup[:, cols] = jnp.sum(low.astype(jnp.float32), axis=0, keepdims=True)

    columns_loop(9, feed_back)

    back_to_width(gup[...], w2, slice(0, 2304), slice(2304, 4608), False)
    narrow_start(5, 2)

    def weight_grad(flip, rows, cols, g, offset):
        made = dot(flip[...], rows[:, cols]).astype(jnp.bfloat16)
        g[:, :, cols] = made[:1024].reshape(64, 16, 256)
        tail_g[:, pl.ds(pl.multiple_of(offset + cols.start, 256), 256)] = made[1024:]

    each(sent, THREE)
    columns_loop(9, lambda cols: weight_grad(flipg, acted, cols, w3, 4608))
    each(scatter_twin, THREE)
    each(sent, TWO)
    columns_loop(9, lambda cols: weight_grad(flip2, gup, cols, w2, 2304))
    each(scatter_twin, TWO)
    each(scatter_relay, THREE, BACK)

    narrow_end(4, 1)
    for s in range(slots):
        grad = cot[s].astype(jnp.float32) * mod(s, 6)
        down = down_keep[s].astype(jnp.bfloat16).astype(jnp.float32) + narrow_recv[1, s].astype(jnp.float32)
        down = down + bias_d[1:2]
        wideg[s, t] = ((middle[s] + mod(s, 5) * down) * mod(s, 6)).astype(jnp.bfloat16)
        grad_mod[s, 5:6] = jnp.sum(grad * down, axis=0, keepdims=True)
    narrow_end(5, 2)
    for s in range(slots):
        grad = cot[s].astype(jnp.float32) * mod(s, 6)
        gh = narrowed(2, s)
        unit, inverse = normed(middle[s])
        grad_mod[s, 3:4] = jnp.sum(gh, axis=0, keepdims=True)
        grad_mod[s, 4:5] = jnp.sum(gh * unit, axis=0, keepdims=True)
        gm = grad + norm_back(gh * (1.0 + mod(s, 4)), unit, inverse)
        grad_mod[s, 2:3] = jnp.sum(gm * branch[s], axis=0, keepdims=True)
        middle[s] = gm
        wideb[s, t] = (mod(s, 2) * gm).astype(jnp.bfloat16)
    widen_start(6, wideb)
    each(scatter_direct, THREE, BACK)
    each(scatter_relay, TWO, BACK)
    grad_bd[0:1] = sum(jnp.sum(wideb[s, t].astype(jnp.float32), axis=0, keepdims=True) for s in range(slots))
    flip1[...] = wide1[...].reshape(256, 1152).T
    gb = widen_end(6, wideb)
    flipb[...] = gb.T
    gatt = dot(gb[:, :1024], w1[:, :, 1664:2304].reshape(1024, 640)) + dot(gb[:, 1024:], tail_w[:, 1664:2304])
    each(scatter_on, THREE, BACK)
    gattp[...] = dot(gatt.astype(jnp.bfloat16), join, 1, 1).astype(jnp.bfloat16)

    def attend_back(i, carry):
        rows = pl.ds(pl.multiple_of(i * 128, 128), 128)
        for h in range(8):
            lanes = slice(128 * h, 128 * h + 128)
            q, k, v = qkvp[0, rows, lanes], qkvp[1, rows, lanes], qkvp[2, rows, lanes]
            ga = gattp[rows, lanes]
            prob = probs[i, h]
            grad = dot(ga, v, 1, 1)
            inner = jnp.sum(prob * grad, axis=-1, keepdims=True)
            gs = (prob * (grad - inner)).astype(jnp.bfloat16)
            qkvp[0, rows, lanes] = (dot(gs, k) * factor).astype(jnp.bfloat16)
            qkvp[1, rows, lanes] = (dot(gs, q, 0, 0) * factor).astype(jnp.bfloat16)
            qkvp[2, rows, lanes] = dot(prob.astype(jnp.bfloat16), ga, 0, 0).astype(jnp.bfloat16)
        return carry

    attend_back(0, 0)
    each(scatter_direct, TWO, BACK)
    attend_back(1, 0)
    each(scatter_on, TWO, BACK)
    each(scatter_middle, THREE, BACK)
    gqkv[...] = jnp.zeros_like(gqkv)
    for i, lane in enumerate((0, 576, 1152)):
        low = lane // 128 * 128
        gather_heads = one_hot(
            (1024, 640), lambda a, b: (b - (lane - low) == (a // 128) * 72 + a % 128) & (a % 128 < 72)
        )
        piece = dot(qkvp[i], gather_heads).astype(jnp.bfloat16)
        gqkv[:, low : low + 640] = gqkv[:, low : low + 640] + piece
    grad_bqkv[...] = jnp.sum(gqkv[...].astype(jnp.float32), axis=0, keepdims=True)
    back_to_width(gqkv[...], w1, slice(0, 1792), slice(0, 1792), False)
    narrow_start(7, 3)

    each(scatter_middle, TWO, BACK)
    each(scatter_outer, THREE)
    each(sent, ONE)
    columns_loop(6, lambda cols: weight_grad(flip1, gqkv, cols, w1, 0))
    for low, high in ((1536, 1664), (1664, 1792), (1792, 2304)):
        made = 0.0
        if low < 1792:
            made = made + dot(flip1[...], gqkv[:, low:high])
        if high > 1664:
            made = made + dot(flipb[...], att[:, low - 1664 : high - 1664])
        made = made.astype(jnp.bfloat16)
        w1[:, :, low:high] = made[:1024].reshape(64, 16, high - low)
        tail_g[:, low:high] = made[1024:]
    tail_g[:, 6912:] = jnp.zeros((128, 256), jnp.bfloat16)
    turn_back = one_hot((256, 256), lambda a, b: a == (b % 32 // 2) * 16 + (b % 2) * 8 + b // 32)
    for i in range(4):
        stacked = jnp.concatenate(
            [tail_g[32 * i : 32 * i + 32, 896 * j : 896 * j + 896] for j in range(8)], axis=0
        )
        wt[16 * i : 16 * i + 16] = dot(turn_back, stacked).astype(jnp.bfloat16).reshape(16, 16, 896)
    each(scatter_twin, ONE)
    each(scatter_x, THREE)
    each(scatter_outer, TWO)
    each(scatter_relay, ONE, BACK)

    narrow_end(7, 3)
    for s in range(slots):
        gh = narrowed(3, s)
        unit, inverse = normed(lat[s].astype(jnp.float32))
        grad_mod[s, 0:1] = jnp.sum(gh, axis=0, keepdims=True)
        grad_mod[s, 1:2] = jnp.sum(gh * unit, axis=0, keepdims=True)
        middle[s] = middle[s] + norm_back(gh * (1.0 + mod(s, 1)), unit, inverse)
        grad_mod[s, 6:8] = jnp.zeros((2, 1152), jnp.float32)
    grad_bd[...] = unshuffled(thirds(grad_bd[...]))
    turn_ring_start()
    each(scatter_x, TWO)
    each(scatter_direct, ONE, BACK)
    turn_plane_start()
    each(scatter_end, THREE)
    each(scatter_on, ONE, BACK)
    tiles_plane()
    each(scatter_end, TWO)
    each(scatter_middle, ONE, (3, 2))
    tiles_ring()
    each(scatter_middle, ONE, (1, 0))
    tiles_back()
    grad_lat[...] = unshuffled(thirds(middle[...].reshape(128, 1152))).reshape(2, 64, 1152)
    done = jnp.concatenate([wideg[0, t], wideg[1, t]], axis=0)
    out[...] = unshuffled([done]).astype(jnp.bfloat16).reshape(2, 64, 1152)
    each(scatter_outer, ONE)
    tiles_out()
    each(scatter_x, ONE)
    each(scatter_end, ONE)
    tiles_end()
    each(sent, ALL)


def whole_block(args, weights, collective_id):
    f32, bf = jnp.float32, jnp.bfloat16
    m = len(WIDTHS)
    vmem = pl.BlockSpec(memory_space=pltpu.VMEM)
    shape = jax.ShapeDtypeStruct
    n = len(PIECES)

    def room(*lead):
        return [pltpu.VMEM(lead + (16, piece[2]), bf) for piece in PIECES]

    dma = pltpu.SemaphoreType.DMA
    return pl.pallas_call(
        block_kernel,
        out_shape=[
            shape((2, 64, 1152), bf), shape((2, 64, 1152), f32),
            *[shape((1, 16, width), f32) for width in WIDTHS],
            shape((96, 128), f32), shape((128, 8, 128), f32),
        ],
        in_specs=[vmem] * (len(args) + m),
        out_specs=[vmem] * (4 + m),
        scratch_shapes=[
            *[pltpu.VMEM((64, 16, width), bf) for width in WIDTHS],
            *[pltpu.VMEM((32, 16, width), bf) for width in WIDTHS],
            *room(4, 6), *room(6), *room(1),
            pltpu.VMEM((128, 7168), bf), pltpu.VMEM((128, 7168), bf),
            *[pltpu.VMEM((2, 2, 64, 1152), bf)] * 4,
            *[pltpu.VMEM((1152, 256), bf)] * 2,
            pltpu.VMEM((4, 2, 64, 1152), bf), pltpu.VMEM((4, 2, 64, 1152), bf),
            pltpu.VMEM((2, 2, 64, 1152), f32),
            pltpu.VMEM((3, 256, 1024), bf), pltpu.VMEM((2, 8, 128, 128), f32), pltpu.VMEM((256, 1024), bf),
            pltpu.VMEM((256, 1792), bf), pltpu.VMEM((256, 640), bf),
            pltpu.VMEM((256, 2304), f32), pltpu.VMEM((256, 2304), bf), pltpu.VMEM((256, 2304), bf),
            *[pltpu.VMEM((2, 64, 1152), f32)] * 3,
            dma((8,)), dma((8,)),
            dma((n,)), dma((n, 31)), dma((n, 16)), dma((n, 21)), dma((n, 16)), dma((n, 31)), dma((n, 16)),
            pltpu.VMEM((2, 8, 1152), f32), pltpu.VMEM((2, 8, 1152), f32),
            pltpu.VMEM((2, 1152), f32), pltpu.VMEM((1, 1792), f32), pltpu.VMEM((1, 2304), f32),
            pltpu.VMEM((16, 16, 128), bf), pltpu.VMEM((4, 16, 128), bf), pltpu.VMEM((8, 16, 128), bf),
            pltpu.VMEM((8, 16, 128), f32), pltpu.VMEM((8, 16, 128), f32),
            pltpu.VMEM((16, 8, 128), f32), pltpu.VMEM((16, 8, 128), f32),
            pltpu.VMEM((128, 8, 128), f32), pltpu.VMEM((16, 8, 8, 128), f32),
            pltpu.VMEM((8, 8, 128), f32), pltpu.VMEM((8, 8, 128), f32),
            dma((8,)), dma((8,)),
            pltpu.VMEM((2, 64, 1152), bf), pltpu.VMEM((2, 64, 1152), bf), pltpu.VMEM((2, 1152), f32),
        ],
        compiler_params=pltpu.CompilerParams(
            collective_id=collective_id, has_side_effects=True, vmem_limit_bytes=63 * 1024 * 1024
        ),
    )(*args, *weights)


MAIN = 1024
CHUNK = 896


def index_tables():
    place = np.arange(1152)
    tail = place - MAIN
    block = np.where(place < MAIN, place // 16, tail // 2)
    row = np.where(place < MAIN, place % 16, 16 + tail % 2)
    plane = (block // 8) % 4 * 4 + (block // 2) % 4
    ring = ((block % 2) * 2 + block // 32) * 2 + row // 9
    lane = np.arange(128)
    rows_at = (ring * PLANE + plane)[None, :] == lane[:, None]
    lanes_at = ((lane % 9)[:, None] == (row % 9)[None, :]) & (lane < 108)[:, None]
    kind = np.arange(16)
    kinds = (lane // 54 * 8 + lane % 54 // 9)[None, :] == kind[:, None]
    kinds = kinds & (lane < 108)[None, :]
    return [jnp.asarray(each.astype(np.float32), jnp.bfloat16) for each in (rows_at, lanes_at, kinds)]


def pack_rows(all_rows):
    third = all_rows.shape[1] // 3
    main, tail = all_rows[:16], all_rows[16:]
    tail = jnp.pad(tail, ((0, 0), (0, 8 * CHUNK - tail.shape[1]))).reshape(1, 16, CHUNK)
    return [*(main[None, :, i * third : (i + 1) * third] for i in range(3)), tail]


def unpack_rows(one, two, three, tail):
    width = one.shape[1] * 3
    main = jnp.concatenate([one, two, three], axis=1)
    return jnp.concatenate([main, tail.reshape(2, 8 * CHUNK)[:, :width]], axis=0)


def local(
    latents,
    condition,
    counts,
    order,
    w_ada,
    b_ada,
    w_qkv,
    b_qv,
    w_proj,
    b_proj,
    w_up,
    b_up,
    w_down,
    b_down,
    cotangent,
):
    slots = latents.shape[0]
    latent_count = condition.shape[0]
    group = lax.axis_index("fsdp")
    ranks = jnp.arange(counts.shape[0], dtype=jnp.int32)
    held = jnp.sum(jnp.where(ranks == group, counts, 0))
    before = jnp.sum(jnp.where(ranks < group, counts, 0))
    slot_rank = jnp.arange(slots, dtype=jnp.int32)
    live = (slot_rank < held).astype(jnp.float32)
    place = jnp.clip(before + slot_rank, 0, latent_count - 1)
    numbers = jnp.arange(latent_count, dtype=jnp.int32)
    owner = jnp.sum(jnp.where(numbers[None, :] == place[:, None], order[None, :], 0), axis=1)
    offsets = jnp.cumsum(counts) - counts
    every = jnp.clip(offsets[:, None] + slot_rank[None, :], 0, latent_count - 1).reshape(-1)
    owners = jnp.sum(jnp.where(numbers[None, :] == every[:, None], order[None, :], 0), axis=1)
    choose_all = (numbers[None, :] == owners[:, None]).astype(jnp.bfloat16)
    groups = counts.shape[0]
    devices = groups * 2
    soft_cond = jax.nn.silu(condition.astype(jnp.float32))
    ada_local = w_ada.astype(jnp.float32)
    mod_part = jnp.einsum("nd,dke->nke", soft_cond, ada_local, precision=highest) + b_ada
    mod_low = mod_part.astype(jnp.bfloat16).reshape(latent_count, -1)
    columns = mod_part.shape[2]
    mod_send = jnp.dot(choose_all, mod_low, preferred_element_type=jnp.float32).astype(jnp.bfloat16)
    mod_send = jnp.pad(
        mod_send.reshape(PLANE, 4, slots * 6 * columns), ((0, 0), (0, 12), (0, 128 - slots * 6 * columns))
    )
    alive_all = slot_rank[None, :] < counts[:, None]
    choose_two = jnp.where(
        (numbers[:, None, None] == owners.reshape(groups, slots)[None]) & alive_all[None], 1.0, 0.0
    )
    choose_two = jnp.transpose(choose_two, (2, 0, 1)).reshape(slots, latent_count, PLANE, 4)
    choose_two = jnp.pad(choose_two, ((0, 0), (0, 0), (0, 0), (0, 4))).reshape(slots, latent_count, 128)
    ada = jnp.transpose(w_ada.reshape(w_ada.shape[0], -1))
    ada = jnp.concatenate([ada, ada, jnp.zeros((128 - 2 * ada.shape[0], ada.shape[1]), ada.dtype)], axis=0)
    bias_d = jnp.stack([b_proj, b_down])
    own_rows = jnp.concatenate([w_qkv[0], w_qkv[1], w_qkv[2], w_proj.T, w_up, w_down.T], axis=1)
    width = own_rows.shape[1]
    head_part = w_qkv.shape[2]
    weights = pack_rows(own_rows)
    live_rows = jnp.broadcast_to(live[:, None, None], (slots, 1, latents.shape[2]))
    nothing = jnp.zeros_like(b_qv[0])
    bias_qkv = jnp.concatenate([b_qv[0], nothing, b_qv[1], nothing])[None]
    block_output, grad_latents, *grads, grad_table, tiles = whole_block(
        (latents, cotangent, live_rows, bias_d, bias_qkv, b_up[None], mod_send, choose_two, ada, *index_tables()),
        weights,
        2,
    )
    summed = unpack_rows(*(each[0] for each in grads))
    grad_w_qkv = jnp.stack([summed[:, i * head_part : (i + 1) * head_part] for i in range(3)])
    grad_w_proj = summed[:, 3 * head_part : 4 * head_part].T
    up_part = w_up.shape[1]
    grad_w_up = summed[:, 4 * head_part : 4 * head_part + up_part]
    grad_w_down = summed[:, 4 * head_part + up_part :].T
    used = 6 * columns
    grad_mod_part = (grad_table[:, :used] + grad_table[:, used : 2 * used]).reshape(latent_count, 6, columns)
    grad_b_ada = jnp.sum(grad_mod_part, axis=0)
    grad_w_ada = jnp.einsum("nd,nke->dke", soft_cond, grad_mod_part, precision=highest)
    grad_soft = jnp.transpose(tiles[:108].reshape(12, 9, 8, 128), (0, 2, 1, 3)).reshape(latent_count, -1)
    lines = tiles[108:].reshape(-1, 128)
    grad_b_proj, grad_b_down = lines[:9].reshape(-1), lines[9:18].reshape(-1)
    halves = lax.dynamic_slice_in_dim(lines, 18 + 32 * lax.axis_index("tp"), 32, 0)
    frame = halves[:14].reshape(-1)
    grad_b_qv = jnp.stack([frame[:head_part], frame[2 * head_part : 3 * head_part]])
    grad_b_up = halves[14:].reshape(-1)
    grad_condition = jax.vjp(jax.nn.silu, condition.astype(jnp.float32))[1](grad_soft)[0]
    return (
        block_output,
        grad_latents,
        grad_condition,
        grad_w_ada,
        grad_b_ada,
        grad_w_qkv,
        grad_b_qv,
        grad_w_proj,
        grad_b_proj,
        grad_w_up,
        grad_b_up,
        grad_w_down,
        grad_b_down,
    )


def solution(mesh):
    in_specs = (
        P("fsdp", "tp", None),
        P(),
        P(),
        P(),
        P(None, None, ("fsdp", "tp")),
        P(None, ("fsdp", "tp")),
        P(None, "fsdp", "tp"),
        P(None, "tp"),
        P("tp", "fsdp"),
        P(),
        P("fsdp", "tp"),
        P("tp"),
        P("tp", "fsdp"),
        P(),
        P("fsdp", "tp", None),
    )
    out_specs = (
        P("fsdp", "tp", None),
        P("fsdp", "tp", None),
        P(),
        P(None, None, ("fsdp", "tp")),
        P(None, ("fsdp", "tp")),
        P(None, "fsdp", "tp"),
        P(None, "tp"),
        P("tp", "fsdp"),
        P(),
        P("fsdp", "tp"),
        P("tp"),
        P("tp", "fsdp"),
        P(),
    )
    return jax.shard_map(local, mesh=mesh, in_specs=in_specs, out_specs=out_specs, check_vma=False)
```
